32 devices in a mesh: dp: 8 (over y, x, core), tensor: 4 (over z).
Axes of the slice: x: 2, y: 2, z: 4, core: 2. Of those that a mesh axis runs over, the one named last changes fastest.
Arguments:
- tokens: bfloat16 [32768, 768], P('dp'), may hold values from -6 to 6
- out_grad: bfloat16 [32768, 768], P('dp'), may hold values from -6 to 6
- segment_ids: int32 [32, 1024], P('dp'), may hold values from -1 to 7, as said below
- row_tasks: int32 [32], P('dp'), may hold values from 0 to 3, as said below
- rel_buckets: int32 [2047], replicated, may hold values from 0 to 511
- norm_gains: bfloat16 [3, 768], replicated, may hold values from 0.099609375 to 1.8984375
- model_biases: bfloat16 [5, 768], replicated, may hold values from -3 to 3
- w_qkv: bfloat16 [3, 768, 768], replicated, may hold values from -0.21875 to 0.21875
- qkv_bias: bfloat16 [2, 12, 64], replicated, may hold values from -3 to 3
- rel_bias: bfloat16 [12, 512], replicated, may hold values from -5 to 5
- head_scale: bfloat16 [12], replicated, may hold values from 0.25 to 4
- w_out: bfloat16 [768, 768], replicated, may hold values from -0.21875 to 0.21875
- w_up: bfloat16 [768, 3072], replicated, may hold values from -0.21875 to 0.21875
- ffn_gain: bfloat16 [3072], replicated, may hold values from 0.099609375 to 1.8984375
- ffn_biases: bfloat16 [2, 3072], replicated, may hold values from -3 to 3
- w_down: bfloat16 [3072, 768], replicated, may hold values from -0.109375 to 0.109375
Outputs:
- layer_out: bfloat16 [32768, 768], P('dp')
- tokens_grad: bfloat16 [32768, 768], P('dp')
- norm_gains_grad: float32 [3, 768], P(None, 'dp')
- model_biases_grad: float32 [5, 768], P(None, 'dp')
- w_qkv_grad: float32 [3, 768, 768], P(None, 'dp', 'tensor')
- qkv_bias_grad: float32 [2, 12, 64], P(None, 'tensor')
- rel_bias_grad: float32 [12, 512], P('tensor', 'dp')
- head_scale_grad: float32 [12], P('tensor')
- w_out_grad: float32 [768, 768], P('tensor', 'dp')
- w_up_grad: float32 [768, 3072], P('dp', 'tensor')
- ffn_gain_grad: float32 [3072], P('tensor')
- ffn_biases_grad: float32 [2, 3072], P(None, 'tensor')
- w_down_grad: float32 [3072, 768], P('tensor', 'dp')
The draws below stay inside these ranges and needn't reach their ends.
Inputs may be any that keep to these rules, and one draw needn't show every extreme that they name: `segment_ids`: in each row the live tokens come first and carry document numbers 0, 1, 2, ... from position 0, never falling, at most 7; the positions after them hold -1, and every row ends with at least one -1. `row_tasks`: all rows of one index of dp have one task; each task's rows are consecutive, cover whole indices of dp, and every task has rows.
All inputs are finite; a program needn't handle non-finite values.
Results may differ from the reference program's by a relative error of at most 0.015.
Values may be sent and summed in bfloat16 or wider, within the bound.
No kernel may reach another device: no remote copies, remote signals or barrier semaphores. Data moves between devices by JAX's collectives and lax.ppermute only.
A program may use at most 320 MiB of HBM per device.

```python
import math
from functools import partial
import jax
import jax.numpy as jnp
from jax import lax

D = 768
H = 12
HD = 64
FF = 3072
NB = 512
SEQ = 1024
TASKS = 4
ROWS_DEV = 4
ROWS = 32
TOKENS = 32768


def draw_segment_ids(key, part):
    key = jax.random.fold_in(key, 11)
    length_key, mark_key = jax.random.split(key)
    devices_count = ROWS // ROWS_DEV
    device = jnp.arange(ROWS) // ROWS_DEV
    lower_end = SEQ // 8 + device * (5 * SEQ // 8) // max(devices_count - 1, 1)
    live_len = lower_end + jax.random.randint(length_key, (ROWS,), 0, SEQ // 4)
    doc_marks = (jax.random.randint(mark_key, (ROWS, SEQ), 0, SEQ // 4) == 0).astype(jnp.int32)
    position = jnp.arange(SEQ)[None, :]
    forced = ((position % (SEQ // 16) == 0) & (position >= SEQ // 16) & (position <= 7 * (SEQ // 16))).astype(jnp.int32)
    last_row = (jnp.arange(ROWS) == ROWS - 1)[:, None]
    doc_marks = jnp.where(last_row, jnp.maximum(doc_marks, forced), doc_marks)
    doc_marks = doc_marks.at[:, 0].set(0)
    doc_number = jnp.minimum(jnp.cumsum(doc_marks, axis=1), 7)
    return jnp.where(position < live_len[:, None], doc_number, -1).astype(jnp.int32)


def draw_row_tasks(key, part):
    key = jax.random.fold_in(key, 23)
    devices_count = ROWS // ROWS_DEV
    cut_points = jnp.sort(jax.random.permutation(key, jnp.arange(1, devices_count))[:TASKS - 1])
    device = jnp.arange(ROWS) // ROWS_DEV
    return jnp.sum(device[:, None] >= cut_points[None, :], axis=1).astype(jnp.int32)


def plant(array, rng, smallest, top_value):
    place = [jax.random.randint(jax.random.fold_in(rng, axis), (), 0, length) for axis, length in enumerate(array.shape)]
    longest = array.shape.index(max(array.shape))
    beside = place[:longest] + [(place[longest] + 1) % array.shape[longest]] + place[longest + 1:]
    return array.at[tuple(place)].set(smallest).at[tuple(beside)].set(top_value)


def block_levels(key, dims, shards, least, top_value):
    level = 1.0
    for dim, shards_of in shards:
        steps = jax.random.uniform(jax.random.fold_in(jax.random.fold_in(key, 6), dim), (shards_of,), jnp.float32, least / len(shards), top_value / len(shards))
        level = level * jnp.repeat(jnp.exp(steps), dims[dim] // shards_of).reshape((-1,) + (1,) * (len(dims) - 1 - dim))
    return level


def normal_values(stream_key, dims, scale, bound, cuts=(), kind=jnp.bfloat16):
    gain = block_levels(stream_key, dims, cuts, -0.22, 0.18) if cuts else 1.0
    array = jax.random.normal(stream_key, dims, jnp.float32) * scale * gain
    return jnp.minimum(jnp.maximum(array, -bound), bound).astype(kind)


def setup_inputs(seed: int = 0) -> dict:
    arg_keys = jax.random.split(jax.random.key(seed), 17)
    tokens = normal_values(arg_keys[0], (TOKENS, D), 1.0, 6.0, ((0, 8),))
    out_grad = normal_values(arg_keys[1], (TOKENS, D), 1.0, 6.0, ((0, 8),))
    segment_ids = draw_segment_ids(jax.random.fold_in(arg_keys[16], 71), 0)
    row_tasks = draw_row_tasks(jax.random.fold_in(arg_keys[16], 71), 0)
    rel_buckets = plant(jax.random.randint(arg_keys[4], (2 * SEQ - 1,), 0, NB), jax.random.fold_in(arg_keys[4], 1), 0, NB - 1).astype(jnp.int32)
    norm_gains = jnp.clip(1.0 + 0.18 * jax.random.normal(arg_keys[5], (3, D), jnp.float32), 0.099609375, 1.8984375).astype(jnp.bfloat16)
    model_biases = normal_values(arg_keys[6], (5, D), 0.5, 3.0)
    w_qkv = normal_values(arg_keys[7], (3, D, D), D ** -0.5, 0.21875)
    qkv_bias = normal_values(arg_keys[8], (2, H, HD), 0.5, 3.0)
    rel_bias = normal_values(arg_keys[9], (H, NB), 1.0, 5.0)
    head_scale = jnp.clip(jnp.exp(jax.random.uniform(arg_keys[10], (H,), jnp.float32, math.log(0.25), math.log(4.0))), 0.25, 4.0).astype(jnp.bfloat16)
    w_out = normal_values(arg_keys[11], (D, D), D ** -0.5, 0.21875)
    w_up = normal_values(arg_keys[12], (D, FF), D ** -0.5, 0.21875)
    ffn_gain = jnp.clip(1.0 + 0.18 * jax.random.normal(arg_keys[13], (FF,), jnp.float32), 0.099609375, 1.8984375).astype(jnp.bfloat16)
    ffn_biases = normal_values(arg_keys[14], (2, FF), 0.5, 3.0)
    w_down = normal_values(arg_keys[15], (FF, D), FF ** -0.5, 0.109375)
    return {"tokens": tokens, "out_grad": out_grad, "segment_ids": segment_ids, "row_tasks": row_tasks, "rel_buckets": rel_buckets, "norm_gains": norm_gains, "model_biases": model_biases, "w_qkv": w_qkv, "qkv_bias": qkv_bias, "rel_bias": rel_bias, "head_scale": head_scale, "w_out": w_out, "w_up": w_up, "ffn_gain": ffn_gain, "ffn_biases": ffn_biases, "w_down": w_down}


@jax.custom_vjp
def low(v):
    return lax.optimization_barrier(v.astype(jnp.bfloat16)).astype(jnp.float32)

@jax.custom_vjp
def low_back(v):
    return v

def low_keep(v):
    return (low(v), None)

def low_pass(kept, grad):
    return (grad,)

def back_keep(v):
    return (v, None)

def back_low(kept, grad):
    return (low(grad),)
low.defvjp(low_keep, low_pass)
low_back.defvjp(back_keep, back_low)
masked_score = -1e+30
highest = lax.Precision.HIGHEST

def layer_norm(values, gain_vec, shift_vec):
    average = lax.optimization_barrier(jnp.mean(values, axis=-1, keepdims=True))
    centred = values - average
    inverse = lax.rsqrt(lax.optimization_barrier(jnp.mean(centred * centred, axis=-1, keepdims=True)) + 1e-05)
    return centred * inverse * gain_vec + shift_vec

def row_layer(params, rel_buckets, row_pair):
    row_tokens, row_segments = row_pair
    gains, biases, w_qkv, qkv_bias, rel_bias, head_scale, w_out, w_up, ffn_gain, ffn_biases, w_down = params
    first = low(layer_norm(row_tokens, gains[0], biases[0]))
    projected = jnp.einsum('td,cde->cte', first, w_qkv, precision=highest)
    query = low_back(low((projected[0] + qkv_bias[0].reshape(D)) * 0.125)).reshape(SEQ, H, HD)
    keys = low_back(low(projected[1])).reshape(SEQ, H, HD)
    values = low_back(low(projected[2] + qkv_bias[1].reshape(D))).reshape(SEQ, H, HD)
    offsets = jnp.arange(SEQ)[None, :] - jnp.arange(SEQ)[:, None] + SEQ - 1
    position_bias = rel_bias[:, rel_buckets[offsets]]
    scores = jnp.einsum('qhe,khe->hqk', query, keys, precision=highest) + position_bias
    same_doc = (row_segments[:, None] == row_segments[None, :])[None]
    scores = low_back(jnp.where(same_doc, scores, masked_score))
    top_score = lax.optimization_barrier(jnp.max(scores, axis=-1, keepdims=True))
    shifted_exp = jnp.exp(scores - top_score)
    weights = low(shifted_exp / lax.optimization_barrier(jnp.sum(shifted_exp, axis=-1, keepdims=True)))
    attended = low_back(jnp.einsum('hqk,khe->qhe', weights, values, precision=highest))
    mixed = low((attended * head_scale[None, :, None]).reshape(SEQ, D))
    attn = low_back(jnp.dot(mixed, w_out, precision=highest) + biases[1])
    middle_resid = row_tokens + layer_norm(attn, gains[1], biases[2])
    third = low(layer_norm(middle_resid, gains[2], biases[3]))
    upward = low_back(jnp.dot(third, w_up, precision=highest) + ffn_biases[0])
    middle = low(layer_norm(jax.nn.gelu(upward, approximate=False), ffn_gain, ffn_biases[1]))
    return middle_resid + low_back(jnp.dot(middle, w_down, precision=highest) + biases[4])

def reference(tokens, out_grad, segment_ids, row_tasks, rel_buckets, norm_gains, model_biases, w_qkv, qkv_bias, rel_bias, head_scale, w_out, w_up, ffn_gain, ffn_biases, w_down):
    params = tuple((weight.astype(jnp.float32) for weight in (norm_gains, model_biases, w_qkv, qkv_bias, rel_bias, head_scale, w_out, w_up, ffn_gain, ffn_biases, w_down)))
    live_mask = (segment_ids >= 0).astype(jnp.float32)
    picked = (row_tasks[:, None] == jnp.arange(TASKS)[None, :]).astype(jnp.float32)
    task_counts = lax.optimization_barrier(jnp.sum(picked * lax.optimization_barrier(jnp.sum(live_mask, axis=1))[:, None], axis=0))
    task_weights = jnp.sum(task_counts) / (TASKS * task_counts)
    token_weight = live_mask * lax.optimization_barrier(jnp.sum(picked * task_weights[None, :], axis=1))[:, None]
    row_tokens = tokens.astype(jnp.float32).reshape(ROWS, SEQ, D)
    cotangent = out_grad.astype(jnp.float32).reshape(ROWS, SEQ, D) * token_weight[:, :, None]

    def forward(all_rows, weights):
        layer = jax.checkpoint(partial(row_layer, weights, rel_buckets))
        return lax.map(layer, (all_rows, segment_ids))
    result, pullback = jax.vjp(forward, row_tokens, params)
    rows_grad, params_grad = pullback(cotangent)
    gains_grad, biases_grad, project_grad, project_bias_grad, position_grad, head_grad, output_grad, upward_grad, middle_gain_grad, middle_bias_grad, downward_grad = params_grad
    return (result.reshape(TOKENS, D).astype(jnp.bfloat16), rows_grad.reshape(TOKENS, D).astype(jnp.bfloat16), gains_grad, biases_grad, project_grad, project_bias_grad, position_grad, head_grad, output_grad, upward_grad, middle_gain_grad, middle_bias_grad, downward_grad)
```

```python
import jax
import jax.numpy as jnp
from jax import lax
from jax.experimental import pallas as pl
from jax.experimental.pallas import tpu as pltpu
from jax.sharding import PartitionSpec as P

F32 = jnp.float32
BF16 = jnp.bfloat16
TASKS = 4
EPS = 1e-05
NEG = -1e30
LOG2E = 1.4426950408889634
HEAD = 64
TILE = 256
SUB = TILE // 128
BLOCK = 256
DOCS = 16
NT = (((1,), (1,)), ((), ()))
NN = (((1,), (0,)), ((), ()))
TN = (((0,), (0,)), ((), ()))


def dot(a, b, dims=NN):
    return lax.dot_general(a, b, dims, preferred_element_type=F32)


def split3(x):
    a = x.astype(BF16)
    r = x - a.astype(F32)
    b = r.astype(BF16)
    c = (r - b.astype(F32)).astype(BF16)
    return a, b, c


def normed(z):
    c = z - jnp.mean(z, axis=-1, keepdims=True)
    r = lax.rsqrt(jnp.mean(c * c, axis=-1, keepdims=True) + EPS)
    return c * r, r


def norm_back(dz, gain, zhat, r):
    s = dz * gain
    return r * (
        s
        - jnp.mean(s, axis=-1, keepdims=True)
        - zhat * jnp.mean(s * zhat, axis=-1, keepdims=True)
    )


def params(mib):
    return pltpu.CompilerParams(vmem_limit_bytes=mib * 2**20)


def whole(shape):
    return pl.BlockSpec(shape, lambda *_: (0,) * len(shape), pipeline_mode=pl.Buffered(1))


def project_body(tok_ref, gains_ref, biases_ref, w_ref, qb_ref, h1_ref, q_ref, k_ref, v_ref):
    z, _ = normed(tok_ref[...].astype(F32))
    h1 = (z * gains_ref[0:1, :].astype(F32) + biases_ref[0:1, :].astype(F32)).astype(BF16)
    h1_ref[...] = h1
    q_ref[...] = (dot(h1, w_ref[0]) * 0.125 + qb_ref[0:1, :].astype(F32) * 0.125).astype(BF16)
    k_ref[...] = dot(h1, w_ref[1]).astype(BF16)
    v_ref[...] = (dot(h1, w_ref[2]) - (-qb_ref[1:2, :].astype(F32))).astype(BF16)


def project(tokens, gains, biases, w_qkv, qkv_bias):
    n, d = tokens.shape
    blk = pl.BlockSpec((BLOCK, d), lambda i: (i, 0))
    return pl.pallas_call(
        project_body,
        grid=(n // BLOCK,),
        in_specs=[blk, whole(gains.shape), whole(biases.shape), whole(w_qkv.shape), whole(qkv_bias.shape)],
        out_specs=[blk] * 4,
        out_shape=[jax.ShapeDtypeStruct((n, d), BF16)] * 4,
        compiler_params=params(40),
        cost_estimate=pl.CostEstimate(flops=6 * n * d * d, bytes_accessed=16 * 2**20, transcendentals=0),
        name="project",
    )(tokens, gains, biases, w_qkv, qkv_bias)


def build_band(row):
    n = row.shape[1]
    x = pltpu.roll(jnp.broadcast_to(row, (8, n)), n - 127, 1, stride=1, stride_axis=0)
    k = 8
    while k < 128:
        x = jnp.concatenate([x, pltpu.roll(x, k, 1)], axis=0)
        k *= 2
    return x


def fold_band(x):
    r = x.shape[0]
    while r > 8:
        r //= 2
        x = pltpu.roll(x[:r], r, 1) + x[r:]
    out = x[7:8]
    for i in range(7):
        out = out + pltpu.roll(x[i : i + 1], 7 - i, 1)
    return out


def bias_tile(band, h, base):
    return jnp.concatenate(
        [
            jnp.concatenate([band[h, base + u - t] for u in range(SUB)], axis=1)
            for t in range(SUB)
        ],
        axis=0,
    )


def attend_body(
    lo_ref, hi_ref, scale_ref, q_ref, k_ref, v_ref, segc_ref, rev_ref,
    oc_ref, lse_ref, band, vt, qx, km, acc, ml,
):
    seq = q_ref.shape[0]
    nb = seq // TILE
    bw = seq // 128 - 1
    nh = q_ref.shape[1] // HEAD
    lane = lax.broadcasted_iota(jnp.int32, (seq, 128), 1)
    doc = segc_ref[...] + 1
    zero = jnp.zeros((), BF16)
    hot = jnp.where(lane == doc, 1.0, 0.0).astype(BF16)
    bar = jnp.where((lane < DOCS) & (lane != doc), NEG, 0.0).astype(BF16)
    for h in range(nh):
        full = build_band(rev_ref[h : h + 1, :])
        for t in range(2 * seq // 128):
            band[h, t] = full[:, 128 * t : 128 * t + 128] * LOG2E
        half = (lane < HEAD) if h % 2 == 0 else (lane >= HEAD)
        c = slice(128 * (h // 2), 128 * (h // 2) + 128)
        km[h, :, :128] = jnp.where(half, k_ref[:, c], zero)
        km[h, :, 128:] = hot
    for j in range(nh // 2):
        c = slice(128 * j, 128 * j + 128)
        qx[j, :, :128] = q_ref[:, c]
        qx[j, :, 128:] = bar
        for b in range(nb):
            vt[b, c, :] = v_ref[b * TILE : (b + 1) * TILE, c].astype(F32).T.astype(BF16)
    for qb in range(nb):
        qs = slice(qb * TILE, (qb + 1) * TILE)
        acc[...] = jnp.zeros_like(acc)
        ml[0] = jnp.full((nh, TILE), -jnp.inf, F32)
        ml[1] = jnp.zeros((nh, TILE), F32)

        def step(kb, _):
            ks = pl.ds(pl.multiple_of(kb * TILE, TILE), TILE)
            base = bw + SUB * qb - SUB * kb
            ss = [dot(km[h, ks, :], qx[h // 2, qs, :], NT) for h in range(nh)]
            for h in range(nh):
                s = ss[h] * LOG2E + bias_tile(band, h, base)
                old = ml[0, h : h + 1, :]
                top = jnp.maximum(old, jnp.max(s, axis=0, keepdims=True))
                fade = jnp.exp2(old - top)
                w = jnp.exp2(s - top)
                ml[0, h : h + 1, :] = top
                ml[1, h : h + 1, :] = ml[1, h : h + 1, :] * fade + jnp.sum(w, axis=0, keepdims=True)
                r = slice(HEAD * h, HEAD * h + HEAD)
                acc[r, :] = acc[r, :] * fade + dot(vt[kb, r, :], w.astype(BF16))
            return _

        lax.fori_loop(lo_ref[qb], hi_ref[qb], step, 0)
        for j in range(nh // 2):
            outs = []
            for h in (2 * j, 2 * j + 1):
                total = ml[1, h : h + 1, :]
                lse_ref[h : h + 1, qs] = ml[0, h : h + 1, :] * (1 / LOG2E) + jnp.log(total)
                outs.append(acc[HEAD * h : HEAD * h + HEAD, :] * (scale_ref[h] / total))
            oc_ref[qs, 128 * j : 128 * j + 128] = jnp.concatenate(outs, axis=0).T.astype(BF16)
    lse_ref[nh:, :] = jnp.zeros((lse_ref.shape[0] - nh, seq), F32)


def attend(q, k, v, segc, rev, lo, hi, scale):
    seq, width = q.shape
    nh = width // HEAD
    rows = -(-nh // 8) * 8
    full = lambda shape: pl.BlockSpec(shape, lambda i, *_: (0,) * len(shape), pipeline_mode=pl.Buffered(1))
    return pl.pallas_call(
        attend_body,
        grid_spec=pltpu.PrefetchScalarGridSpec(
            num_scalar_prefetch=3,
            grid=(1,),
            in_specs=[full(q.shape)] * 3 + [full(segc.shape), full(rev.shape)],
            out_specs=[full(q.shape), full((rows, seq)), full((nh, 2 * seq // 128, 128, 128))],
            scratch_shapes=[
                pltpu.VMEM((seq // TILE, width, TILE), BF16),
                pltpu.VMEM((nh // 2, seq, 256), BF16),
                pltpu.VMEM((nh, seq, 256), BF16),
                pltpu.VMEM((width, TILE), F32),
                pltpu.VMEM((2, nh, TILE), F32),
            ],
        ),
        out_shape=[
            jax.ShapeDtypeStruct((seq, width), BF16),
            jax.ShapeDtypeStruct((rows, seq), F32),
            jax.ShapeDtypeStruct((nh, 2 * seq // 128, 128, 128), F32),
        ],
        compiler_params=params(56),
        cost_estimate=pl.CostEstimate(flops=20 * 10**9, bytes_accessed=24 * 2**20, transcendentals=0),
        name="attend",
    )(lo, hi, scale, q, k, v, segc, rev)


def attend_back_body(
    lo_ref, hi_ref, q_ref, k_ref, v_ref, do_ref, x_ref, segc_ref, band,
    dq_ref, dk_ref, dv_ref, tg_ref, gband, qx, dx, km, vm, kt, dqt, dka, dva,
):
    seq = q_ref.shape[0]
    nb = seq // TILE
    bw = seq // 128 - 1
    nh = q_ref.shape[1] // HEAD
    heads = pl.num_programs(0) * nh
    first = pl.program_id(0) * nh
    lane = lax.broadcasted_iota(jnp.int32, (seq, 128), 1)
    hot = lane == segc_ref[...] + 1
    zero = jnp.zeros((), BF16)
    gband[...] = jnp.zeros_like(gband)
    dqt[...] = jnp.zeros_like(dqt)
    for h in range(nh):
        half = (lane < HEAD) if h % 2 == 0 else (lane >= HEAD)
        c = slice(128 * (h // 2), 128 * (h // 2) + 128)
        at = DOCS + 3 * (first + h)
        km[h, :, :128] = jnp.where(half, k_ref[:, c], zero)
        km[h, :, 128:] = jnp.where(hot | ((lane >= at) & (lane < at + 3)), 1.0, 0.0).astype(BF16)
        at = at + 3 * heads
        vm[h, :, :128] = jnp.where(half, v_ref[:, c], zero)
        vm[h, :, 128:] = jnp.where((lane >= at) & (lane < at + 3), 1.0, 0.0).astype(BF16)
    for j in range(nh // 2):
        c = slice(128 * j, 128 * j + 128)
        qx[j, :, :128] = q_ref[:, c]
        qx[j, :, 128:] = x_ref[...]
        dx[j, :, :128] = do_ref[:, c]
        dx[j, :, 128:] = x_ref[...]
        kt[c, :] = k_ref[:, c].astype(F32).T.astype(BF16)
    low = lax.broadcasted_iota(jnp.int32, (TILE, 128), 1) < HEAD
    for kb in range(nb):
        dka[...] = jnp.zeros_like(dka)
        dva[...] = jnp.zeros_like(dva)
        ks = slice(kb * TILE, (kb + 1) * TILE)

        def step(qb, _):
            qs = pl.ds(pl.multiple_of(qb * TILE, TILE), TILE)
            base = bw + SUB * qb - SUB * kb
            ss = [dot(km[h, ks, :], qx[h // 2, qs, :], NT) for h in range(nh)]
            dps = [dot(vm[h, ks, :], dx[h // 2, qs, :], NT) for h in range(nh)]
            for h in range(nh):
                w = jnp.exp2(ss[h] * LOG2E + bias_tile(band, h, base))
                ds = (w * dps[h]).astype(BF16)
                dsf = ds.astype(F32)
                for off in range(1 - SUB, SUB):
                    total = None
                    for t in range(SUB):
                        u = off + t
                        if 0 <= u < SUB:
                            piece = dsf[128 * t : 128 * t + 128, 128 * u : 128 * u + 128]
                            total = piece if total is None else total + piece
                    gband[h, base + off] += total
                dva[h] += dot(w.astype(BF16), dx[h // 2, qs, :128])
                dka[h] += dot(ds, qx[h // 2, qs, :128])
                r = slice(HEAD * h, HEAD * h + HEAD)
                dqt[qb, r, :] += dot(kt[r, ks], ds)
            return _

        lax.fori_loop(lo_ref[kb], hi_ref[kb], step, 0)
        for j in range(nh // 2):
            c = slice(128 * j, 128 * j + 128)
            dk_ref[ks, c] = jnp.where(low, dka[2 * j], dka[2 * j + 1]).astype(BF16)
            dv_ref[ks, c] = jnp.where(low, dva[2 * j], dva[2 * j + 1]).astype(BF16)
    for j in range(nh // 2):
        c = slice(128 * j, 128 * j + 128)
        for b in range(nb):
            dq_ref[b * TILE : (b + 1) * TILE, c] = (
                dqt[b, c, :].T.astype(BF16).astype(F32) * 0.125
            ).astype(BF16)
    for h in range(nh):
        tg_ref[0, h : h + 1, :] = fold_band(
            jnp.concatenate([gband[h, t] for t in range(2 * seq // 128)], axis=1)
        )


def attend_back(q, k, v, do, aux, segc, band, lo, hi):
    seq, width = q.shape
    heads = width // HEAD
    nh = 4 if heads % 4 == 0 else 2
    groups = heads // nh
    blk = pl.BlockSpec((seq, HEAD * nh), lambda p, *_: (0, p))
    tiles = 2 * seq // 128
    dq, dk, dv, tg = pl.pallas_call(
        attend_back_body,
        grid_spec=pltpu.PrefetchScalarGridSpec(
            num_scalar_prefetch=2,
            grid=(groups,),
            in_specs=[blk] * 4
            + [
                pl.BlockSpec((seq, 128), lambda p, *_: (0, 0)),
                pl.BlockSpec((seq, 1), lambda p, *_: (0, 0)),
                pl.BlockSpec((nh, tiles, 128, 128), lambda p, *_: (p, 0, 0, 0)),
            ],
            out_specs=[blk] * 3 + [pl.BlockSpec((1, nh, 2 * seq), lambda p, *_: (p, 0, 0))],
            scratch_shapes=[
                pltpu.VMEM((nh, tiles, 128, 128), F32),
                pltpu.VMEM((nh // 2, seq, 256), BF16),
                pltpu.VMEM((nh // 2, seq, 256), BF16),
                pltpu.VMEM((nh, seq, 256), BF16),
                pltpu.VMEM((nh, seq, 256), BF16),
                pltpu.VMEM((HEAD * nh, seq), BF16),
                pltpu.VMEM((seq // TILE, HEAD * nh, TILE), F32),
                pltpu.VMEM((nh, TILE, 128), F32),
                pltpu.VMEM((nh, TILE, 128), F32),
            ],
        ),
        out_shape=[jax.ShapeDtypeStruct((seq, width), BF16)] * 3
        + [jax.ShapeDtypeStruct((groups, nh, 2 * seq), F32)],
        compiler_params=params(56),
        cost_estimate=pl.CostEstimate(flops=40 * 10**9, bytes_accessed=24 * 2**20, transcendentals=0),
        name="attend_back",
    )(lo, hi, q, k, v, do, aux, segc, band)
    return dq, dk, dv, tg.reshape(heads, 2 * seq)


def gelu_parts(u):
    dens = jnp.exp2(u * u * (-0.5 * LOG2E))
    t = 1.0 / (1.0 + (0.3275911 * 0.7071067811865476) * jnp.abs(u))
    poly = t * (0.127414796 + t * (-0.142248368 + t * (0.7107068705 + t * (-0.7265760135 + t * 0.5307027145))))
    tail = poly * dens
    phi = jnp.where(u >= 0, 1.0 - tail, tail)
    return phi, phi + u * (dens * 0.3989422804014327)


def middle_body(
    tok_ref, oc_ref, og_ref, wt_ref, segc_ref, lse_ref, gains_ref, biases_ref, fgain_ref, fbias_ref, hs_ref,
    wo_ref, wu_ref, wd_ref,
    out_ref, h3_ref, m_ref, df_ref, du_ref, dx2_ref, da_ref, do_ref, aux_ref, nv_ref, fv_ref,
    e_s, g_s, d_s,
):
    ff = wu_ref.shape[1]
    d = wu_ref.shape[0]
    heads = d // HEAD
    step = 512
    gains = gains_ref[...].astype(F32)
    biases = biases_ref[...].astype(F32)
    tok = tok_ref[...].astype(F32)
    oc = oc_ref[...]
    z2, r2 = normed(dot(oc, wo_ref[...]) - (-biases[1:2]))
    x2 = tok + (z2 * gains[1:2] + biases[2:3])
    z3, r3 = normed(x2)
    h3 = (z3 * gains[2:3] + biases[3:4]).astype(BF16)
    h3_ref[...] = h3
    g = og_ref[...].astype(F32) * wt_ref[...]
    df = g.astype(BF16)
    df_ref[...] = df
    s1 = jnp.zeros((tok.shape[0], 1), F32)
    s2 = jnp.zeros((tok.shape[0], 1), F32)
    for c0 in range(0, ff, step):
        c = slice(c0, c0 + step)
        u = dot(h3, wu_ref[:, c]) - (-fbias_ref[0:1, c].astype(F32))
        phi, slope = gelu_parts(u)
        e = u * phi
        e_s[:, c] = e
        g_s[:, c] = slope
        s1 += jnp.sum(e, axis=1, keepdims=True)
        s2 += jnp.sum(e * e, axis=1, keepdims=True)
    mean = s1 / ff
    r = lax.rsqrt(s2 / ff - mean * mean + EPS)
    y = jnp.zeros(tok.shape, F32)
    b1 = jnp.zeros((tok.shape[0], 1), F32)
    b2 = jnp.zeros((tok.shape[0], 1), F32)
    gsum, bsum, usum = [], [], []
    for c0 in range(0, ff, step):
        c = slice(c0, c0 + step)
        gain = fgain_ref[0:1, c].astype(F32)
        mh = (e_s[:, c] - mean) * r
        e_s[:, c] = mh
        m = (mh * gain + fbias_ref[1:2, c].astype(F32)).astype(BF16)
        m_ref[:, c] = m
        y += dot(m, wd_ref[c, :])
        dm = dot(df, wd_ref[c, :], NT)
        gsum.append(jnp.sum(dm * mh, axis=0, keepdims=True))
        bsum.append(jnp.sum(dm, axis=0, keepdims=True))
        sc = dm * gain
        d_s[:, c] = sc
        b1 += jnp.sum(sc, axis=1, keepdims=True)
        b2 += jnp.sum(sc * mh, axis=1, keepdims=True)
    out_ref[...] = (x2 + (y + biases[4:5])).astype(BF16)
    b1 = b1 / ff
    b2 = b2 / ff
    dh3 = jnp.zeros(tok.shape, F32)
    for c0 in range(0, ff, step):
        c = slice(c0, c0 + step)
        de = r * (d_s[:, c] - b1 - e_s[:, c] * b2)
        du = (de * g_s[:, c]).astype(BF16)
        du_ref[:, c] = du
        usum.append(jnp.sum(du.astype(F32), axis=0, keepdims=True))
        dh3 += dot(du, wu_ref[:, c], NT)
    dx2 = g + norm_back(dh3, gains[2:3], z3, r3)
    dx2_ref[...] = dx2
    da = norm_back(dx2, gains[1:2], z2, r2).astype(BF16)
    da_ref[...] = da
    doc = dot(da, wo_ref[...], NT)
    hs = hs_ref[...]
    o = oc.astype(F32) / hs
    do = (doc * hs).astype(BF16)
    do_ref[...] = do

    rows = tok.shape[0]
    prod = do.astype(F32) * o
    hi = prod.astype(BF16)
    lo = (prod - hi.astype(F32)).astype(BF16)
    at = DOCS + 3 * heads
    head_of = lax.broadcasted_iota(jnp.int32, (d, 128), 0) // HEAD
    lane = lax.broadcasted_iota(jnp.int32, (d, 128), 1)
    put = jnp.where((lane >= at + 3 * head_of) & (lane < at + 3 * head_of + 3), -1.0, 0.0).astype(BF16)
    delta = dot(hi, put) + dot(lo, put)
    pa, pb, pc = split3(delta)
    lane = lax.broadcasted_iota(jnp.int32, (rows, 128), 1)
    part = (lane - at + 3 * 128) % 3
    delta = jnp.where(part == 0, pa.astype(F32), jnp.where(part == 1, pb.astype(F32), pc.astype(F32)))
    hrows = lse_ref.shape[0]
    la, lb, lc = split3(lse_ref[...])
    stack = jnp.concatenate([la.astype(F32), lb.astype(F32), lc.astype(F32)], axis=0).astype(BF16)
    row = lax.broadcasted_iota(jnp.int32, (3 * hrows, 128), 0)
    col = lax.broadcasted_iota(jnp.int32, (3 * hrows, 128), 1)
    put = jnp.where((row % hrows < heads) & (col == DOCS + 3 * (row % hrows) + row // hrows), -1.0, 0.0)
    lse = dot(stack, put.astype(BF16), TN)
    bar = jnp.where((lane < DOCS) & (lane != segc_ref[...] + 1), NEG, 0.0)
    aux_ref[...] = (bar + lse + delta).astype(BF16)

    @pl.when(pl.program_id(0) == 0)
    def _():
        nv_ref[...] = jnp.zeros_like(nv_ref)
        fv_ref[...] = jnp.zeros_like(fv_ref)

    sums = (
        dx2 * z2,
        dh3 * z3,
        da.astype(F32),
        dx2,
        dh3,
        df.astype(F32),
        doc * o,
    )
    for i, term in enumerate(sums):
        nv_ref[i : i + 1, :] += jnp.sum(term, axis=0, keepdims=True)
    for i, terms in enumerate((gsum, usum, bsum)):
        fv_ref[i : i + 1, :] += jnp.concatenate(terms, axis=1)


def middle(tokens, oc, out_grad, weight, segc, lse, gains, biases, fgain, fbias, hs, w_out, w_up, w_down):
    n, d = tokens.shape
    ff = w_up.shape[1]
    blk = pl.BlockSpec((BLOCK, d), lambda i: (i, 0))
    wide = pl.BlockSpec((BLOCK, ff), lambda i: (i, 0))
    col = pl.BlockSpec((BLOCK, 1), lambda i: (i, 0))
    s = jax.ShapeDtypeStruct
    return pl.pallas_call(
        middle_body,
        grid=(n // BLOCK,),
        in_specs=[blk, blk, blk, col, col, pl.BlockSpec((lse.shape[0], BLOCK), lambda i: (0, i))]
        + [whole(x.shape) for x in (gains, biases, fgain, fbias, hs, w_out, w_up, w_down)],
        out_specs=[blk, blk, wide, blk, wide, blk, blk, blk, pl.BlockSpec((BLOCK, 128), lambda i: (i, 0))]
        + [pl.BlockSpec((8, d), lambda i: (0, 0)), pl.BlockSpec((8, ff), lambda i: (0, 0))],
        out_shape=[
            s((n, d), BF16), s((n, d), BF16), s((n, ff), BF16), s((n, d), BF16), s((n, ff), BF16),
            s((n, d), F32), s((n, d), BF16), s((n, d), BF16), s((n, 128), BF16), s((8, d), F32), s((8, ff), F32),
        ],
        scratch_shapes=[pltpu.VMEM((BLOCK, ff), F32)] * 3,
        compiler_params=params(58),
        cost_estimate=pl.CostEstimate(flops=30 * 10**9, bytes_accessed=40 * 2**20, transcendentals=0),
        name="middle",
    )(tokens, oc, out_grad, weight, segc, lse, gains, biases, fgain, fbias, hs, w_out, w_up, w_down)


def early_body(h3_ref, df_ref, da_ref, du_ref, m_ref, oc_ref, e_ref, ht, ft):
    i = pl.program_id(0)
    last = pl.num_programs(0) - 1

    @pl.when(i == 0)
    def _():
        ht[...] = h3_ref[...].astype(F32).T.astype(BF16)
        ft[...] = df_ref[...].astype(F32).T.astype(BF16)

    @pl.when((i % 2 == 0) & (i < last))
    def _():
        e_ref[...] = dot(ht[...], du_ref[...]).astype(BF16)

    @pl.when(i % 2 == 1)
    def _():
        e_ref[...] = dot(ft[...], m_ref[...]).astype(BF16)

    @pl.when(i == last)
    def _():
        e_ref[...] = dot(da_ref[...], oc_ref[...], TN).astype(BF16)


def early_grads(h3, df, da, du, m, oc, parts):
    n, d = h3.shape
    ff = du.shape[1]
    width = ff // parts
    assert width == d
    wide = pl.BlockSpec((n, width), lambda i: (0, jnp.minimum(i // 2, parts - 1)))
    return pl.pallas_call(
        early_body,
        grid=(2 * parts + 1,),
        in_specs=[whole((n, d))] * 3 + [wide, wide, whole((n, d))],
        out_specs=pl.BlockSpec((d, width), lambda i: (0, i)),
        out_shape=jax.ShapeDtypeStruct((d, 2 * ff + d), BF16),
        scratch_shapes=[pltpu.VMEM((d, n), BF16)] * 2,
        compiler_params=params(48),
        cost_estimate=pl.CostEstimate(flops=2 * n * d * (2 * ff + d), bytes_accessed=32 * 2**20, transcendentals=0),
        name="early_grads",
    )(h3, df, da, du, m, oc)


def late_body(h1_ref, dq_ref, dk_ref, dv_ref, out_ref, ht):
    ht[...] = h1_ref[...].astype(F32).T.astype(BF16)
    d = h1_ref.shape[1]
    for i, ref in enumerate((dq_ref, dk_ref, dv_ref)):
        out_ref[:, i * d : (i + 1) * d] = dot(ht[...], ref[...]).astype(BF16)


def late_grads(h1, dq, dk, dv):
    n, d = h1.shape
    return pl.pallas_call(
        late_body,
        out_shape=jax.ShapeDtypeStruct((d, 3 * d), BF16),
        scratch_shapes=[pltpu.VMEM((d, n), BF16)],
        compiler_params=params(48),
        cost_estimate=pl.CostEstimate(flops=6 * n * d * d, bytes_accessed=12 * 2**20, transcendentals=0),
        name="late_grads",
    )(h1, dq, dk, dv)


def input_body(tok_ref, dx2_ref, dq_ref, dk_ref, dv_ref, gains_ref, w_ref, tg_ref, nv_ref):
    z, r = normed(tok_ref[...].astype(F32))
    dh1 = (
        dot(dq_ref[...], w_ref[0], NT) + dot(dk_ref[...], w_ref[1], NT) + dot(dv_ref[...], w_ref[2], NT)
    )
    tg_ref[...] = (dx2_ref[...] + norm_back(dh1, gains_ref[0:1, :].astype(F32), z, r)).astype(BF16)

    @pl.when(pl.program_id(0) == 0)
    def _():
        nv_ref[...] = jnp.zeros_like(nv_ref)

    sums = (dh1 * z, dh1, dq_ref[...].astype(F32), dv_ref[...].astype(F32))
    for i, term in enumerate(sums):
        nv_ref[i : i + 1, :] += jnp.sum(term, axis=0, keepdims=True)


def input_grad(tokens, dx2, dq, dk, dv, gains, w_qkv):
    n, d = tokens.shape
    blk = pl.BlockSpec((BLOCK, d), lambda i: (i, 0))
    return pl.pallas_call(
        input_body,
        grid=(n // BLOCK,),
        in_specs=[blk] * 5 + [whole(gains.shape), whole(w_qkv.shape)],
        out_specs=[blk, pl.BlockSpec((8, d), lambda i: (0, 0))],
        out_shape=[jax.ShapeDtypeStruct((n, d), BF16), jax.ShapeDtypeStruct((8, d), F32)],
        compiler_params=params(40),
        cost_estimate=pl.CostEstimate(flops=6 * n * d * d, bytes_accessed=16 * 2**20, transcendentals=0),
        name="input_grad",
    )(tokens, dx2, dq, dk, dv, gains, w_qkv)


def tile_ranges(seg):
    seq = seg.shape[0]
    nb = seq // TILE
    blocks = seg.reshape(nb, TILE)
    first = blocks[:, 0]
    last = blocks[:, -1]
    pos = jnp.arange(seq)
    lo = jnp.min(jnp.where(seg[None, :] == first[:, None], pos[None, :], seq), axis=1)
    hi = jnp.max(jnp.where(seg[None, :] == last[:, None], pos[None, :] + 1, 0), axis=1)
    live = jnp.sum((seg >= 0).astype(jnp.int32))
    lo = lo // TILE
    hi = (hi + TILE - 1) // TILE
    hi_back = jnp.where(first >= 0, jnp.minimum(hi, (live + TILE - 1) // TILE), lo)
    return lo.astype(jnp.int32), hi.astype(jnp.int32), hi_back.astype(jnp.int32)


def add_all(x, axis):
    size = lax.axis_size(axis)
    step = 1
    while step < size:
        x = x + lax.ppermute(x, axis, [(i, i ^ step) for i in range(size)])
        step *= 2
    return x


def local(
    tokens, out_grad, segment_ids, row_tasks, rel_buckets, norm_gains, model_biases, w_qkv, qkv_bias,
    rel_bias, head_scale, w_out, w_up, ffn_gain, ffn_biases, w_down,
):
    parts = lax.axis_size("tensor")
    dps = lax.axis_size("dp")
    tensor_index = lax.axis_index("tensor")
    dp_index = lax.axis_index("dp")
    heads = head_scale.shape[0]
    d = tokens.shape[1]
    seq = segment_ids.shape[1]
    row_share = segment_ids.shape[0] // parts

    live_mask = (segment_ids >= 0).astype(F32)
    picked = (row_tasks[:, None] == jnp.arange(TASKS)[None, :]).astype(F32)
    counts = jnp.sum(picked * jnp.sum(live_mask, axis=1)[:, None], axis=0)
    counts = add_all(jnp.broadcast_to(counts[None, :], (8, TASKS)), "dp")[0]
    task_weights = jnp.sum(counts) / (TASKS * counts)

    rel_onehot = (jnp.arange(rel_bias.shape[1])[:, None] == rel_buckets[None, :]).astype(BF16)
    table = jnp.dot(rel_bias, rel_onehot, preferred_element_type=F32)
    rev = jnp.pad(table[:, ::-1], ((0, 0), (0, 1)))
    scale = head_scale.astype(F32)
    hs_row = jnp.repeat(scale, d // heads)[None, :]
    fgain = ffn_gain[None, :]
    qb = qkv_bias.reshape(2, d)

    assert row_share == 1
    own_tokens = lax.dynamic_slice_in_dim(tokens, tensor_index * seq, seq, 0)
    own_grad = lax.dynamic_slice_in_dim(out_grad, tensor_index * seq, seq, 0)
    seg = lax.dynamic_slice_in_dim(segment_ids, tensor_index, 1, 0)[0]
    own_task = lax.dynamic_slice_in_dim(picked, tensor_index, 1, 0)
    weight = (jnp.where(seg >= 0, 1.0, 0.0) * jnp.sum(own_task[0] * task_weights))[:, None]
    segc = seg[:, None]
    lo, hi, hi_back = tile_ranges(seg)

    h1, q, k, v = project(own_tokens, norm_gains, model_biases, w_qkv, qb)
    oc, lse, band = attend(q, k, v, segc, rev, lo, hi, scale)
    layer_out, h3, m, df, du, dx2, da, do, aux, nv, fv = middle(
        own_tokens, oc, own_grad, weight, segc, lse, norm_gains, model_biases, fgain, ffn_biases,
        hs_row, w_out, w_up, w_down,
    )
    layer_out = lax.all_gather(layer_out, "tensor", axis=0, tiled=True)
    early = early_grads(h3, df, da, du, m, oc, parts)
    early = lax.psum_scatter(early, "dp", scatter_dimension=0, tiled=True)
    dq, dk, dv, tg = attend_back(q, k, v, do, aux, segc, band, lo, hi_back)
    tokens_grad, nv2 = input_grad(own_tokens, dx2, dq, dk, dv, norm_gains, w_qkv)
    tokens_grad = lax.all_gather(tokens_grad, "tensor", axis=0, tiled=True)
    late = late_grads(h1, dq, dk, dv)
    late = lax.psum_scatter(late, "dp", scatter_dimension=0, tiled=True)

    piece = d // dps
    ff = w_up.shape[1]
    share = ff // parts
    cols = d // parts
    pair = early[:, : 2 * ff].reshape(piece, parts, 2 * share)
    small = jnp.concatenate([early[:, 2 * ff :], late], axis=1).reshape(piece, 4, parts, cols)
    pair = jnp.concatenate(
        [pair.transpose(1, 0, 2), small.transpose(2, 0, 1, 3).reshape(parts, piece, 4 * cols)], axis=2
    )
    pair = lax.psum_scatter(pair, "tensor", scatter_dimension=0, tiled=True)[0].astype(F32)
    up_grad = pair[:, :share]
    down_grad = pair[:, share : 2 * share].T
    small = pair[:, 2 * share :].reshape(piece, 4, cols)
    output_grad = small[:, 0].T
    project_grad = small[:, 1:].transpose(1, 0, 2)

    table_grad = tg[:, : 2 * seq - 1][:, ::-1]
    position = jnp.einsum("hs,bs->hb", table_grad, rel_onehot.astype(F32), precision=lax.Precision.HIGHEST)
    head_sum = jnp.sum(nv[6].reshape(heads, d // heads), axis=1)
    vec = jnp.concatenate(
        [
            nv2[0:1].reshape(-1), nv[0:2].reshape(-1),
            nv2[1:2].reshape(-1), nv[2:6].reshape(-1),
            nv2[2:4].reshape(-1),
            fv[0:3].reshape(-1),
            position.reshape(-1),
            head_sum,
        ]
    )
    size = vec.shape[0]
    vec = jnp.pad(vec, (0, -size % 1024)).reshape(-1, 128)
    vec = add_all(add_all(vec, "dp"), "tensor").reshape(-1)
    at = 0

    def take(shape):
        nonlocal at
        n = 1
        for s in shape:
            n *= s
        out = vec[at : at + n].reshape(shape)
        at += n
        return out

    gains_grad = lax.dynamic_slice_in_dim(take((3, d)), dp_index * piece, piece, 1)
    biases_grad = lax.dynamic_slice_in_dim(take((5, d)), dp_index * piece, piece, 1)
    hp = heads // parts
    project_bias = lax.dynamic_slice_in_dim(take((2, heads, d // heads)), tensor_index * hp, hp, 1)
    fgain_grad = lax.dynamic_slice_in_dim(take((ff,)), tensor_index * share, share, 0)
    fbias_grad = lax.dynamic_slice_in_dim(take((2, ff)), tensor_index * share, share, 1)
    position = take(position.shape)
    bp = position.shape[1] // dps
    position = lax.dynamic_slice(position, (tensor_index * hp, dp_index * bp), (hp, bp))
    head_grad = lax.dynamic_slice_in_dim(take((heads,)), tensor_index * hp, hp, 0)
    return (
        layer_out, tokens_grad, gains_grad, biases_grad, project_grad, project_bias, position, head_grad,
        output_grad, up_grad, fgain_grad, fbias_grad, down_grad,
    )


def solution(mesh):
    rows = P("dp", None)
    return jax.shard_map(
        local,
        mesh=mesh,
        in_specs=(rows, rows, rows, P("dp")) + (P(),) * 12,
        out_specs=(
            rows,
            rows,
            P(None, "dp"),
            P(None, "dp"),
            P(None, "dp", "tensor"),
            P(None, "tensor", None),
            P("tensor", "dp"),
            P("tensor"),
            P("tensor", "dp"),
            P("dp", "tensor"),
            P("tensor"),
            P(None, "tensor"),
            P("tensor", "dp"),
        ),
        check_vma=False,
    )
```

```python
import jax
import jax.numpy as jnp
from jax import lax
from jax.experimental import pallas as pl
from jax.experimental.pallas import tpu as pltpu
from jax.sharding import PartitionSpec as P

F32 = jnp.float32
BF16 = jnp.bfloat16
TASKS = 4
EPS = 1e-05
NEG = -1e30
LOG2E = 1.4426950408889634
HEAD = 64
TILE = 256
SUB = TILE // 128
BLOCK = 256
COST = 10**6
DOCS = 16
NT = (((1,), (1,)), ((), ()))
NN = (((1,), (0,)), ((), ()))
TN = (((0,), (0,)), ((), ()))


def dot(a, b, dims=NN):
    return lax.dot_general(a, b, dims, preferred_element_type=F32)


def split3(x):
    a = x.astype(BF16)
    r = x - a.astype(F32)
    b = r.astype(BF16)
    c = (r - b.astype(F32)).astype(BF16)
    return a, b, c


def normed(z):
    c = z - jnp.mean(z, axis=-1, keepdims=True)
    r = lax.rsqrt(jnp.mean(c * c, axis=-1, keepdims=True) + EPS)
    return c * r, r


def norm_back(dz, gain, zhat, r):
    s = dz * gain
    return r * (
        s
        - jnp.mean(s, axis=-1, keepdims=True)
        - zhat * jnp.mean(s * zhat, axis=-1, keepdims=True)
    )


def params(mib):
    return pltpu.CompilerParams(vmem_limit_bytes=mib * 2**20)


ANYWHERE = pl.BlockSpec(memory_space=pl.ANY)


def whole(shape):
    return pl.BlockSpec(shape, lambda *_: (0,) * len(shape), pipeline_mode=pl.Buffered(1))


def build_band(row):
    n = row.shape[1]
    x = pltpu.roll(jnp.broadcast_to(row, (8, n)), n - 127, 1, stride=1, stride_axis=0)
    k = 8
    while k < 128:
        x = jnp.concatenate([x, pltpu.roll(x, k, 1)], axis=0)
        k *= 2
    return x


def fold_band(x):
    r = x.shape[0]
    while r > 8:
        r //= 2
        x = pltpu.roll(x[:r], r, 1) + x[r:]
    out = x[7:8]
    for i in range(7):
        out = out + pltpu.roll(x[i : i + 1], 7 - i, 1)
    return out


def bias_tile(band, h, base):
    return jnp.concatenate(
        [
            jnp.concatenate([band[h, base + u - t] for u in range(SUB)], axis=1)
            for t in range(SUB)
        ],
        axis=0,
    )


def column(row):
    return jnp.broadcast_to(row.astype(F32), (8, row.shape[1])).T[:, 0:1]


def tile_range(segs, row, i, nb, back=False):
    ends = [(segs[row, t * TILE], segs[row, t * TILE + TILE - 1]) for t in range(nb)]
    first, last = ends[i]
    lo, hi = i, i + 1
    for t in range(i):
        lo = lo - (ends[t][1] == first).astype(jnp.int32)
    for t in range(i + 1, nb):
        shared = ends[t][0] == last
        if back:
            shared = shared & (last >= 0)
        hi = hi + shared.astype(jnp.int32)
    if back:
        hi = jnp.where(first >= 0, hi, lo)
    return lo, hi


def attend_body(
    row_ref, segs, tok_ref, seg_ref, gains_ref, biases_ref, w_ref, hv_ref, rev_ref, *rest
):
    oc_ref, lse_ref, h1t_hbm, q_hbm, k_hbm, v_hbm, band_hbm = rest[-19:-12]
    h1, h1t, q_s, k_s, v_s, band, vt, qx, km, acc, ml, sems = rest[-12:]
    row = row_ref[0]
    seq, d = tok_ref.shape
    nb = seq // TILE
    bw = seq // 128 - 1
    nh = d // HEAD
    tiles = 2 * seq // 128
    gain = gains_ref[0:1, :].astype(F32)
    shift = biases_ref[0:1, :].astype(F32)
    for b in range(seq // BLOCK):
        r = slice(b * BLOCK, (b + 1) * BLOCK)
        z, _ = normed(tok_ref[r, :].astype(F32))
        y = (z * gain + shift).astype(BF16)
        h1[r, :] = y
        h1t[:, r] = y.astype(F32).T.astype(BF16)
    lane = lax.broadcasted_iota(jnp.int32, (seq, 128), 1)
    doc = column(seg_ref[pl.ds(row, 1), :]).astype(jnp.int32) + 1
    zero = jnp.zeros((), BF16)
    hot = jnp.where(lane == doc, 1.0, 0.0).astype(BF16)
    bar = jnp.where((lane < DOCS) & (lane != doc), NEG, 0.0).astype(BF16)
    for c0 in range(0, d, 256):
        cc = slice(c0, c0 + 256)
        x = h1[...]
        q_s[:, cc] = (dot(x, w_ref[0, :, cc]) * 0.125 + hv_ref[1:2, cc] * 0.125).astype(BF16)
        k_s[:, cc] = dot(x, w_ref[1, :, cc]).astype(BF16)
        v_s[:, cc] = (dot(x, w_ref[2, :, cc]) - (-hv_ref[2:3, cc])).astype(BF16)
        for h in range(c0 // HEAD, c0 // HEAD + 4):
            full = build_band(rev_ref[h : h + 1, :]) * LOG2E
            for t in range(tiles):
                band[h, t] = full[:, 128 * t : 128 * t + 128]
            half = (lane < HEAD) if h % 2 == 0 else (lane >= HEAD)
            c = slice(128 * (h // 2), 128 * (h // 2) + 128)
            km[h, :, :128] = jnp.where(half, k_s[:, c], zero)
            km[h, :, 128:] = hot
        for j in (c0 // 128, c0 // 128 + 1):
            c = slice(128 * j, 128 * j + 128)
            qx[j, :, :128] = q_s[:, c]
            qx[j, :, 128:] = bar
            for b in range(nb):
                vt[b, c, :] = v_s[b * TILE : (b + 1) * TILE, c].astype(F32).T.astype(BF16)
    copies = [
        pltpu.make_async_copy(a, b, sems.at[i])
        for i, (a, b) in enumerate(
            ((h1t, h1t_hbm), (q_s, q_hbm), (k_s, k_hbm), (v_s, v_hbm), (band, band_hbm))
        )
    ]
    for copy in copies:
        copy.start()
    for qb in range(nb):
        qs = slice(qb * TILE, (qb + 1) * TILE)
        acc[...] = jnp.zeros_like(acc)
        ml[0] = jnp.full((nh, TILE), -jnp.inf, F32)
        ml[1] = jnp.zeros((nh, TILE), F32)

        def step(kb, _):
            ks = pl.ds(pl.multiple_of(kb * TILE, TILE), TILE)
            base = bw + SUB * qb - SUB * kb
            ss = [dot(km[h, ks, :], qx[h // 2, qs, :], NT) for h in range(nh)]
            for h in range(nh):
                s = ss[h] * LOG2E + bias_tile(band, h, base)
                old = ml[0, h : h + 1, :]
                top = jnp.maximum(old, jnp.max(s, axis=0, keepdims=True))
                fade = jnp.exp2(old - top)
                w = jnp.exp2(s - top)
                ml[0, h : h + 1, :] = top
                ml[1, h : h + 1, :] = ml[1, h : h + 1, :] * fade + jnp.sum(w, axis=0, keepdims=True)
                r = slice(HEAD * h, HEAD * h + HEAD)
                acc[r, :] = acc[r, :] * fade + dot(vt[kb, r, :], w.astype(BF16))
            return _

        lo, hi = tile_range(segs, row, qb, nb)
        lax.fori_loop(lo, hi, step, 0)
        for j in range(nh // 2):
            outs = []
            for h in (2 * j, 2 * j + 1):
                total = ml[1, h : h + 1, :]
                lse_ref[h : h + 1, qs] = ml[0, h : h + 1, :] * (1 / LOG2E) + jnp.log(total)
                outs.append(acc[HEAD * h : HEAD * h + HEAD, :] * (1.0 / total))
            c = slice(128 * j, 128 * j + 128)
            oc_ref[qs, c] = (jnp.concatenate(outs, axis=0).T * hv_ref[0:1, c]).astype(BF16)
    lse_ref[nh:, :] = jnp.zeros((lse_ref.shape[0] - nh, seq), F32)
    for copy in copies:
        copy.wait()


def attend(row, tokens, segs, gains, biases, w_qkv, hv, rev, after=()):
    d = tokens.shape[1]
    seq = segs.shape[1]
    nh = d // HEAD
    rows = -(-nh // 8) * 8
    tiles = 2 * seq // 128
    s = jax.ShapeDtypeStruct
    return pl.pallas_call(
        attend_body,
        grid_spec=pltpu.PrefetchScalarGridSpec(
            num_scalar_prefetch=2,
            grid=(1,),
            in_specs=[pl.BlockSpec((seq, d), lambda i, row, *_: (row[0], 0), pipeline_mode=pl.Buffered(1))]
            + [whole(x.shape) for x in (segs, gains, biases, w_qkv, hv, rev)]
            + [ANYWHERE] * len(after),
            out_specs=[whole((seq, d)), whole((rows, seq))] + [ANYWHERE] * 5,
            scratch_shapes=[pltpu.VMEM((seq, d), BF16), pltpu.VMEM((d, seq), BF16)]
            + [pltpu.VMEM((seq, d), BF16)] * 3
            + [
                pltpu.VMEM((nh, tiles, 128, 128), F32),
                pltpu.VMEM((seq // TILE, d, TILE), BF16),
                pltpu.VMEM((nh // 2, seq, 256), BF16),
                pltpu.VMEM((nh, seq, 256), BF16),
                pltpu.VMEM((d, TILE), F32),
                pltpu.VMEM((2, nh, TILE), F32),
                pltpu.SemaphoreType.DMA((5,)),
            ],
        ),
        out_shape=[s((seq, d), BF16), s((rows, seq), F32), s((d, seq), BF16)]
        + [s((seq, d), BF16)] * 3
        + [s((nh, tiles, 128, 128), F32)],
        compiler_params=params(60),
        cost_estimate=pl.CostEstimate(flops=COST, bytes_accessed=COST, transcendentals=0),
        name="attend",
    )(row, segs, tokens, segs, gains, biases, w_qkv, hv, rev, *after)


def attend_back_body(
    row_ref, segs, q_ref, k_ref, v_ref, do_ref, x_ref, seg_ref, band, h1t_ref, *rest
):
    dq_ref, dk_ref, dv_ref, tg_ref, wg_ref, gband, qx, dx, km, vm, kt, dqt, dka, dva = rest[-14:]
    seq = q_ref.shape[0]
    nb = seq // TILE
    bw = seq // 128 - 1
    nh = q_ref.shape[1] // HEAD
    heads = pl.num_programs(0) * nh
    first = pl.program_id(0) * nh
    lane = lax.broadcasted_iota(jnp.int32, (seq, 128), 1)
    row = row_ref[0]
    hot = lane == column(seg_ref[pl.ds(row, 1), :]).astype(jnp.int32) + 1
    zero = jnp.zeros((), BF16)
    gband[...] = jnp.zeros_like(gband)
    dqt[...] = jnp.zeros_like(dqt)
    for h in range(nh):
        half = (lane < HEAD) if h % 2 == 0 else (lane >= HEAD)
        c = slice(128 * (h // 2), 128 * (h // 2) + 128)
        at = DOCS + 3 * (first + h)
        km[h, :, :128] = jnp.where(half, k_ref[:, c], zero)
        km[h, :, 128:] = jnp.where(hot | ((lane >= at) & (lane < at + 3)), 1.0, 0.0).astype(BF16)
        at = at + 3 * heads
        vm[h, :, :128] = jnp.where(half, v_ref[:, c], zero)
        vm[h, :, 128:] = jnp.where((lane >= at) & (lane < at + 3), 1.0, 0.0).astype(BF16)
    for j in range(nh // 2):
        c = slice(128 * j, 128 * j + 128)
        qx[j, :, :128] = q_ref[:, c]
        qx[j, :, 128:] = x_ref[...]
        dx[j, :, :128] = do_ref[:, c]
        dx[j, :, 128:] = x_ref[...]
        kt[c, :] = k_ref[:, c].astype(F32).T.astype(BF16)
    low = lax.broadcasted_iota(jnp.int32, (TILE, 128), 1) < HEAD
    for kb in range(nb):
        dka[...] = jnp.zeros_like(dka)
        dva[...] = jnp.zeros_like(dva)
        ks = slice(kb * TILE, (kb + 1) * TILE)

        def step(qb, _):
            qs = pl.ds(pl.multiple_of(qb * TILE, TILE), TILE)
            base = bw + SUB * qb - SUB * kb
            ss = [dot(km[h, ks, :], qx[h // 2, qs, :], NT) for h in range(nh)]
            dps = [dot(vm[h, ks, :], dx[h // 2, qs, :], NT) for h in range(nh)]
            for h in range(nh):
                w = jnp.exp2(ss[h] * LOG2E + bias_tile(band, h, base))
                ds = (w * dps[h]).astype(BF16)
                dsf = ds.astype(F32)
                for off in range(1 - SUB, SUB):
                    total = None
                    for t in range(SUB):
                        u = off + t
                        if 0 <= u < SUB:
                            piece = dsf[128 * t : 128 * t + 128, 128 * u : 128 * u + 128]
                            total = piece if total is None else total + piece
                    gband[h, base + off] += total
                dva[h] += dot(w.astype(BF16), dx[h // 2, qs, :128])
                dka[h] += dot(ds, qx[h // 2, qs, :128])
                r = slice(HEAD * h, HEAD * h + HEAD)
                dqt[qb, r, :] += dot(kt[r, ks], ds)
            return _

        lo, hi = tile_range(segs, row, kb, nb, True)
        lax.fori_loop(lo, hi, step, 0)
        for j in range(nh // 2):
            c = slice(128 * j, 128 * j + 128)
            dk_ref[ks, c] = jnp.where(low, dka[2 * j], dka[2 * j + 1]).astype(BF16)
            dv_ref[ks, c] = jnp.where(low, dva[2 * j], dva[2 * j + 1]).astype(BF16)
    for j in range(nh // 2):
        c = slice(128 * j, 128 * j + 128)
        for b in range(nb):
            dq_ref[b * TILE : (b + 1) * TILE, c] = (
                dqt[b, c, :].T.astype(BF16).astype(F32) * 0.125
            ).astype(BF16)
    wide = HEAD * nh
    for i, ref in enumerate((dq_ref, dk_ref, dv_ref)):
        wg_ref[:, i * wide : (i + 1) * wide] = dot(h1t_ref[...], ref[...]).astype(BF16)
    for h in range(nh):
        tg_ref[0, h : h + 1, :] = fold_band(
            jnp.concatenate([gband[h, t] for t in range(2 * seq // 128)], axis=1)
        )


def attend_back(row, q, k, v, do, aux, segs, band, h1t, grads):
    seq, width = q.shape
    heads = width // HEAD
    nh = 4 if heads % 4 == 0 else 2
    groups = heads // nh
    blk = pl.BlockSpec((seq, HEAD * nh), lambda p, *_: (0, p))
    tiles = 2 * seq // 128
    start = (grads.shape[1] - 3 * width) // (3 * HEAD * nh)
    assert start * 3 * HEAD * nh == grads.shape[1] - 3 * width
    dq, dk, dv, tg, wg = pl.pallas_call(
        attend_back_body,
        grid_spec=pltpu.PrefetchScalarGridSpec(
            num_scalar_prefetch=2,
            grid=(groups,),
            in_specs=[blk] * 4
            + [
                pl.BlockSpec((seq, 128), lambda p, *_: (0, 0)),
                whole(segs.shape),
                pl.BlockSpec((nh, tiles, 128, 128), lambda p, *_: (p, 0, 0, 0)),
                whole(h1t.shape),
            ]
            + [ANYWHERE],
            out_specs=[blk] * 3
            + [
                pl.BlockSpec((1, nh, 2 * seq), lambda p, *_: (p, 0, 0)),
                pl.BlockSpec((width, 3 * HEAD * nh), lambda p, *_: (0, start + p)),
            ],
            scratch_shapes=[
                pltpu.VMEM((nh, tiles, 128, 128), F32),
                pltpu.VMEM((nh // 2, seq, 256), BF16),
                pltpu.VMEM((nh // 2, seq, 256), BF16),
                pltpu.VMEM((nh, seq, 256), BF16),
                pltpu.VMEM((nh, seq, 256), BF16),
                pltpu.VMEM((HEAD * nh, seq), BF16),
                pltpu.VMEM((seq // TILE, HEAD * nh, TILE), F32),
                pltpu.VMEM((nh, TILE, 128), F32),
                pltpu.VMEM((nh, TILE, 128), F32),
            ],
        ),
        out_shape=[jax.ShapeDtypeStruct((seq, width), BF16)] * 3
        + [jax.ShapeDtypeStruct((groups, nh, 2 * seq), F32), jax.ShapeDtypeStruct(grads.shape, BF16)],
        input_output_aliases={10: 4},
        compiler_params=params(60),
        cost_estimate=pl.CostEstimate(flops=COST, bytes_accessed=COST, transcendentals=0),
        name="attend_back",
    )(row, segs, q, k, v, do, aux, segs, band, h1t, grads)
    return dq, dk, dv, tg.reshape(heads, 2 * seq), wg, groups


def gelu_parts(u):
    dens = jnp.exp2(u * u * (-0.5 * LOG2E))
    t = 1.0 / (1.0 + (0.3275911 * 0.7071067811865476) * jnp.abs(u))
    poly = t * (0.127414796 + t * (-0.142248368 + t * (0.7107068705 + t * (-0.7265760135 + t * 0.5307027145))))
    tail = poly * dens
    phi = jnp.where(u >= 0, 1.0 - tail, tail)
    return phi, phi + u * (dens * 0.3989422804014327)


STEP = 512


def middle_body(
    row_ref, tok_ref, oc_ref, gains_ref, biases_ref, fgain_ref, fbias_ref, wo_ref, wu_ref, wd_ref, *rest
):
    out_ref, h3_ref, m_ref, mh_ref, gp_ref, z_ref, stat_ref, e_s = rest[-8:]
    ff = wu_ref.shape[1]
    gains = gains_ref[...].astype(F32)
    biases = biases_ref[...].astype(F32)
    tok = tok_ref[...].astype(F32)
    n, d = tok.shape
    z2, r2 = normed(dot(oc_ref[...], wo_ref[...]) - (-biases[1:2]))
    x2 = tok + (z2 * gains[1:2] + biases[2:3])
    z3, r3 = normed(x2)
    h3 = (z3 * gains[2:3] + biases[3:4]).astype(BF16)
    h3_ref[...] = h3
    z_ref[:, :d] = z2.astype(BF16)
    z_ref[:, d:] = z3.astype(BF16)
    s1 = jnp.zeros((n, 1), F32)
    s2 = jnp.zeros((n, 1), F32)
    for c0 in range(0, ff, STEP):
        c = slice(c0, c0 + STEP)
        u = dot(h3, wu_ref[:, c]) - (-fbias_ref[0:1, c].astype(F32))
        phi, slope = gelu_parts(u)
        e = u * phi
        e_s[:, c] = e
        gp_ref[:, c] = slope.astype(BF16)
        s1 += jnp.sum(e, axis=1, keepdims=True)
        s2 += jnp.sum(e * e, axis=1, keepdims=True)
    mean = s1 / ff
    r = lax.rsqrt(s2 / ff - mean * mean + EPS)
    y = jnp.zeros((n, d), F32)
    for c0 in range(0, ff, STEP):
        c = slice(c0, c0 + STEP)
        mh = (e_s[:, c] - mean) * r
        mh_ref[:, c] = mh.astype(BF16)
        m = (mh * fgain_ref[0:1, c].astype(F32) + fbias_ref[1:2, c].astype(F32)).astype(BF16)
        m_ref[:, c] = m
        y += dot(m, wd_ref[c, :])
    out_ref[...] = (x2 + (y + biases[4:5])).astype(BF16)
    lane = lax.broadcasted_iota(jnp.int32, (n, 128), 1)
    stat_ref[...] = jnp.where(lane == 0, r2, jnp.where(lane == 1, r3, r))


def middle(row, tokens, oc, gains, biases, fgain, fbias, w_out, w_up, w_down, after=()):
    n, d = oc.shape
    ff = w_up.shape[1]
    steps = n // BLOCK
    blk = pl.BlockSpec((BLOCK, d), lambda i, row: (i, 0))
    wide = pl.BlockSpec((BLOCK, ff), lambda i, row: (i, 0))
    s = jax.ShapeDtypeStruct
    return pl.pallas_call(
        middle_body,
        grid_spec=pltpu.PrefetchScalarGridSpec(
            num_scalar_prefetch=1,
            grid=(steps,),
            in_specs=[pl.BlockSpec((BLOCK, d), lambda i, row: (row[0] * steps + i, 0)), blk]
            + [whole(x.shape) for x in (gains, biases, fgain, fbias, w_out, w_up, w_down)]
            + [ANYWHERE] * len(after),
            out_specs=[
                blk, blk, wide, wide, wide,
                pl.BlockSpec((BLOCK, 2 * d), lambda i, row: (i, 0)),
                pl.BlockSpec((BLOCK, 128), lambda i, row: (i, 0)),
            ],
            scratch_shapes=[pltpu.VMEM((BLOCK, ff), F32)],
        ),
        out_shape=[s((n, d), BF16)] * 2 + [s((n, ff), BF16)] * 3 + [s((n, 2 * d), BF16), s((n, 128), F32)],
        compiler_params=params(60),
        cost_estimate=pl.CostEstimate(flops=COST, bytes_accessed=COST, transcendentals=0),
        name="middle",
    )(row, tokens, oc, gains, biases, fgain, fbias, w_out, w_up, w_down, *after)


def task_weight(counts_ref, tasks):
    counts = counts_ref[0:1, :]
    lane = lax.broadcasted_iota(jnp.int32, counts.shape, 1)
    own = jnp.sum(jnp.where(lane == tasks[0], counts, 0.0), axis=1, keepdims=True)
    return jnp.sum(counts, axis=1, keepdims=True) / (TASKS * own)


def middle_back_body(
    row_ref, tasks, og_ref, seg_ref, counts_ref, oc_ref, lse_ref, mh_ref, gp_ref, z_ref, stat_ref,
    gains_ref, fgain_ref, hs_ref, wo_ref, wu_ref, wd_ref, *rest
):
    du_ref, dx2_ref, da_ref, do_ref, aux_ref, nv_ref, fv_ref, d_s = rest[-8:]
    d, ff = wu_ref.shape
    heads = d // HEAD
    gains = gains_ref[...].astype(F32)
    oc = oc_ref[...]
    rows = oc.shape[0]
    here = pl.ds(pl.multiple_of(pl.program_id(0) * rows, rows), rows)
    doc = column(seg_ref[pl.ds(row_ref[0], 1), here])
    g = og_ref[...].astype(F32) * jnp.where(doc >= 0, task_weight(counts_ref, tasks), 0.0)
    df = g.astype(BF16)
    r2 = stat_ref[:, 0:1]
    r3 = stat_ref[:, 1:2]
    r = stat_ref[:, 2:3]
    b1 = jnp.zeros((rows, 1), F32)
    b2 = jnp.zeros((rows, 1), F32)
    gsum, bsum, usum = [], [], []
    for c0 in range(0, ff, STEP):
        c = slice(c0, c0 + STEP)
        mh = mh_ref[:, c].astype(F32)
        dm = dot(df, wd_ref[c, :], NT)
        gsum.append(jnp.sum(dm * mh, axis=0, keepdims=True))
        bsum.append(jnp.sum(dm, axis=0, keepdims=True))
        sc = dm * fgain_ref[0:1, c].astype(F32)
        d_s[:, c] = sc
        b1 += jnp.sum(sc, axis=1, keepdims=True)
        b2 += jnp.sum(sc * mh, axis=1, keepdims=True)
    b1 = b1 / ff
    b2 = b2 / ff
    dh3 = jnp.zeros((rows, d), F32)
    for c0 in range(0, ff, STEP):
        c = slice(c0, c0 + STEP)
        de = r * (d_s[:, c] - b1 - mh_ref[:, c].astype(F32) * b2)
        du = (de * gp_ref[:, c].astype(F32)).astype(BF16)
        du_ref[:, c] = du
        usum.append(jnp.sum(du.astype(F32), axis=0, keepdims=True))
        dh3 += dot(du, wu_ref[:, c], NT)
    z2 = z_ref[:, :d].astype(F32)
    z3 = z_ref[:, d:].astype(F32)
    dx2 = g + norm_back(dh3, gains[2:3], z3, r3)
    dx2_ref[...] = dx2
    da = norm_back(dx2, gains[1:2], z2, r2).astype(BF16)
    da_ref[...] = da
    doc_ = dot(da, wo_ref[...], NT)
    hs = hs_ref[0:1, :]
    o = oc.astype(F32) / hs
    do = (doc_ * hs).astype(BF16)
    do_ref[...] = do

    prod = do.astype(F32) * o
    hi = prod.astype(BF16)
    lo = (prod - hi.astype(F32)).astype(BF16)
    at = DOCS + 3 * heads
    head_of = lax.broadcasted_iota(jnp.int32, (d, 128), 0) // HEAD
    lane = lax.broadcasted_iota(jnp.int32, (d, 128), 1)
    put = jnp.where((lane >= at + 3 * head_of) & (lane < at + 3 * head_of + 3), -1.0, 0.0).astype(BF16)
    delta = dot(hi, put) + dot(lo, put)
    pa, pb, pc = split3(delta)
    lane = lax.broadcasted_iota(jnp.int32, (rows, 128), 1)
    part = (lane - at + 3 * 128) % 3
    delta = jnp.where(part == 0, pa.astype(F32), jnp.where(part == 1, pb.astype(F32), pc.astype(F32)))
    hrows = lse_ref.shape[0]
    la, lb, lc = split3(lse_ref[...])
    stack = jnp.concatenate([la.astype(F32), lb.astype(F32), lc.astype(F32)], axis=0).astype(BF16)
    row = lax.broadcasted_iota(jnp.int32, (3 * hrows, 128), 0)
    col = lax.broadcasted_iota(jnp.int32, (3 * hrows, 128), 1)
    put = jnp.where((row % hrows < heads) & (col == DOCS + 3 * (row % hrows) + row // hrows), -1.0, 0.0)
    lse = dot(stack, put.astype(BF16), TN)
    bar = jnp.where((lane < DOCS) & (lane != doc.astype(jnp.int32) + 1), NEG, 0.0)
    aux_ref[...] = (bar + lse + delta).astype(BF16)

    @pl.when(pl.program_id(0) == 0)
    def _():
        nv_ref[...] = jnp.zeros_like(nv_ref)
        fv_ref[...] = jnp.zeros_like(fv_ref)

    sums = (dx2 * z2, dh3 * z3, da.astype(F32), dx2, dh3, df.astype(F32), doc_ * o)
    for i, term in enumerate(sums):
        nv_ref[i : i + 1, :] += jnp.sum(term, axis=0, keepdims=True)
    for i, terms in enumerate((gsum, usum, bsum)):
        fv_ref[i : i + 1, :] += jnp.concatenate(terms, axis=1)


def middle_back(row, tasks, counts, out_grad, segs, oc, lse, mh, gp, z, stat, gains, fgain, hs, w_out, w_up, w_down, after=()):
    n, d = oc.shape
    ff = w_up.shape[1]
    steps = n // BLOCK
    blk = pl.BlockSpec((BLOCK, d), lambda i, *_: (i, 0))
    wide = pl.BlockSpec((BLOCK, ff), lambda i, *_: (i, 0))
    thin = pl.BlockSpec((BLOCK, 128), lambda i, *_: (i, 0))
    s = jax.ShapeDtypeStruct
    return pl.pallas_call(
        middle_back_body,
        grid_spec=pltpu.PrefetchScalarGridSpec(
            num_scalar_prefetch=2,
            grid=(steps,),
            in_specs=[
                pl.BlockSpec((BLOCK, d), lambda i, row, *_: (row[0] * steps + i, 0)),
                whole(segs.shape),
                whole(counts.shape),
                blk,
                pl.BlockSpec((lse.shape[0], BLOCK), lambda i, *_: (0, i)),
                wide, wide, pl.BlockSpec((BLOCK, 2 * d), lambda i, *_: (i, 0)), thin,
            ]
            + [whole(x.shape) for x in (gains, fgain, hs, w_out, w_up, w_down)]
            + [ANYWHERE] * len(after),
            out_specs=[
                wide, blk, blk, blk, thin,
                pl.BlockSpec((8, d), lambda i, *_: (0, 0)),
                pl.BlockSpec((8, ff), lambda i, *_: (0, 0)),
            ],
            scratch_shapes=[pltpu.VMEM((BLOCK, ff), F32)],
        ),
        out_shape=[
            s((n, ff), BF16), s((n, d), F32), s((n, d), BF16), s((n, d), BF16), s((n, 128), BF16), s((8, d), F32), s((8, ff), F32),
        ],
        compiler_params=params(60),
        cost_estimate=pl.CostEstimate(flops=COST, bytes_accessed=COST, transcendentals=0),
        name="middle_back",
    )(row, tasks, out_grad, segs, counts, oc, lse, mh, gp, z, stat, gains, fgain, hs, w_out, w_up, w_down, *after)


def down_body(row_ref, tasks, og_ref, seg_ref, counts_ref, m_ref, out_ref, ft):
    @pl.when(pl.program_id(0) == 0)
    def _():
        live = jnp.where(seg_ref[pl.ds(row_ref[0], 1), :] >= 0, task_weight(counts_ref, tasks), 0.0)
        ft[...] = (og_ref[...].astype(F32).T * live).astype(BF16)

    out_ref[...] = dot(ft[...], m_ref[...]).astype(BF16)


def down_grads(row, tasks, counts, out_grad, segs, m):
    n, ff = m.shape
    d = out_grad.shape[1]
    width = 512
    once = pl.Buffered(1)
    return pl.pallas_call(
        down_body,
        grid_spec=pltpu.PrefetchScalarGridSpec(
            num_scalar_prefetch=2,
            grid=(ff // width,),
            in_specs=[
                pl.BlockSpec((n, d), lambda i, row, *_: (row[0], 0), pipeline_mode=once),
                whole(segs.shape),
                whole(counts.shape),
                pl.BlockSpec((n, width), lambda i, *_: (0, i)),
            ],
            out_specs=pl.BlockSpec((d, width), lambda i, *_: (0, i)),
            scratch_shapes=[pltpu.VMEM((d, n), BF16)],
        ),
        out_shape=jax.ShapeDtypeStruct((d, ff), BF16),
        compiler_params=params(60),
        cost_estimate=pl.CostEstimate(flops=COST, bytes_accessed=COST, transcendentals=0),
        name="down_grads",
    )(row, tasks, out_grad, segs, counts, m)


def up_body(h3_ref, da_ref, du_ref, oc_ref, *rest):
    out_ref, ht, at = rest[-3:]
    i = pl.program_id(0)
    wide = pl.num_programs(0) - 2

    @pl.when(i == 0)
    def _():
        ht[...] = h3_ref[...].astype(F32).T.astype(BF16)
        at[...] = da_ref[...].astype(F32).T.astype(BF16)

    @pl.when(i < wide)
    def _():
        out_ref[...] = dot(ht[...], du_ref[...]).astype(BF16)

    @pl.when(i >= wide)
    def _():
        out_ref[...] = dot(at[...], oc_ref[...]).astype(BF16)


def up_grads(h3, da, du, oc, after=()):
    n, d = h3.shape
    ff = du.shape[1]
    width = d // 2
    wide = ff // width
    return pl.pallas_call(
        up_body,
        grid=(wide + 2,),
        in_specs=[whole((n, d))] * 2
        + [
            pl.BlockSpec((n, width), lambda i: (0, jnp.minimum(i, wide - 1))),
            pl.BlockSpec((n, width), lambda i: (0, jnp.maximum(i - wide, 0))),
        ]
        + [pl.BlockSpec(memory_space=pl.ANY)] * len(after),
        out_specs=pl.BlockSpec((d, width), lambda i: (0, i)),
        out_shape=jax.ShapeDtypeStruct((d, ff + 4 * d), BF16),
        scratch_shapes=[pltpu.VMEM((d, n), BF16)] * 2,
        compiler_params=params(60),
        cost_estimate=pl.CostEstimate(flops=COST, bytes_accessed=COST, transcendentals=0),
        name="up_grads",
    )(h3, da, du, oc, *after)


def input_body(row_ref, tok_ref, dx2_ref, dq_ref, dk_ref, dv_ref, gains_ref, w_ref, *rest):
    tg_ref, nv_ref = rest[-2:]
    z, r = normed(tok_ref[...].astype(F32))
    dh1 = (
        dot(dq_ref[...], w_ref[0], NT) + dot(dk_ref[...], w_ref[1], NT) + dot(dv_ref[...], w_ref[2], NT)
    )
    tg_ref[...] = (dx2_ref[...] + norm_back(dh1, gains_ref[0:1, :].astype(F32), z, r)).astype(BF16)

    @pl.when(pl.program_id(0) == 0)
    def _():
        nv_ref[...] = jnp.zeros_like(nv_ref)

    sums = (dh1 * z, dh1, dq_ref[...].astype(F32), dv_ref[...].astype(F32))
    for i, term in enumerate(sums):
        nv_ref[i : i + 1, :] += jnp.sum(term, axis=0, keepdims=True)


def input_grad(row, tokens, dx2, dq, dk, dv, gains, w_qkv, after=()):
    n, d = dx2.shape
    steps = n // BLOCK
    blk = pl.BlockSpec((BLOCK, d), lambda i, row: (i, 0))
    return pl.pallas_call(
        input_body,
        grid_spec=pltpu.PrefetchScalarGridSpec(
            num_scalar_prefetch=1,
            grid=(steps,),
            in_specs=[pl.BlockSpec((BLOCK, d), lambda i, row: (row[0] * steps + i, 0))]
            + [blk] * 4
            + [whole(gains.shape), whole(w_qkv.shape)]
            + [pl.BlockSpec(memory_space=pl.ANY)] * len(after),
            out_specs=[blk, pl.BlockSpec((8, d), lambda i, row: (0, 0))],
        ),
        out_shape=[jax.ShapeDtypeStruct((n, d), BF16), jax.ShapeDtypeStruct((8, d), F32)],
        compiler_params=params(60),
        cost_estimate=pl.CostEstimate(flops=10**10, bytes_accessed=COST, transcendentals=0),
        name="input_grad",
    )(row, tokens, dx2, dq, dk, dv, gains, w_qkv, *after)


def gate_body(*refs):
    refs[-1][0] = 0


def gate(x, *after):
    return pl.pallas_call(
        gate_body,
        in_specs=[ANYWHERE] * (1 + len(after)),
        out_specs=[ANYWHERE, pl.BlockSpec(memory_space=pltpu.SMEM)],
        out_shape=[jax.ShapeDtypeStruct(x.shape, x.dtype), jax.ShapeDtypeStruct((1,), jnp.int32)],
        input_output_aliases={0: 0},
        cost_estimate=pl.CostEstimate(flops=COST, bytes_accessed=COST, transcendentals=0),
        name="gate",
    )(x, *after)[0]


def copy_body(x_ref, o_ref):
    o_ref[...] = x_ref[...]


def copy(x):
    n, d = x.shape
    blk = pl.BlockSpec((n // 8, d), lambda i: (i, 0))
    return pl.pallas_call(
        copy_body,
        grid=(8,),
        in_specs=[blk],
        out_specs=blk,
        out_shape=jax.ShapeDtypeStruct(x.shape, x.dtype),
        name="copy",
    )(x)


def spread_body(row_ref, pair_ref, right_ref, left_ref, qkv_out, o_out, up_out, down_out):
    share = up_out.shape[1]
    cols = qkv_out.shape[2]
    pair = pair_ref[0].astype(F32) + right_ref[...].astype(F32) + left_ref[...].astype(F32)
    down_out[...] = pair[:, :share]
    up_out[...] = pair[:, share : 2 * share]
    small = pair[:, 2 * share :]
    o_out[...] = small[:, :cols].T
    for i in range(3):
        qkv_out[i] = small[:, (i + 1) * cols : (i + 2) * cols]


def spread(row, pair, pair_sums, share):
    _, n, width = pair.shape
    cols = (width - 2 * share) // 4
    s = jax.ShapeDtypeStruct
    own = lambda x: pl.BlockSpec((1,) + x.shape[1:], lambda i, row: (row[0], 0, 0))
    other = lambda x: pl.BlockSpec(x.shape[1:], lambda i, row: (0, 0))
    outs = [s((3, n, cols), F32), s((cols, n), F32), s((n, share), F32), s((n, share), F32)]
    return pl.pallas_call(
        spread_body,
        grid_spec=pltpu.PrefetchScalarGridSpec(
            num_scalar_prefetch=1,
            grid=(1,),
            in_specs=[own(pair), other(pair), other(pair)],
            out_specs=[pl.BlockSpec(x.shape, lambda i, row, k=len(x.shape): (0,) * k) for x in outs],
        ),
        out_shape=outs,
        name="spread",
    )(row, pair, *pair_sums)


def line_sums(blocks, axis):
    size = lax.axis_size(axis)
    me = lax.axis_index(axis)
    right = left = None
    for step in range(1, size):
        at = jnp.minimum(size - step + me, size - 1)
        pairs = [(i, i + 1) for i in range(step)]
        send = lax.dynamic_index_in_dim(blocks, at, 0, keepdims=False)
        right = lax.ppermute(send if right is None else send + right, axis, pairs)
        at = jnp.maximum(step - 1 - (size - 1 - me), 0)
        pairs = [(size - 1 - i, size - 2 - i) for i in range(step)]
        send = lax.dynamic_index_in_dim(blocks, at, 0, keepdims=False)
        left = lax.ppermute(send if left is None else send + left, axis, pairs)
    return right, left


def partial_sums(x, axis):
    size = lax.axis_size(axis)
    sums = [x]
    step = 1
    while step < size:
        sums.append(sums[-1] + lax.ppermute(sums[-1], axis, [(i, i ^ step) for i in range(size)]))
        step *= 2
    return sums


def add_all(x, axis):
    return partial_sums(x, axis)[-1]


def local(
    tokens, out_grad, segment_ids, row_tasks, rel_buckets, norm_gains, model_biases, w_qkv, qkv_bias,
    rel_bias, head_scale, w_out, w_up, ffn_gain, ffn_biases, w_down,
):
    parts = lax.axis_size("tensor")
    dps = lax.axis_size("dp")
    tensor_index = lax.axis_index("tensor")
    dp_index = lax.axis_index("dp")
    heads = head_scale.shape[0]
    d = tokens.shape[1]
    ff = w_up.shape[1]
    rows, seq = segment_ids.shape
    assert rows == parts

    live = jnp.sum((segment_ids >= 0).astype(F32), axis=1, keepdims=True)
    counts = jnp.sum(jnp.where(row_tasks[:, None] == jnp.arange(TASKS)[None, :], live, 0.0), axis=0)
    sums = partial_sums(jnp.broadcast_to(counts[None, :], (8, TASKS)), "dp")
    counts = sums[-1]

    back = jnp.pad(rel_buckets, (1, 0), constant_values=-1)[::-1]
    onehot = (jnp.arange(rel_bias.shape[1])[:, None] == back[None, :]).astype(BF16)
    rev = jnp.dot(rel_bias, onehot, preferred_element_type=F32)
    hv = jnp.concatenate(
        [jnp.broadcast_to(head_scale[None, :, None], (1, heads, d // heads)), qkv_bias], axis=0
    )
    hv = hv.astype(F32).reshape(3, d)
    fgain = ffn_gain[None, :]
    segs = segment_ids
    row = tensor_index[None]

    oc, lse, h1t, q, k, v, band = attend(
        row, tokens, segs, norm_gains, model_biases, w_qkv, hv, rev, sums[1:2]
    )
    layer_out, h3, m, mh, gp, z, stat = middle(
        row, tokens, oc, norm_gains, model_biases, fgain, ffn_biases, w_out, w_up, w_down, sums[2:3]
    )
    piece = d // dps
    share = ff // parts
    cols = d // parts
    layer_out = lax.all_gather(layer_out, "tensor", axis=0, tiled=True)
    down = down_grads(row, row_tasks, counts, out_grad, segs, m)
    du, dx2, da, do, aux, nv, fv = middle_back(
        row, row_tasks, counts, out_grad, segs, oc, lse, mh, gp, z, stat, norm_gains, fgain, hv, w_out, w_up,
        w_down, (down,),
    )
    down = lax.psum_scatter(down, "dp", scatter_dimension=0, tiled=True)
    dq, dk, dv, tg, rest, groups = attend_back(
        row, q, k, v, do, aux, segs, band, h1t, up_grads(h3, da, du, oc)
    )
    rest = lax.psum_scatter(rest, "dp", scatter_dimension=0, tiled=True)
    tokens_grad, nv2 = input_grad(row, tokens, dx2, dq, dk, dv, norm_gains, w_qkv, (layer_out,))
    down = gate(down, nv2)
    layer_out = copy(layer_out)
    tokens_grad = lax.all_gather(tokens_grad, "tensor", axis=0, tiled=True)

    pair = jnp.concatenate([down.reshape(piece, parts, share), rest[:, :ff].reshape(piece, parts, share)], axis=2)
    late = rest[:, ff + d :].reshape(piece, groups, 3, d // groups).transpose(0, 2, 1, 3).reshape(piece, 3 * d)
    small = jnp.concatenate([rest[:, ff : ff + d], late], axis=1).reshape(piece, 4, parts, cols)
    small = small.transpose(0, 2, 1, 3).reshape(piece, parts, 4 * cols)
    pair = jnp.concatenate([pair, small], axis=2).transpose(1, 0, 2)
    pair_sums = line_sums(pair, "tensor")
    project_grad, output_grad, up_grad, down_grad = spread(row, pair, pair_sums, share)
    down_grad = down_grad.T

    position = jnp.einsum("hs,bs->hb", tg, onehot.astype(F32), precision=lax.Precision.HIGHEST)
    head_sum = jnp.sum(nv[6].reshape(heads, d // heads), axis=1)
    vec = jnp.concatenate(
        [
            nv2[0:1].reshape(-1), nv[0:2].reshape(-1),
            nv2[1:2].reshape(-1), nv[2:6].reshape(-1),
            nv2[2:4].reshape(-1),
            fv[0:3].reshape(-1),
            position.reshape(-1),
            head_sum,
        ]
    )
    size = vec.shape[0]
    vec = jnp.pad(vec, (0, -size % 1024)).reshape(-1, 128)
    vec = add_all(add_all(vec, "dp"), "tensor").reshape(-1)
    at = 0

    def take(shape):
        nonlocal at
        n = 1
        for s in shape:
            n *= s
        out = vec[at : at + n].reshape(shape)
        at += n
        return out

    gains_grad = lax.dynamic_slice_in_dim(take((3, d)), dp_index * piece, piece, 1)
    biases_grad = lax.dynamic_slice_in_dim(take((5, d)), dp_index * piece, piece, 1)
    hp = heads // parts
    project_bias = lax.dynamic_slice_in_dim(take((2, heads, d // heads)), tensor_index * hp, hp, 1)
    fgain_grad = lax.dynamic_slice_in_dim(take((ff,)), tensor_index * share, share, 0)
    fbias_grad = lax.dynamic_slice_in_dim(take((2, ff)), tensor_index * share, share, 1)
    position = take(position.shape)
    bp = position.shape[1] // dps
    position = lax.dynamic_slice(position, (tensor_index * hp, dp_index * bp), (hp, bp))
    head_grad = lax.dynamic_slice_in_dim(take((heads,)), tensor_index * hp, hp, 0)
    return (
        layer_out, tokens_grad, gains_grad, biases_grad, project_grad, project_bias, position, head_grad,
        output_grad, up_grad, fgain_grad, fbias_grad, down_grad,
    )


def solution(mesh):
    rows = P("dp", None)
    return jax.shard_map(
        local,
        mesh=mesh,
        in_specs=(rows, rows, rows, P("dp")) + (P(),) * 12,
        out_specs=(
            rows,
            rows,
            P(None, "dp"),
            P(None, "dp"),
            P(None, "dp", "tensor"),
            P(None, "tensor", None),
            P("tensor", "dp"),
            P("tensor"),
            P("tensor", "dp"),
            P("dp", "tensor"),
            P("tensor"),
            P(None, "tensor"),
            P("tensor", "dp"),
        ),
        check_vma=False,
    )
```

```python
import jax
import jax.numpy as jnp
from jax import lax
from jax.experimental import pallas as pl
from jax.experimental.pallas import tpu as pltpu
from jax.sharding import PartitionSpec as P

F32 = jnp.float32
BF16 = jnp.bfloat16
TASKS = 4
EPS = 1e-05
NEG = -1e30
LOG2E = 1.4426950408889634
HEAD = 64
LONG = HEAD + 16
TILE = 256
SUB = TILE // 128
BLOCK = 256
COST = 10**6
DOCS = 16
NT = (((1,), (1,)), ((), ()))
NN = (((1,), (0,)), ((), ()))
TN = (((0,), (0,)), ((), ()))


def dot(a, b, dims=NN):
    return lax.dot_general(a, b, dims, preferred_element_type=F32)


def split3(x):
    a = x.astype(BF16)
    r = x - a.astype(F32)
    b = r.astype(BF16)
    c = (r - b.astype(F32)).astype(BF16)
    return a, b, c


def normed(z):
    c = z - jnp.mean(z, axis=-1, keepdims=True)
    r = lax.rsqrt(jnp.mean(c * c, axis=-1, keepdims=True) + EPS)
    return c * r, r


def norm_back(dz, gain, zhat, r):
    s = dz * gain
    return r * (
        s
        - jnp.mean(s, axis=-1, keepdims=True)
        - zhat * jnp.mean(s * zhat, axis=-1, keepdims=True)
    )


def params(mib):
    return pltpu.CompilerParams(vmem_limit_bytes=mib * 2**20)


ANYWHERE = pl.BlockSpec(memory_space=pl.ANY)


def whole(shape):
    return pl.BlockSpec(shape, lambda *_: (0,) * len(shape), pipeline_mode=pl.Buffered(1))


def fold_band(x):
    r = x.shape[0]
    while r > 8:
        r //= 2
        x = pltpu.roll(x[:r], r, 1) + x[r:]
    out = x[7:8]
    for i in range(7):
        out = out + pltpu.roll(x[i : i + 1], 7 - i, 1)
    return out


def bias_tile(band, h, base):
    return jnp.concatenate(
        [
            jnp.concatenate([band[h, base + u - t] for u in range(SUB)], axis=1)
            for t in range(SUB)
        ],
        axis=0,
    )


def column(row):
    return jnp.broadcast_to(row.astype(F32), (8, row.shape[1])).T[:, 0:1]


def tile_range(segs, row, i, nb, back=False):
    ends = [(segs[row, t * TILE], segs[row, t * TILE + TILE - 1]) for t in range(nb)]
    first, last = ends[i]
    lo, hi = i, i + 1
    for t in range(i):
        lo = lo - (ends[t][1] == first).astype(jnp.int32)
    for t in range(i + 1, nb):
        shared = ends[t][0] == last
        if back:
            shared = shared & (last >= 0)
        hi = hi + shared.astype(jnp.int32)
    if back:
        hi = jnp.where(first >= 0, hi, lo)
    return lo, hi


def attend_body(
    row_ref, segs, tok_ref, seg_ref, gains_ref, biases_ref, w_ref, hv_ref, rev_ref, *rest
):
    oc_ref, lse_ref, h1t_hbm, q_hbm, k_hbm, v_hbm, band_hbm = rest[-19:-12]
    h1, h1t, q_s, k_s, v_s, band, vt, docs, km, acc, ml, sems = rest[-12:]
    row = row_ref[0]
    seq, d = tok_ref.shape
    nb = seq // TILE
    bw = seq // 128 - 1
    nh = d // HEAD
    tiles = 2 * seq // 128
    gain = gains_ref[0:1, :].astype(F32)
    shift = biases_ref[0:1, :].astype(F32)
    for b in range(seq // BLOCK):
        r = slice(b * BLOCK, (b + 1) * BLOCK)
        z, _ = normed(tok_ref[r, :].astype(F32))
        y = (z * gain + shift).astype(BF16)
        h1[r, :] = y
        h1t[:, r] = y.astype(F32).T.astype(BF16)
    lane = lax.broadcasted_iota(jnp.int32, (seq, 128), 1)
    doc = column(seg_ref[pl.ds(row, 1), :]).astype(jnp.int32) + 1
    zero = jnp.zeros((), BF16)
    hot = jnp.where(lane == doc, 1.0, 0.0).astype(BF16)
    bar = jnp.where((lane < DOCS) & (lane != doc), NEG, 0.0).astype(BF16)
    docs[0] = hot
    docs[1] = bar
    for c0 in range(0, d, 256):
        cc = slice(c0, c0 + 256)
        x = h1[...]
        q_s[:, cc] = (dot(x, w_ref[0, :, cc]) * 0.125 + hv_ref[1:2, cc] * 0.125).astype(BF16)
        k_s[:, cc] = dot(x, w_ref[1, :, cc]).astype(BF16)
        v_s[:, cc] = (dot(x, w_ref[2, :, cc]) - (-hv_ref[2:3, cc])).astype(BF16)
        for h in range(c0 // HEAD, c0 // HEAD + 4):
            base8 = jnp.broadcast_to(rev_ref[h : h + 1, :] * LOG2E, (8, 2 * seq))
            base8 = pltpu.roll(base8, 2 * seq - 127, 1, stride=1, stride_axis=0)
            for g in range(16):
                y = pltpu.roll(base8, 8 * g, 1) if g else base8
                for t in range(tiles):
                    band[h, t, 8 * g : 8 * g + 8, :] = y[:, 128 * t : 128 * t + 128]
            half = (lane < HEAD) if h % 2 == 0 else (lane >= HEAD)
            c = slice(128 * (h // 2), 128 * (h // 2) + 128)
            km[h] = jnp.where(half, k_s[:, c], zero)
        for j in (c0 // 128, c0 // 128 + 1):
            c = slice(128 * j, 128 * j + 128)
            for b in range(nb):
                vv = v_s[b * TILE : (b + 1) * TILE, c].astype(F32).T.astype(BF16)
                for h in range(2):
                    at = LONG * (2 * j + h)
                    vt[b, at : at + HEAD, :] = vv[HEAD * h : HEAD * h + HEAD]
                    vt[b, at + HEAD : at + LONG, :] = jnp.ones((LONG - HEAD, TILE), BF16)
    copies = [
        pltpu.make_async_copy(a, b, sems.at[i])
        for i, (a, b) in enumerate(
            ((h1t, h1t_hbm), (q_s, q_hbm), (k_s, k_hbm), (v_s, v_hbm), (band, band_hbm))
        )
    ]
    for copy in copies:
        copy.start()
    for qb in range(nb):
        qs = slice(qb * TILE, (qb + 1) * TILE)
        acc[...] = jnp.zeros_like(acc)
        ml[...] = jnp.full((nh, TILE), -jnp.inf, F32)

        def step(kb, _):
            ks = pl.ds(pl.multiple_of(kb * TILE, TILE), TILE)
            base = bw + SUB * qb - SUB * kb
            ss = [
                dot(
                    jnp.concatenate([km[h, ks, :], docs[0, ks, :]], axis=1),
                    jnp.concatenate([q_s[qs, 128 * (h // 2) : 128 * (h // 2) + 128], docs[1, qs, :]], axis=1),
                    NT,
                )
                for h in range(nh)
            ]
            for h in range(nh):
                s = ss[h] * LOG2E + bias_tile(band, h, base)
                old = ml[h : h + 1, :]
                top = jnp.maximum(old, jnp.max(s, axis=0, keepdims=True))
                fade = jnp.exp2(old - top)
                w = jnp.exp2(s - top)
                ml[h : h + 1, :] = top
                r = slice(LONG * h, LONG * h + LONG)
                acc[r, :] = acc[r, :] * fade + dot(vt[kb, r, :], w.astype(BF16))
            return _

        lo, hi = tile_range(segs, row, qb, nb)
        lax.fori_loop(lo, hi, step, 0)
        for j in range(nh // 2):
            outs = []
            for h in (2 * j, 2 * j + 1):
                total = acc[LONG * h + HEAD : LONG * h + HEAD + 1, :]
                lse_ref[h : h + 1, qs] = ml[h : h + 1, :] * (1 / LOG2E) + jnp.log(total)
                outs.append(acc[LONG * h : LONG * h + HEAD, :] * (1.0 / total))
            c = slice(128 * j, 128 * j + 128)
            oc_ref[qs, c] = (jnp.concatenate(outs, axis=0).T * hv_ref[0:1, c]).astype(BF16)
    lse_ref[nh:, :] = jnp.zeros((lse_ref.shape[0] - nh, seq), F32)
    for copy in copies:
        copy.wait()


def attend(row, tokens, segs, gains, biases, w_qkv, hv, rev, after=()):
    d = tokens.shape[1]
    seq = segs.shape[1]
    nh = d // HEAD
    rows = -(-nh // 8) * 8
    tiles = 2 * seq // 128
    s = jax.ShapeDtypeStruct
    return pl.pallas_call(
        attend_body,
        grid_spec=pltpu.PrefetchScalarGridSpec(
            num_scalar_prefetch=2,
            grid=(1,),
            in_specs=[pl.BlockSpec((seq, d), lambda i, row, *_: (row[0], 0), pipeline_mode=pl.Buffered(1))]
            + [whole(x.shape) for x in (segs, gains, biases, w_qkv, hv, rev)]
            + [ANYWHERE] * len(after),
            out_specs=[whole((seq, d)), whole((rows, seq))] + [ANYWHERE] * 5,
            scratch_shapes=[pltpu.VMEM((seq, d), BF16), pltpu.VMEM((d, seq), BF16)]
            + [pltpu.VMEM((seq, d), BF16)] * 3
            + [
                pltpu.VMEM((nh, tiles, 128, 128), F32),
                pltpu.VMEM((seq // TILE, LONG * nh, TILE), BF16),
                pltpu.VMEM((2, seq, 128), BF16),
                pltpu.VMEM((nh, seq, 128), BF16),
                pltpu.VMEM((LONG * nh, TILE), F32),
                pltpu.VMEM((nh, TILE), F32),
                pltpu.SemaphoreType.DMA((5,)),
            ],
        ),
        out_shape=[s((seq, d), BF16), s((rows, seq), F32), s((d, seq), BF16)]
        + [s((seq, d), BF16)] * 3
        + [s((nh, tiles, 128, 128), F32)],
        compiler_params=params(60),
        cost_estimate=pl.CostEstimate(flops=COST, bytes_accessed=COST, transcendentals=0),
        name="attend",
    )(row, segs, tokens, segs, gains, biases, w_qkv, hv, rev, *after)


def attend_back_body(
    row_ref, segs, q_ref, k_ref, v_ref, do_ref, x_ref, seg_ref, band, h1t_ref, *rest
):
    dq_ref, dk_ref, dv_ref, tg_ref, wg_ref, gband, qx, dx, km, vm, kt, dqt, dka, dva = rest[-14:]
    seq = q_ref.shape[0]
    nb = seq // TILE
    bw = seq // 128 - 1
    nh = q_ref.shape[1] // HEAD
    heads = pl.num_programs(0) * nh
    first = pl.program_id(0) * nh
    lane = lax.broadcasted_iota(jnp.int32, (seq, 128), 1)
    row = row_ref[0]
    hot = lane == column(seg_ref[pl.ds(row, 1), :]).astype(jnp.int32) + 1
    zero = jnp.zeros((), BF16)
    gband[...] = jnp.zeros_like(gband)
    dqt[...] = jnp.zeros_like(dqt)
    for h in range(nh):
        half = (lane < HEAD) if h % 2 == 0 else (lane >= HEAD)
        c = slice(128 * (h // 2), 128 * (h // 2) + 128)
        at = DOCS + 3 * (first + h)
        km[h, :, :128] = jnp.where(half, k_ref[:, c], zero)
        km[h, :, 128:] = jnp.where(hot | ((lane >= at) & (lane < at + 3)), 1.0, 0.0).astype(BF16)
        at = at + 3 * heads
        vm[h, :, :128] = jnp.where(half, v_ref[:, c], zero)
        vm[h, :, 128:] = jnp.where((lane >= at) & (lane < at + 3), 1.0, 0.0).astype(BF16)
    for j in range(nh // 2):
        c = slice(128 * j, 128 * j + 128)
        qx[j, :, :128] = q_ref[:, c]
        qx[j, :, 128:] = x_ref[...]
        dx[j, :, :128] = do_ref[:, c]
        dx[j, :, 128:] = x_ref[...]
        kt[c, :] = k_ref[:, c].astype(F32).T.astype(BF16)
    low = lax.broadcasted_iota(jnp.int32, (TILE, 128), 1) < HEAD
    for kb in range(nb):
        dka[...] = jnp.zeros_like(dka)
        dva[...] = jnp.zeros_like(dva)
        ks = slice(kb * TILE, (kb + 1) * TILE)

        def step(qb, _):
            qs = pl.ds(pl.multiple_of(qb * TILE, TILE), TILE)
            base = bw + SUB * qb - SUB * kb
            ss = [dot(km[h, ks, :], qx[h // 2, qs, :], NT) for h in range(nh)]
            dps = [dot(vm[h, ks, :], dx[h // 2, qs, :], NT) for h in range(nh)]
            for h in range(nh):
                w = jnp.exp2(ss[h] * LOG2E + bias_tile(band, h, base))
                ds = (w * dps[h]).astype(BF16)
                dsf = ds.astype(F32)
                for off in range(1 - SUB, SUB):
                    total = None
                    for t in range(SUB):
                        u = off + t
                        if 0 <= u < SUB:
                            piece = dsf[128 * t : 128 * t + 128, 128 * u : 128 * u + 128]
                            total = piece if total is None else total + piece
                    gband[h, base + off] += total
                dva[h] += dot(w.astype(BF16), dx[h // 2, qs, :128])
                dka[h] += dot(ds, qx[h // 2, qs, :128])
                r = slice(HEAD * h, HEAD * h + HEAD)
                dqt[qb, r, :] += dot(kt[r, ks], ds)
            return _

        lo, hi = tile_range(segs, row, kb, nb, True)
        lax.fori_loop(lo, hi, step, 0)
        for j in range(nh // 2):
            c = slice(128 * j, 128 * j + 128)
            dk_ref[ks, c] = jnp.where(low, dka[2 * j], dka[2 * j + 1]).astype(BF16)
            dv_ref[ks, c] = jnp.where(low, dva[2 * j], dva[2 * j + 1]).astype(BF16)
    for j in range(nh // 2):
        c = slice(128 * j, 128 * j + 128)
        for b in range(nb):
            dq_ref[b * TILE : (b + 1) * TILE, c] = (
                dqt[b, c, :].T.astype(BF16).astype(F32) * 0.125
            ).astype(BF16)
    wide = HEAD * nh
    for i, ref in enumerate((dq_ref, dk_ref, dv_ref)):
        wg_ref[:, i * wide : (i + 1) * wide] = dot(h1t_ref[...], ref[...]).astype(BF16)
    for h in range(nh):
        tg_ref[0, h : h + 1, :] = fold_band(
            jnp.concatenate([gband[h, t] for t in range(2 * seq // 128)], axis=1)
        )


def attend_back(row, q, k, v, do, aux, segs, band, h1t, after=()):
    seq, width = q.shape
    heads = width // HEAD
    nh = 4 if heads % 4 == 0 else 2
    groups = heads // nh
    blk = pl.BlockSpec((seq, HEAD * nh), lambda p, *_: (0, p))
    tiles = 2 * seq // 128
    dq, dk, dv, tg, wg = pl.pallas_call(
        attend_back_body,
        grid_spec=pltpu.PrefetchScalarGridSpec(
            num_scalar_prefetch=2,
            grid=(groups,),
            in_specs=[blk] * 4
            + [
                pl.BlockSpec((seq, 128), lambda p, *_: (0, 0)),
                whole(segs.shape),
                pl.BlockSpec((nh, tiles, 128, 128), lambda p, *_: (p, 0, 0, 0)),
                whole(h1t.shape),
            ]
            + [ANYWHERE] * len(after),
            out_specs=[blk] * 3
            + [
                pl.BlockSpec((1, nh, 2 * seq), lambda p, *_: (p, 0, 0)),
                pl.BlockSpec((width, 3 * HEAD * nh), lambda p, *_: (0, p)),
            ],
            scratch_shapes=[
                pltpu.VMEM((nh, tiles, 128, 128), F32),
                pltpu.VMEM((nh // 2, seq, 256), BF16),
                pltpu.VMEM((nh // 2, seq, 256), BF16),
                pltpu.VMEM((nh, seq, 256), BF16),
                pltpu.VMEM((nh, seq, 256), BF16),
                pltpu.VMEM((HEAD * nh, seq), BF16),
                pltpu.VMEM((seq // TILE, HEAD * nh, TILE), F32),
                pltpu.VMEM((nh, TILE, 128), F32),
                pltpu.VMEM((nh, TILE, 128), F32),
            ],
        ),
        out_shape=[jax.ShapeDtypeStruct((seq, width), BF16)] * 3
        + [jax.ShapeDtypeStruct((groups, nh, 2 * seq), F32), jax.ShapeDtypeStruct((width, 3 * width), BF16)],
        compiler_params=params(60),
        cost_estimate=pl.CostEstimate(flops=COST, bytes_accessed=COST, transcendentals=0),
        name="attend_back",
    )(row, segs, q, k, v, do, aux, segs, band, h1t, *after)
    return dq, dk, dv, tg.reshape(heads, 2 * seq), wg, groups


def gelu_parts(u):
    dens = jnp.exp2(u * u * (-0.5 * LOG2E))
    t = 1.0 / (1.0 + (0.3275911 * 0.7071067811865476) * jnp.abs(u))
    poly = t * (0.127414796 + t * (-0.142248368 + t * (0.7107068705 + t * (-0.7265760135 + t * 0.5307027145))))
    tail = poly * dens
    phi = jnp.where(u >= 0, 1.0 - tail, tail)
    return phi, phi + u * (dens * 0.3989422804014327)


STEP = 512


def middle_body(
    row_ref, tok_ref, oc_ref, gains_ref, biases_ref, fgain_ref, fbias_ref, wo_ref, wu_ref, wd_ref, *rest
):
    out_ref, h3_ref, m_ref, mh_ref, gp_ref, z_ref, stat_ref, e_s, wu, wd, sems = rest[-11:]
    ff = wu_ref.shape[1]
    copies = [pltpu.make_async_copy(a, b, sems.at[i]) for i, (a, b) in enumerate(((wu_ref, wu), (wd_ref, wd)))]

    @pl.when(pl.program_id(0) == 0)
    def _():
        for copy in copies:
            copy.start()

    gains = gains_ref[...].astype(F32)
    biases = biases_ref[...].astype(F32)
    tok = tok_ref[...].astype(F32)
    n, d = tok.shape
    z2, r2 = normed(dot(oc_ref[...], wo_ref[...]) - (-biases[1:2]))
    x2 = tok + (z2 * gains[1:2] + biases[2:3])
    z3, r3 = normed(x2)
    h3 = (z3 * gains[2:3] + biases[3:4]).astype(BF16)
    h3_ref[...] = h3
    z_ref[:, :d] = z2.astype(BF16)
    z_ref[:, d:] = z3.astype(BF16)

    @pl.when(pl.program_id(0) == 0)
    def _():
        copies[0].wait()

    s1 = jnp.zeros((n, 1), F32)
    s2 = jnp.zeros((n, 1), F32)
    for c0 in range(0, ff, STEP):
        c = slice(c0, c0 + STEP)
        u = dot(h3, wu[:, c]) - (-fbias_ref[0:1, c].astype(F32))
        phi, slope = gelu_parts(u)
        e = u * phi
        e_s[:, c] = e
        gp_ref[:, c] = slope.astype(BF16)
        s1 += jnp.sum(e, axis=1, keepdims=True)
        s2 += jnp.sum(e * e, axis=1, keepdims=True)

    @pl.when(pl.program_id(0) == 0)
    def _():
        copies[1].wait()

    mean = s1 / ff
    r = lax.rsqrt(s2 / ff - mean * mean + EPS)
    y = jnp.zeros((n, d), F32)
    for c0 in range(0, ff, STEP):
        c = slice(c0, c0 + STEP)
        mh = (e_s[:, c] - mean) * r
        mh_ref[:, c] = mh.astype(BF16)
        m = (mh * fgain_ref[0:1, c].astype(F32) + fbias_ref[1:2, c].astype(F32)).astype(BF16)
        m_ref[:, c] = m
        y += dot(m, wd[c, :])
    out_ref[...] = (x2 + (y + biases[4:5])).astype(BF16)
    lane = lax.broadcasted_iota(jnp.int32, (n, 128), 1)
    stat_ref[...] = jnp.where(lane == 0, r2, jnp.where(lane == 1, r3, r))


def middle(row, tokens, oc, gains, biases, fgain, fbias, w_out, w_up, w_down, after=()):
    n, d = oc.shape
    ff = w_up.shape[1]
    steps = n // BLOCK
    blk = pl.BlockSpec((BLOCK, d), lambda i, row: (i, 0))
    wide = pl.BlockSpec((BLOCK, ff), lambda i, row: (i, 0))
    s = jax.ShapeDtypeStruct
    return pl.pallas_call(
        middle_body,
        grid_spec=pltpu.PrefetchScalarGridSpec(
            num_scalar_prefetch=1,
            grid=(steps,),
            in_specs=[pl.BlockSpec((BLOCK, d), lambda i, row: (row[0] * steps + i, 0)), blk]
            + [whole(x.shape) for x in (gains, biases, fgain, fbias, w_out)]
            + [ANYWHERE] * (2 + len(after)),
            out_specs=[
                blk, blk, wide, wide, wide,
                pl.BlockSpec((BLOCK, 2 * d), lambda i, row: (i, 0)),
                pl.BlockSpec((BLOCK, 128), lambda i, row: (i, 0)),
            ],
            scratch_shapes=[
                pltpu.VMEM((BLOCK, ff), F32),
                pltpu.VMEM((d, ff), BF16),
                pltpu.VMEM((ff, d), BF16),
                pltpu.SemaphoreType.DMA((2,)),
            ],
        ),
        out_shape=[s((n, d), BF16)] * 2 + [s((n, ff), BF16)] * 3 + [s((n, 2 * d), BF16), s((n, 128), F32)],
        compiler_params=params(60),
        cost_estimate=pl.CostEstimate(flops=COST, bytes_accessed=COST, transcendentals=0),
        name="middle",
    )(row, tokens, oc, gains, biases, fgain, fbias, w_out, w_up, w_down, *after)


def task_weight(counts_ref, tasks):
    counts = counts_ref[0:1, :]
    lane = lax.broadcasted_iota(jnp.int32, counts.shape, 1)
    own = jnp.sum(jnp.where(lane == tasks[0], counts, 0.0), axis=1, keepdims=True)
    return jnp.sum(counts, axis=1, keepdims=True) / (TASKS * own)


def middle_back_body(
    row_ref, tasks, og_ref, seg_ref, counts_ref, oc_ref, lse_ref, mh_ref, gp_ref, z_ref, stat_ref,
    gains_ref, fgain_ref, hs_ref, wo_ref, wu_ref, wd_ref, *rest
):
    df_ref, du_ref, dx2_ref, da_ref, do_ref, aux_ref, nv_ref, fv_ref, d_s = rest[-9:]
    d, ff = wu_ref.shape
    heads = d // HEAD
    gains = gains_ref[...].astype(F32)
    oc = oc_ref[...]
    rows = oc.shape[0]
    here = pl.ds(pl.multiple_of(pl.program_id(0) * rows, rows), rows)
    doc = column(seg_ref[pl.ds(row_ref[0], 1), here])
    g = og_ref[...].astype(F32) * jnp.where(doc >= 0, task_weight(counts_ref, tasks), 0.0)
    df = g.astype(BF16)
    df_ref[...] = df
    r2 = stat_ref[:, 0:1]
    r3 = stat_ref[:, 1:2]
    r = stat_ref[:, 2:3]
    b1 = jnp.zeros((rows, 1), F32)
    b2 = jnp.zeros((rows, 1), F32)
    gsum, bsum, usum = [], [], []
    for c0 in range(0, ff, STEP):
        c = slice(c0, c0 + STEP)
        mh = mh_ref[:, c].astype(F32)
        dm = dot(df, wd_ref[c, :], NT)
        gsum.append(jnp.sum(dm * mh, axis=0, keepdims=True))
        bsum.append(jnp.sum(dm, axis=0, keepdims=True))
        sc = dm * fgain_ref[0:1, c].astype(F32)
        d_s[:, c] = sc
        b1 += jnp.sum(sc, axis=1, keepdims=True)
        b2 += jnp.sum(sc * mh, axis=1, keepdims=True)
    b1 = b1 / ff
    b2 = b2 / ff
    dh3 = jnp.zeros((rows, d), F32)
    for c0 in range(0, ff, STEP):
        c = slice(c0, c0 + STEP)
        de = r * (d_s[:, c] - b1 - mh_ref[:, c].astype(F32) * b2)
        du = (de * gp_ref[:, c].astype(F32)).astype(BF16)
        du_ref[:, c] = du
        usum.append(jnp.sum(du.astype(F32), axis=0, keepdims=True))
        dh3 += dot(du, wu_ref[:, c], NT)
    z2 = z_ref[:, :d].astype(F32)
    z3 = z_ref[:, d:].astype(F32)
    dx2 = g + norm_back(dh3, gains[2:3], z3, r3)
    dx2_ref[...] = dx2
    da = norm_back(dx2, gains[1:2], z2, r2).astype(BF16)
    da_ref[...] = da
    doc_ = dot(da, wo_ref[...], NT)
    hs = hs_ref[0:1, :]
    o = oc.astype(F32) / hs
    do = (doc_ * hs).astype(BF16)
    do_ref[...] = do

    prod = do.astype(F32) * o
    hi = prod.astype(BF16)
    lo = (prod - hi.astype(F32)).astype(BF16)
    at = DOCS + 3 * heads
    head_of = lax.broadcasted_iota(jnp.int32, (d, 128), 0) // HEAD
    lane = lax.broadcasted_iota(jnp.int32, (d, 128), 1)
    put = jnp.where((lane >= at + 3 * head_of) & (lane < at + 3 * head_of + 3), -1.0, 0.0).astype(BF16)
    delta = dot(hi, put) + dot(lo, put)
    pa, pb, pc = split3(delta)
    lane = lax.broadcasted_iota(jnp.int32, (rows, 128), 1)
    part = (lane - at + 3 * 128) % 3
    delta = jnp.where(part == 0, pa.astype(F32), jnp.where(part == 1, pb.astype(F32), pc.astype(F32)))
    hrows = lse_ref.shape[0]
    la, lb, lc = split3(lse_ref[...])
    stack = jnp.concatenate([la.astype(F32), lb.astype(F32), lc.astype(F32)], axis=0).astype(BF16)
    row = lax.broadcasted_iota(jnp.int32, (3 * hrows, 128), 0)
    col = lax.broadcasted_iota(jnp.int32, (3 * hrows, 128), 1)
    put = jnp.where((row % hrows < heads) & (col == DOCS + 3 * (row % hrows) + row // hrows), -1.0, 0.0)
    lse = dot(stack, put.astype(BF16), TN)
    bar = jnp.where((lane < DOCS) & (lane != doc.astype(jnp.int32) + 1), NEG, 0.0)
    aux_ref[...] = (bar + lse + delta).astype(BF16)

    @pl.when(pl.program_id(0) == 0)
    def _():
        nv_ref[...] = jnp.zeros_like(nv_ref)
        fv_ref[...] = jnp.zeros_like(fv_ref)

    sums = (dx2 * z2, dh3 * z3, da.astype(F32), dx2, dh3, df.astype(F32), doc_ * o)
    for i, term in enumerate(sums):
        nv_ref[i : i + 1, :] += jnp.sum(term, axis=0, keepdims=True)
    for i, terms in enumerate((gsum, usum, bsum)):
        fv_ref[i : i + 1, :] += jnp.concatenate(terms, axis=1)


def middle_back(row, tasks, counts, out_grad, segs, oc, lse, mh, gp, z, stat, gains, fgain, hs, w_out, w_up, w_down, after=()):
    n, d = oc.shape
    ff = w_up.shape[1]
    steps = n // BLOCK
    blk = pl.BlockSpec((BLOCK, d), lambda i, *_: (i, 0))
    wide = pl.BlockSpec((BLOCK, ff), lambda i, *_: (i, 0))
    thin = pl.BlockSpec((BLOCK, 128), lambda i, *_: (i, 0))
    s = jax.ShapeDtypeStruct
    return pl.pallas_call(
        middle_back_body,
        grid_spec=pltpu.PrefetchScalarGridSpec(
            num_scalar_prefetch=2,
            grid=(steps,),
            in_specs=[
                pl.BlockSpec((BLOCK, d), lambda i, row, *_: (row[0] * steps + i, 0)),
                whole(segs.shape),
                whole(counts.shape),
                blk,
                pl.BlockSpec((lse.shape[0], BLOCK), lambda i, *_: (0, i)),
                wide, wide, pl.BlockSpec((BLOCK, 2 * d), lambda i, *_: (i, 0)), thin,
            ]
            + [whole(x.shape) for x in (gains, fgain, hs, w_out, w_up, w_down)]
            + [ANYWHERE] * len(after),
            out_specs=[
                blk, wide, blk, blk, blk, thin,
                pl.BlockSpec((8, d), lambda i, *_: (0, 0)),
                pl.BlockSpec((8, ff), lambda i, *_: (0, 0)),
            ],
            scratch_shapes=[pltpu.VMEM((BLOCK, ff), F32)],
        ),
        out_shape=[
            s((n, d), BF16), s((n, ff), BF16), s((n, d), F32), s((n, d), BF16), s((n, d), BF16), s((n, 128), BF16), s((8, d), F32), s((8, ff), F32),
        ],
        compiler_params=params(60),
        cost_estimate=pl.CostEstimate(flops=COST, bytes_accessed=COST, transcendentals=0),
        name="middle_back",
    )(row, tasks, out_grad, segs, counts, oc, lse, mh, gp, z, stat, gains, fgain, hs, w_out, w_up, w_down, *after)


def early_body(h3_ref, df_ref, da_ref, du_ref, m_ref, oc_ref, out_ref, ht, ft, at):
    i = pl.program_id(0)
    steps = (pl.num_programs(0) - 1) // 2

    @pl.when(i == 0)
    def _():
        for source, target in ((h3_ref, ht), (df_ref, ft), (da_ref, at)):
            target[...] = source[...].astype(F32).T.astype(BF16)

    @pl.when(i < steps)
    def _():
        out_ref[...] = dot(ft[...], m_ref[...]).astype(BF16)

    @pl.when((i >= steps) & (i < 2 * steps))
    def _():
        out_ref[...] = dot(ht[...], du_ref[...]).astype(BF16)

    @pl.when(i >= 2 * steps)
    def _():
        out_ref[...] = dot(at[...], oc_ref[...]).astype(BF16)


def early_grads(h3, df, da, du, m, oc):
    n, d = h3.shape
    ff = du.shape[1]
    width = d
    steps = ff // width
    pick = lambda first, count: pl.BlockSpec((n, width), lambda i: (0, jnp.clip(i - first, 0, count - 1)))
    return pl.pallas_call(
        early_body,
        grid=(2 * steps + 1,),
        in_specs=[whole((n, d))] * 3 + [pick(steps, steps), pick(0, steps), pick(2 * steps, 1)],
        out_specs=pl.BlockSpec((d, width), lambda i: (0, i)),
        out_shape=jax.ShapeDtypeStruct((d, 2 * ff + d), BF16),
        scratch_shapes=[pltpu.VMEM((d, n), BF16)] * 3,
        compiler_params=params(60),
        cost_estimate=pl.CostEstimate(flops=COST, bytes_accessed=COST, transcendentals=0),
        name="early_grads",
    )(h3, df, da, du, m, oc)


def input_body(row_ref, tok_ref, dx2_ref, dq_ref, dk_ref, dv_ref, gains_ref, w_ref, *rest):
    tg_ref, nv_ref = rest[-2:]
    z, r = normed(tok_ref[...].astype(F32))
    dh1 = (
        dot(dq_ref[...], w_ref[0], NT) + dot(dk_ref[...], w_ref[1], NT) + dot(dv_ref[...], w_ref[2], NT)
    )
    tg_ref[...] = (dx2_ref[...] + norm_back(dh1, gains_ref[0:1, :].astype(F32), z, r)).astype(BF16)

    @pl.when(pl.program_id(0) == 0)
    def _():
        nv_ref[...] = jnp.zeros_like(nv_ref)

    sums = (dh1 * z, dh1, dq_ref[...].astype(F32), dv_ref[...].astype(F32))
    for i, term in enumerate(sums):
        nv_ref[i : i + 1, :] += jnp.sum(term, axis=0, keepdims=True)


def input_grad(row, tokens, dx2, dq, dk, dv, gains, w_qkv, after=()):
    n, d = dx2.shape
    steps = n // BLOCK
    blk = pl.BlockSpec((BLOCK, d), lambda i, row: (i, 0))
    return pl.pallas_call(
        input_body,
        grid_spec=pltpu.PrefetchScalarGridSpec(
            num_scalar_prefetch=1,
            grid=(steps,),
            in_specs=[pl.BlockSpec((BLOCK, d), lambda i, row: (row[0] * steps + i, 0))]
            + [blk] * 4
            + [whole(gains.shape), whole(w_qkv.shape)]
            + [pl.BlockSpec(memory_space=pl.ANY)] * len(after),
            out_specs=[blk, pl.BlockSpec((8, d), lambda i, row: (0, 0))],
        ),
        out_shape=[jax.ShapeDtypeStruct((n, d), BF16), jax.ShapeDtypeStruct((8, d), F32)],
        compiler_params=params(60),
        cost_estimate=pl.CostEstimate(flops=COST, bytes_accessed=COST, transcendentals=0),
        name="input_grad",
    )(row, tokens, dx2, dq, dk, dv, gains, w_qkv, *after)


def gate_body(*refs):
    refs[-1][0] = 0


def gate(x, *after):
    return pl.pallas_call(
        gate_body,
        in_specs=[ANYWHERE] * (1 + len(after)),
        out_specs=[ANYWHERE, pl.BlockSpec(memory_space=pltpu.SMEM)],
        out_shape=[jax.ShapeDtypeStruct(x.shape, x.dtype), jax.ShapeDtypeStruct((1,), jnp.int32)],
        input_output_aliases={0: 0},
        cost_estimate=pl.CostEstimate(flops=COST, bytes_accessed=COST, transcendentals=0),
        name="gate",
    )(x, *after)[0]


def copy_body(x_ref, o_ref):
    o_ref[...] = x_ref[...]


def copy(x):
    n, d = x.shape
    blk = pl.BlockSpec((n // 8, d), lambda i: (i, 0))
    return pl.pallas_call(
        copy_body,
        grid=(8,),
        in_specs=[blk],
        out_specs=blk,
        out_shape=jax.ShapeDtypeStruct(x.shape, x.dtype),
        name="copy",
    )(x)


def spread_body(row_ref, pair_ref, right_ref, left_ref, qkv_out, o_out, up_out, down_out):
    share = up_out.shape[1]
    cols = qkv_out.shape[2]
    pair = pair_ref[0].astype(F32) + right_ref[...].astype(F32) + left_ref[...].astype(F32)
    down_out[...] = pair[:, :share]
    up_out[...] = pair[:, share : 2 * share]
    small = pair[:, 2 * share :]
    o_out[...] = small[:, :cols].T
    for i in range(3):
        qkv_out[i] = small[:, (i + 1) * cols : (i + 2) * cols]


def spread(row, pair, pair_sums, share):
    _, n, width = pair.shape
    cols = (width - 2 * share) // 4
    s = jax.ShapeDtypeStruct
    own = lambda x: pl.BlockSpec((1,) + x.shape[1:], lambda i, row: (row[0], 0, 0))
    other = lambda x: pl.BlockSpec(x.shape[1:], lambda i, row: (0, 0))
    outs = [s((3, n, cols), F32), s((cols, n), F32), s((n, share), F32), s((n, share), F32)]
    return pl.pallas_call(
        spread_body,
        grid_spec=pltpu.PrefetchScalarGridSpec(
            num_scalar_prefetch=1,
            grid=(1,),
            in_specs=[own(pair), other(pair), other(pair)],
            out_specs=[pl.BlockSpec(x.shape, lambda i, row, k=len(x.shape): (0,) * k) for x in outs],
        ),
        out_shape=outs,
        name="spread",
    )(row, pair, *pair_sums)


def sum_scatter(x, axis):
    size = lax.axis_size(axis)
    me = lax.axis_index(axis)
    count = size.bit_length() - 1

    def swap(x, left, b):
        dim = left.index(b)
        mine = (me >> b) & 1
        send = lax.dynamic_index_in_dim(x, 1 - mine, dim, keepdims=False)
        keep = lax.dynamic_index_in_dim(x, mine, dim, keepdims=False)
        pairs = [(i, i ^ (1 << b)) for i in range(size)]
        return keep + lax.ppermute(send, axis, pairs), [o for o in left if o != b]

    left = list(range(count - 1, -1, -1))
    x, left = swap(x.reshape((2,) * count + (x.shape[0] // size, x.shape[1])), left, 0)
    half = x.shape[-1] // 2
    near, far = (x[..., :half], left), (x[..., half:], left)
    for i in range(1, count):
        near = swap(*near, i)
        far = swap(*far, count - i)
    return jnp.concatenate([near[0], far[0]], axis=-1)


def line_sums(blocks, axis):
    size = lax.axis_size(axis)
    me = lax.axis_index(axis)
    right = left = None
    for step in range(1, size):
        at = jnp.minimum(size - step + me, size - 1)
        pairs = [(i, i + 1) for i in range(step)]
        send = lax.dynamic_index_in_dim(blocks, at, 0, keepdims=False)
        right = lax.ppermute(send if right is None else send + right, axis, pairs)
        at = jnp.maximum(step - 1 - (size - 1 - me), 0)
        pairs = [(size - 1 - i, size - 2 - i) for i in range(step)]
        send = lax.dynamic_index_in_dim(blocks, at, 0, keepdims=False)
        left = lax.ppermute(send if left is None else send + left, axis, pairs)
    return right, left


def partial_sums(x, axis):
    size = lax.axis_size(axis)
    sums = [x]
    step = 1
    while step < size:
        sums.append(sums[-1] + lax.ppermute(sums[-1], axis, [(i, i ^ step) for i in range(size)]))
        step *= 2
    return sums


def add_all(x, axis):
    return partial_sums(x, axis)[-1]


def local(
    tokens, out_grad, segment_ids, row_tasks, rel_buckets, norm_gains, model_biases, w_qkv, qkv_bias,
    rel_bias, head_scale, w_out, w_up, ffn_gain, ffn_biases, w_down,
):
    parts = lax.axis_size("tensor")
    dps = lax.axis_size("dp")
    tensor_index = lax.axis_index("tensor")
    dp_index = lax.axis_index("dp")
    heads = head_scale.shape[0]
    d = tokens.shape[1]
    ff = w_up.shape[1]
    rows, seq = segment_ids.shape
    assert rows == parts

    live = jnp.sum((segment_ids >= 0).astype(F32), axis=1, keepdims=True)
    counts = jnp.sum(jnp.where(row_tasks[:, None] == jnp.arange(TASKS)[None, :], live, 0.0), axis=0)
    sums = partial_sums(jnp.broadcast_to(counts[None, :], (8, TASKS)), "dp")
    counts = sums[-1]

    back = jnp.pad(rel_buckets, (1, 0), constant_values=-1)[::-1]
    onehot = (jnp.arange(rel_bias.shape[1])[:, None] == back[None, :]).astype(BF16)
    rev = jnp.dot(rel_bias, onehot, preferred_element_type=F32)
    hv = jnp.concatenate(
        [jnp.broadcast_to(head_scale[None, :, None], (1, heads, d // heads)), qkv_bias], axis=0
    )
    hv = hv.astype(F32).reshape(3, d)
    fgain = ffn_gain[None, :]
    segs = segment_ids
    row = tensor_index[None]

    oc, lse, h1t, q, k, v, band = attend(
        row, tokens, segs, norm_gains, model_biases, w_qkv, hv, rev, sums[1:2]
    )
    layer_out, h3, m, mh, gp, z, stat = middle(
        row, tokens, oc, norm_gains, model_biases, fgain, ffn_biases, w_out, w_up, w_down, sums[2:3]
    )
    piece = d // dps
    share = ff // parts
    cols = d // parts
    layer_out = lax.all_gather(layer_out, "tensor", axis=0, tiled=True)
    df, du, dx2, da, do, aux, nv, fv = middle_back(
        row, row_tasks, counts, out_grad, segs, oc, lse, mh, gp, z, stat, norm_gains, fgain, hv, w_out, w_up, w_down
    )
    early = early_grads(h3, df, da, du, m, oc)
    dq, dk, dv, tg, late, groups = attend_back(row, q, k, v, do, aux, segs, band, h1t, (early,))
    early = lax.psum_scatter(early, "dp", scatter_dimension=0, tiled=True)
    tokens_grad, nv2 = input_grad(row, tokens, dx2, dq, dk, dv, norm_gains, w_qkv)
    nv2 = gate(nv2, layer_out)
    layer_out = copy(layer_out)
    tokens_grad = lax.all_gather(tokens_grad, "tensor", axis=0, tiled=True)
    late = sum_scatter(gate(late, nv2, early, layer_out), "dp")

    late = late.reshape(piece, groups, 3, d // groups).transpose(0, 2, 1, 3).reshape(piece, 3 * d)
    small = jnp.concatenate([early[:, 2 * ff :], late], axis=1).reshape(piece, 4, parts, cols)
    pair = jnp.concatenate(
        [
            early[:, :ff].reshape(piece, parts, share),
            early[:, ff : 2 * ff].reshape(piece, parts, share),
            small.transpose(0, 2, 1, 3).reshape(piece, parts, 4 * cols),
        ],
        axis=2,
    ).transpose(1, 0, 2)
    pair_sums = line_sums(pair, "tensor")
    project_grad, output_grad, up_grad, down_grad = spread(row, pair, pair_sums, share)
    tokens_grad = gate(tokens_grad, up_grad)
    down_grad = down_grad.T

    position = jnp.einsum("hs,bs->hb", tg, onehot.astype(F32), precision=lax.Precision.HIGHEST)
    head_sum = jnp.sum(nv[6].reshape(heads, d // heads), axis=1)
    vec = jnp.concatenate(
        [
            nv2[0:1].reshape(-1), nv[0:2].reshape(-1),
            nv2[1:2].reshape(-1), nv[2:6].reshape(-1),
            nv2[2:4].reshape(-1),
            fv[0:3].reshape(-1),
            position.reshape(-1),
            head_sum,
        ]
    )
    size = vec.shape[0]
    vec = jnp.pad(vec, (0, -size % 1024)).reshape(-1, 128)
    vec = add_all(add_all(vec, "dp"), "tensor").reshape(-1)
    at = 0

    def take(shape):
        nonlocal at
        n = 1
        for s in shape:
            n *= s
        out = vec[at : at + n].reshape(shape)
        at += n
        return out

    gains_grad = lax.dynamic_slice_in_dim(take((3, d)), dp_index * piece, piece, 1)
    biases_grad = lax.dynamic_slice_in_dim(take((5, d)), dp_index * piece, piece, 1)
    hp = heads // parts
    project_bias = lax.dynamic_slice_in_dim(take((2, heads, d // heads)), tensor_index * hp, hp, 1)
    fgain_grad = lax.dynamic_slice_in_dim(take((ff,)), tensor_index * share, share, 0)
    fbias_grad = lax.dynamic_slice_in_dim(take((2, ff)), tensor_index * share, share, 1)
    position = take(position.shape)
    bp = position.shape[1] // dps
    position = lax.dynamic_slice(position, (tensor_index * hp, dp_index * bp), (hp, bp))
    head_grad = lax.dynamic_slice_in_dim(take((heads,)), tensor_index * hp, hp, 0)
    return (
        layer_out, tokens_grad, gains_grad, biases_grad, project_grad, project_bias, position, head_grad,
        output_grad, up_grad, fgain_grad, fbias_grad, down_grad,
    )


def solution(mesh):
    rows = P("dp", None)
    return jax.shard_map(
        local,
        mesh=mesh,
        in_specs=(rows, rows, rows, P("dp")) + (P(),) * 12,
        out_specs=(
            rows,
            rows,
            P(None, "dp"),
            P(None, "dp"),
            P(None, "dp", "tensor"),
            P(None, "tensor", None),
            P("tensor", "dp"),
            P("tensor"),
            P("tensor", "dp"),
            P("dp", "tensor"),
            P("tensor"),
            P(None, "tensor"),
            P("tensor", "dp"),
        ),
        check_vma=False,
    )
```

```python
import jax
import jax.numpy as jnp
from jax import lax
from jax.experimental import pallas as pl
from jax.experimental.pallas import tpu as pltpu
from jax.sharding import PartitionSpec as P

F32 = jnp.float32
BF16 = jnp.bfloat16
TASKS = 4
EPS = 1e-05
NEG = -1e30
LOG2E = 1.4426950408889634
HEAD = 64
LONG = HEAD + 16
TILE = 256
SUB = TILE // 128
BLOCK = 256
COST = 10**6
DOCS = 16
NT = (((1,), (1,)), ((), ()))
NN = (((1,), (0,)), ((), ()))
TN = (((0,), (0,)), ((), ()))


def dot(a, b, dims=NN):
    return lax.dot_general(a, b, dims, preferred_element_type=F32)


def split3(x):
    a = x.astype(BF16)
    r = x - a.astype(F32)
    b = r.astype(BF16)
    c = (r - b.astype(F32)).astype(BF16)
    return a, b, c


def normed(z):
    c = z - jnp.mean(z, axis=-1, keepdims=True)
    r = lax.rsqrt(jnp.mean(c * c, axis=-1, keepdims=True) + EPS)
    return c * r, r


def norm_back(dz, gain, zhat, r):
    s = dz * gain
    return r * (
        s
        - jnp.mean(s, axis=-1, keepdims=True)
        - zhat * jnp.mean(s * zhat, axis=-1, keepdims=True)
    )


def params(mib):
    return pltpu.CompilerParams(vmem_limit_bytes=mib * 2**20)


ANYWHERE = pl.BlockSpec(memory_space=pl.ANY)


def whole(shape):
    return pl.BlockSpec(shape, lambda *_: (0,) * len(shape), pipeline_mode=pl.Buffered(1))


def fold_band(x):
    r = x.shape[0]
    while r > 1:
        r //= 2
        x = pltpu.roll(x[:r], r, 1) + x[r:]
    return x


def bias_tile(band, h, base):
    return jnp.concatenate(
        [
            jnp.concatenate([band[h, base + u - t] for u in range(SUB)], axis=1)
            for t in range(SUB)
        ],
        axis=0,
    )


def column(row):
    return jnp.broadcast_to(row.astype(F32), (8, row.shape[1])).T[:, 0:1]


def tile_range(segs, row, i, nb, back=False):
    ends = [(segs[row, t * TILE], segs[row, t * TILE + TILE - 1]) for t in range(nb)]
    first, last = ends[i]
    lo, hi = i, i + 1
    for t in range(i):
        lo = lo - (ends[t][1] == first).astype(jnp.int32)
    for t in range(i + 1, nb):
        shared = ends[t][0] == last
        if back:
            shared = shared & (last >= 0)
        hi = hi + shared.astype(jnp.int32)
    if back:
        hi = jnp.where(first >= 0, hi, lo)
    return lo, hi


def attend_body(
    row_ref, segs, tok_ref, seg_ref, gains_ref, biases_ref, w_ref, hv_ref, rev_ref, *rest
):
    oc_ref, lse_ref, h1t_hbm, q_hbm, k_hbm, v_hbm, band_hbm = rest[-19:-12]
    h1, h1t, q_s, k_s, v_s, band, vt, docs, km, acc, ml, sems = rest[-12:]
    row = row_ref[0]
    seq, d = tok_ref.shape
    nb = seq // TILE
    bw = seq // 128 - 1
    nh = d // HEAD
    tiles = 2 * seq // 128
    gain = gains_ref[0:1, :].astype(F32)
    shift = biases_ref[0:1, :].astype(F32)
    for b in range(seq // BLOCK):
        r = slice(b * BLOCK, (b + 1) * BLOCK)
        z, _ = normed(tok_ref[r, :].astype(F32))
        y = (z * gain + shift).astype(BF16)
        h1[r, :] = y
        h1t[:, r] = y.astype(F32).T.astype(BF16)
    lane = lax.broadcasted_iota(jnp.int32, (seq, 128), 1)
    doc = column(seg_ref[pl.ds(row, 1), :]).astype(jnp.int32) + 1
    zero = jnp.zeros((), BF16)
    hot = jnp.where(lane == doc, 1.0, 0.0).astype(BF16)
    bar = jnp.where((lane < DOCS) & (lane != doc), NEG, 0.0).astype(BF16)
    docs[0] = hot
    docs[1] = bar
    for c0 in range(0, d, 256):
        cc = slice(c0, c0 + 256)
        x = h1[...]
        q_s[:, cc] = (dot(x, w_ref[0, :, cc]) * 0.125 + hv_ref[1:2, cc] * 0.125).astype(BF16)
        k_s[:, cc] = dot(x, w_ref[1, :, cc]).astype(BF16)
        v_s[:, cc] = (dot(x, w_ref[2, :, cc]) - (-hv_ref[2:3, cc])).astype(BF16)
        for h in range(c0 // HEAD, c0 // HEAD + 4):
            base8 = jnp.broadcast_to(rev_ref[h : h + 1, :] * LOG2E, (8, 2 * seq))
            base8 = pltpu.roll(base8, 2 * seq - 127, 1, stride=1, stride_axis=0)
            for g in range(16):
                y = pltpu.roll(base8, 8 * g, 1) if g else base8
                for t in range(tiles):
                    band[h, t, 8 * g : 8 * g + 8, :] = y[:, 128 * t : 128 * t + 128]
            half = (lane < HEAD) if h % 2 == 0 else (lane >= HEAD)
            c = slice(128 * (h // 2), 128 * (h // 2) + 128)
            km[h] = jnp.where(half, k_s[:, c], zero)
        for j in (c0 // 128, c0 // 128 + 1):
            c = slice(128 * j, 128 * j + 128)
            for b in range(nb):
                vv = v_s[b * TILE : (b + 1) * TILE, c].astype(F32).T.astype(BF16)
                for h in range(2):
                    at = LONG * (2 * j + h)
                    vt[b, at : at + HEAD, :] = vv[HEAD * h : HEAD * h + HEAD]
                    vt[b, at + HEAD : at + LONG, :] = jnp.ones((LONG - HEAD, TILE), BF16)
    copies = [
        pltpu.make_async_copy(a, b, sems.at[i])
        for i, (a, b) in enumerate(
            ((h1t, h1t_hbm), (q_s, q_hbm), (k_s, k_hbm), (v_s, v_hbm), (band, band_hbm))
        )
    ]
    for copy in copies:
        copy.start()
    for qb in range(nb):
        qs = slice(qb * TILE, (qb + 1) * TILE)
        acc[...] = jnp.zeros_like(acc)
        ml[...] = jnp.full((nh, TILE), -jnp.inf, F32)

        def step(kb, _):
            ks = pl.ds(pl.multiple_of(kb * TILE, TILE), TILE)
            base = bw + SUB * qb - SUB * kb
            ss = [
                dot(
                    jnp.concatenate([km[h, ks, :], docs[0, ks, :]], axis=1),
                    jnp.concatenate([q_s[qs, 128 * (h // 2) : 128 * (h // 2) + 128], docs[1, qs, :]], axis=1),
                    NT,
                )
                for h in range(nh)
            ]
            for h in range(nh):
                s = ss[h] * LOG2E + bias_tile(band, h, base)
                old = ml[h : h + 1, :]
                top = jnp.maximum(old, jnp.max(s, axis=0, keepdims=True))
                fade = jnp.exp2(old - top)
                w = jnp.exp2(s - top)
                ml[h : h + 1, :] = top
                r = slice(LONG * h, LONG * h + LONG)
                acc[r, :] = acc[r, :] * fade + dot(vt[kb, r, :], w.astype(BF16))
            return _

        lo, hi = tile_range(segs, row, qb, nb)
        lax.fori_loop(lo, hi, step, 0)
        for j in range(nh // 2):
            outs = []
            for h in (2 * j, 2 * j + 1):
                total = acc[LONG * h + HEAD : LONG * h + HEAD + 1, :]
                lse_ref[h : h + 1, qs] = ml[h : h + 1, :] * (1 / LOG2E) + jnp.log(total)
                outs.append(acc[LONG * h : LONG * h + HEAD, :] * (1.0 / total))
            c = slice(128 * j, 128 * j + 128)
            oc_ref[qs, c] = (jnp.concatenate(outs, axis=0).T * hv_ref[0:1, c]).astype(BF16)
    lse_ref[nh:, :] = jnp.zeros((lse_ref.shape[0] - nh, seq), F32)
    for copy in copies:
        copy.wait()


def attend(row, tokens, segs, gains, biases, w_qkv, hv, rev, after=()):
    d = tokens.shape[1]
    seq = segs.shape[1]
    nh = d // HEAD
    rows = -(-nh // 8) * 8
    tiles = 2 * seq // 128
    s = jax.ShapeDtypeStruct
    return pl.pallas_call(
        attend_body,
        grid_spec=pltpu.PrefetchScalarGridSpec(
            num_scalar_prefetch=2,
            grid=(1,),
            in_specs=[pl.BlockSpec((seq, d), lambda i, row, *_: (row[0], 0), pipeline_mode=pl.Buffered(1))]
            + [whole(x.shape) for x in (segs, gains, biases, w_qkv, hv, rev)]
            + [ANYWHERE] * len(after),
            out_specs=[whole((seq, d)), whole((rows, seq))] + [ANYWHERE] * 5,
            scratch_shapes=[pltpu.VMEM((seq, d), BF16), pltpu.VMEM((d, seq), BF16)]
            + [pltpu.VMEM((seq, d), BF16)] * 3
            + [
                pltpu.VMEM((nh, tiles, 128, 128), F32),
                pltpu.VMEM((seq // TILE, LONG * nh, TILE), BF16),
                pltpu.VMEM((2, seq, 128), BF16),
                pltpu.VMEM((nh, seq, 128), BF16),
                pltpu.VMEM((LONG * nh, TILE), F32),
                pltpu.VMEM((nh, TILE), F32),
                pltpu.SemaphoreType.DMA((5,)),
            ],
        ),
        out_shape=[s((seq, d), BF16), s((rows, seq), F32), s((d, seq), BF16)]
        + [s((seq, d), BF16)] * 3
        + [s((nh, tiles, 128, 128), F32)],
        compiler_params=params(60),
        cost_estimate=pl.CostEstimate(flops=COST, bytes_accessed=COST, transcendentals=0),
        name="attend",
    )(row, segs, tokens, segs, gains, biases, w_qkv, hv, rev, *after)


def attend_back_body(
    row_ref, segs, q_ref, k_ref, v_ref, do_ref, x_ref, seg_ref, band, h1t_ref, *rest
):
    dq_ref, dk_ref, dv_ref, tg_ref, wg_ref, gband, km, vm, kt, dqt, dka, dva = rest[-12:]
    seq = q_ref.shape[0]
    nb = seq // TILE
    bw = seq // 128 - 1
    nh = q_ref.shape[1] // HEAD
    heads = pl.num_programs(0) * nh
    first = pl.program_id(0) * nh
    lane = lax.broadcasted_iota(jnp.int32, (seq, 128), 1)
    row = row_ref[0]
    hot = lane == column(seg_ref[pl.ds(row, 1), :]).astype(jnp.int32) + 1
    zero = jnp.zeros((), BF16)
    gband[...] = jnp.zeros_like(gband)
    dqt[...] = jnp.zeros_like(dqt)
    for h in range(nh):
        half = (lane < HEAD) if h % 2 == 0 else (lane >= HEAD)
        c = slice(128 * (h // 2), 128 * (h // 2) + 128)
        at = DOCS + 3 * (first + h)
        km[h, :, :128] = jnp.where(half, k_ref[:, c], zero)
        km[h, :, 128:] = jnp.where(hot | ((lane >= at) & (lane < at + 3)), 1.0, 0.0).astype(BF16)
        at = at + 3 * heads
        vm[h, :, :128] = jnp.where(half, v_ref[:, c], zero)
        vm[h, :, 128:] = jnp.where((lane >= at) & (lane < at + 3), 1.0, 0.0).astype(BF16)
    for j in range(nh // 2):
        c = slice(128 * j, 128 * j + 128)
        kt[c, :] = k_ref[:, c].astype(F32).T.astype(BF16)
    low = lax.broadcasted_iota(jnp.int32, (TILE, 128), 1) < HEAD
    for kb in range(nb):
        dka[...] = jnp.zeros_like(dka)
        dva[...] = jnp.zeros_like(dva)
        ks = slice(kb * TILE, (kb + 1) * TILE)

        def step(qb, _):
            qs = pl.ds(pl.multiple_of(qb * TILE, TILE), TILE)
            base = bw + SUB * qb - SUB * kb
            cols = [slice(128 * j, 128 * j + 128) for j in range(nh // 2)]
            qs_ = [jnp.concatenate([q_ref[qs, c], x_ref[qs, :]], axis=1) for c in cols]
            ds_ = [jnp.concatenate([do_ref[qs, c], x_ref[qs, :]], axis=1) for c in cols]
            ss = [dot(km[h, ks, :], qs_[h // 2], NT) for h in range(nh)]
            dps = [dot(vm[h, ks, :], ds_[h // 2], NT) for h in range(nh)]
            for h in range(nh):
                w = jnp.exp2(ss[h] * LOG2E + bias_tile(band, h, base))
                ds = (w * dps[h]).astype(BF16)
                dsf = ds.astype(F32)
                for off in range(1 - SUB, SUB):
                    total = None
                    for t in range(SUB):
                        u = off + t
                        if 0 <= u < SUB:
                            piece = dsf[128 * t : 128 * t + 128, 128 * u : 128 * u + 128]
                            total = piece if total is None else total + piece
                    gband[h, base + off] += total
                dva[h] += dot(w.astype(BF16), do_ref[qs, cols[h // 2]])
                dka[h] += dot(ds, q_ref[qs, cols[h // 2]])
                r = slice(HEAD * h, HEAD * h + HEAD)
                dqt[qb, r, :] += dot(kt[r, ks], ds)
            return _

        lo, hi = tile_range(segs, row, kb, nb, True)
        lax.fori_loop(lo, hi, step, 0)
        for j in range(nh // 2):
            c = slice(128 * j, 128 * j + 128)
            dk_ref[ks, c] = jnp.where(low, dka[2 * j], dka[2 * j + 1]).astype(BF16)
            dv_ref[ks, c] = jnp.where(low, dva[2 * j], dva[2 * j + 1]).astype(BF16)
    for j in range(nh // 2):
        c = slice(128 * j, 128 * j + 128)
        for b in range(nb):
            dq_ref[b * TILE : (b + 1) * TILE, c] = (
                dqt[b, c, :].T.astype(BF16).astype(F32) * 0.125
            ).astype(BF16)
    wide = HEAD * nh
    for i, ref in enumerate((dq_ref, dk_ref, dv_ref)):
        wg_ref[:, i * wide : (i + 1) * wide] = dot(h1t_ref[...], ref[...]).astype(BF16)
    for h in range(nh):
        tg_ref[0, h : h + 1, :] = fold_band(
            jnp.concatenate([gband[h, t] for t in range(2 * seq // 128)], axis=1)
        )


def attend_back(row, q, k, v, do, aux, segs, band, h1t, after=()):
    seq, width = q.shape
    heads = width // HEAD
    nh = 4 if heads % 4 == 0 else 2
    groups = heads // nh
    blk = pl.BlockSpec((seq, HEAD * nh), lambda p, *_: (0, p))
    tiles = 2 * seq // 128
    dq, dk, dv, tg, wg = pl.pallas_call(
        attend_back_body,
        grid_spec=pltpu.PrefetchScalarGridSpec(
            num_scalar_prefetch=2,
            grid=(groups,),
            in_specs=[blk] * 4
            + [
                pl.BlockSpec((seq, 128), lambda p, *_: (0, 0)),
                whole(segs.shape),
                pl.BlockSpec((nh, tiles, 128, 128), lambda p, *_: (p, 0, 0, 0)),
                whole(h1t.shape),
            ]
            + [ANYWHERE] * len(after),
            out_specs=[blk] * 3
            + [
                pl.BlockSpec((1, nh, 2 * seq), lambda p, *_: (p, 0, 0)),
                pl.BlockSpec((width, 3 * HEAD * nh), lambda p, *_: (0, p)),
            ],
            scratch_shapes=[
                pltpu.VMEM((nh, tiles, 128, 128), F32),
                pltpu.VMEM((nh, seq, 256), BF16),
                pltpu.VMEM((nh, seq, 256), BF16),
                pltpu.VMEM((HEAD * nh, seq), BF16),
                pltpu.VMEM((seq // TILE, HEAD * nh, TILE), F32),
                pltpu.VMEM((nh, TILE, 128), F32),
                pltpu.VMEM((nh, TILE, 128), F32),
            ],
        ),
        out_shape=[jax.ShapeDtypeStruct((seq, width), BF16)] * 3
        + [jax.ShapeDtypeStruct((groups, nh, 2 * seq), F32), jax.ShapeDtypeStruct((width, 3 * width), BF16)],
        compiler_params=params(60),
        cost_estimate=pl.CostEstimate(flops=COST, bytes_accessed=COST, transcendentals=0),
        name="attend_back",
    )(row, segs, q, k, v, do, aux, segs, band, h1t, *after)
    return dq, dk, dv, tg.reshape(heads, 2 * seq), wg, groups


def gelu_parts(u):
    dens = jnp.exp2(u * u * (-0.5 * LOG2E))
    t = 1.0 / (1.0 + (0.3275911 * 0.7071067811865476) * jnp.abs(u))
    poly = t * (0.127414796 + t * (-0.142248368 + t * (0.7107068705 + t * (-0.7265760135 + t * 0.5307027145))))
    tail = poly * dens
    phi = jnp.where(u >= 0, 1.0 - tail, tail)
    return phi, phi + u * (dens * 0.3989422804014327)


STEP = 512


def middle_body(
    row_ref, tok_ref, oc_ref, gains_ref, biases_ref, fgain_ref, fbias_ref, wo_ref, wu_ref, wd_ref, *rest
):
    out_ref, h3_ref, m_ref, mh_ref, gp_ref, z_ref, stat_ref, e_s, wu, wd, sems = rest[-11:]
    ff = wu_ref.shape[1]
    copies = [pltpu.make_async_copy(a, b, sems.at[i]) for i, (a, b) in enumerate(((wu_ref, wu), (wd_ref, wd)))]

    @pl.when(pl.program_id(0) == 0)
    def _():
        for copy in copies:
            copy.start()

    gains = gains_ref[...].astype(F32)
    biases = biases_ref[...].astype(F32)
    tok = tok_ref[...].astype(F32)
    n, d = tok.shape
    z2, r2 = normed(dot(oc_ref[...], wo_ref[...]) - (-biases[1:2]))
    x2 = tok + (z2 * gains[1:2] + biases[2:3])
    z3, r3 = normed(x2)
    h3 = (z3 * gains[2:3] + biases[3:4]).astype(BF16)
    h3_ref[...] = h3
    z_ref[:, :d] = z2.astype(BF16)
    z_ref[:, d:] = z3.astype(BF16)

    @pl.when(pl.program_id(0) == 0)
    def _():
        copies[0].wait()

    s1 = jnp.zeros((n, 1), F32)
    s2 = jnp.zeros((n, 1), F32)
    for c0 in range(0, ff, STEP):
        c = slice(c0, c0 + STEP)
        u = dot(h3, wu[:, c]) - (-fbias_ref[0:1, c].astype(F32))
        phi, slope = gelu_parts(u)
        e = u * phi
        e_s[:, c] = e
        gp_ref[:, c] = slope.astype(BF16)
        s1 += jnp.sum(e, axis=1, keepdims=True)
        s2 += jnp.sum(e * e, axis=1, keepdims=True)

    @pl.when(pl.program_id(0) == 0)
    def _():
        copies[1].wait()

    mean = s1 / ff
    r = lax.rsqrt(s2 / ff - mean * mean + EPS)
    y = jnp.zeros((n, d), F32)
    for c0 in range(0, ff, STEP):
        c = slice(c0, c0 + STEP)
        mh = (e_s[:, c] - mean) * r
        mh_ref[:, c] = mh.astype(BF16)
        m = (mh * fgain_ref[0:1, c].astype(F32) + fbias_ref[1:2, c].astype(F32)).astype(BF16)
        m_ref[:, c] = m
        y += dot(m, wd[c, :])
    out_ref[...] = (x2 + (y + biases[4:5])).astype(BF16)
    lane = lax.broadcasted_iota(jnp.int32, (n, 128), 1)
    stat_ref[...] = jnp.where(lane == 0, r2, jnp.where(lane == 1, r3, r))


def middle(row, tokens, oc, gains, biases, fgain, fbias, w_out, w_up, w_down, after=()):
    n, d = oc.shape
    ff = w_up.shape[1]
    steps = n // BLOCK
    blk = pl.BlockSpec((BLOCK, d), lambda i, row: (i, 0))
    wide = pl.BlockSpec((BLOCK, ff), lambda i, row: (i, 0))
    s = jax.ShapeDtypeStruct
    return pl.pallas_call(
        middle_body,
        grid_spec=pltpu.PrefetchScalarGridSpec(
            num_scalar_prefetch=1,
            grid=(steps,),
            in_specs=[pl.BlockSpec((BLOCK, d), lambda i, row: (row[0] * steps + i, 0)), blk]
            + [whole(x.shape) for x in (gains, biases, fgain, fbias, w_out)]
            + [ANYWHERE] * (2 + len(after)),
            out_specs=[
                blk, blk, wide, wide, wide,
                pl.BlockSpec((BLOCK, 2 * d), lambda i, row: (i, 0)),
                pl.BlockSpec((BLOCK, 128), lambda i, row: (i, 0)),
            ],
            scratch_shapes=[
                pltpu.VMEM((BLOCK, ff), F32),
                pltpu.VMEM((d, ff), BF16),
                pltpu.VMEM((ff, d), BF16),
                pltpu.SemaphoreType.DMA((2,)),
            ],
        ),
        out_shape=[s((n, d), BF16)] * 2 + [s((n, ff), BF16)] * 3 + [s((n, 2 * d), BF16), s((n, 128), F32)],
        compiler_params=params(60),
        cost_estimate=pl.CostEstimate(flops=COST, bytes_accessed=COST, transcendentals=0),
        name="middle",
    )(row, tokens, oc, gains, biases, fgain, fbias, w_out, w_up, w_down, *after)


def task_weight(counts_ref, tasks):
    counts = counts_ref[0:1, :]
    lane = lax.broadcasted_iota(jnp.int32, counts.shape, 1)
    own = jnp.sum(jnp.where(lane == tasks[0], counts, 0.0), axis=1, keepdims=True)
    return jnp.sum(counts, axis=1, keepdims=True) / (TASKS * own)


def middle_back_body(
    row_ref, tasks, og_ref, seg_ref, counts_ref, oc_ref, lse_ref, mh_ref, gp_ref, z_ref, stat_ref,
    gains_ref, fgain_ref, hs_ref, wo_ref, wu_ref, wd_ref, *rest
):
    df_ref, du_ref, dx2_ref, da_ref, do_ref, aux_ref, nv_ref, fv_ref, d_s, wu, sem = rest[-11:]
    copy = pltpu.make_async_copy(wu_ref, wu, sem.at[0])

    @pl.when(pl.program_id(0) == 0)
    def _():
        copy.start()

    d, ff = wu_ref.shape
    heads = d // HEAD
    gains = gains_ref[...].astype(F32)
    oc = oc_ref[...]
    rows = oc.shape[0]
    here = pl.ds(pl.multiple_of(pl.program_id(0) * rows, rows), rows)
    doc = column(seg_ref[pl.ds(row_ref[0], 1), here])
    g = og_ref[...].astype(F32) * jnp.where(doc >= 0, task_weight(counts_ref, tasks), 0.0)
    df = g.astype(BF16)
    df_ref[...] = df
    r2 = stat_ref[:, 0:1]
    r3 = stat_ref[:, 1:2]
    r = stat_ref[:, 2:3]
    b1 = jnp.zeros((rows, 1), F32)
    b2 = jnp.zeros((rows, 1), F32)
    gsum, bsum, usum = [], [], []
    for c0 in range(0, ff, STEP):
        c = slice(c0, c0 + STEP)
        mh = mh_ref[:, c].astype(F32)
        dm = dot(df, wd_ref[c, :], NT)
        gsum.append(jnp.sum(dm * mh, axis=0, keepdims=True))
        bsum.append(jnp.sum(dm, axis=0, keepdims=True))
        sc = dm * fgain_ref[0:1, c].astype(F32)
        d_s[:, c] = sc
        b1 += jnp.sum(sc, axis=1, keepdims=True)
        b2 += jnp.sum(sc * mh, axis=1, keepdims=True)
    b1 = b1 / ff
    b2 = b2 / ff

    @pl.when(pl.program_id(0) == 0)
    def _():
        copy.wait()

    dh3 = jnp.zeros((rows, d), F32)
    for c0 in range(0, ff, STEP):
        c = slice(c0, c0 + STEP)
        de = r * (d_s[:, c] - b1 - mh_ref[:, c].astype(F32) * b2)
        du = (de * gp_ref[:, c].astype(F32)).astype(BF16)
        du_ref[:, c] = du
        usum.append(jnp.sum(du.astype(F32), axis=0, keepdims=True))
        dh3 += dot(du, wu[:, c], NT)
    z2 = z_ref[:, :d].astype(F32)
    z3 = z_ref[:, d:].astype(F32)
    dx2 = g + norm_back(dh3, gains[2:3], z3, r3)
    dx2_ref[...] = dx2
    da = norm_back(dx2, gains[1:2], z2, r2).astype(BF16)
    da_ref[...] = da
    doc_ = dot(da, wo_ref[...], NT)
    hs = hs_ref[0:1, :]
    o = oc.astype(F32) / hs
    do = (doc_ * hs).astype(BF16)
    do_ref[...] = do

    prod = do.astype(F32) * o
    hi = prod.astype(BF16)
    lo = (prod - hi.astype(F32)).astype(BF16)
    at = DOCS + 3 * heads
    head_of = lax.broadcasted_iota(jnp.int32, (d, 128), 0) // HEAD
    lane = lax.broadcasted_iota(jnp.int32, (d, 128), 1)
    put = jnp.where((lane >= at + 3 * head_of) & (lane < at + 3 * head_of + 3), -1.0, 0.0).astype(BF16)
    delta = dot(hi, put) + dot(lo, put)
    pa, pb, pc = split3(delta)
    lane = lax.broadcasted_iota(jnp.int32, (rows, 128), 1)
    part = (lane - at + 3 * 128) % 3
    delta = jnp.where(part == 0, pa.astype(F32), jnp.where(part == 1, pb.astype(F32), pc.astype(F32)))
    hrows = lse_ref.shape[0]
    la, lb, lc = split3(lse_ref[...])
    stack = jnp.concatenate([la.astype(F32), lb.astype(F32), lc.astype(F32)], axis=0).astype(BF16)
    row = lax.broadcasted_iota(jnp.int32, (3 * hrows, 128), 0)
    col = lax.broadcasted_iota(jnp.int32, (3 * hrows, 128), 1)
    put = jnp.where((row % hrows < heads) & (col == DOCS + 3 * (row % hrows) + row // hrows), -1.0, 0.0)
    lse = dot(stack, put.astype(BF16), TN)
    bar = jnp.where((lane < DOCS) & (lane != doc.astype(jnp.int32) + 1), NEG, 0.0)
    aux_ref[...] = (bar + lse + delta).astype(BF16)

    @pl.when(pl.program_id(0) == 0)
    def _():
        nv_ref[...] = jnp.zeros_like(nv_ref)
        fv_ref[...] = jnp.zeros_like(fv_ref)

    sums = (dx2 * z2, dh3 * z3, da.astype(F32), dx2, dh3, df.astype(F32), doc_ * o)
    for i, term in enumerate(sums):
        nv_ref[i : i + 1, :] += jnp.sum(term, axis=0, keepdims=True)
    for i, terms in enumerate((gsum, usum, bsum)):
        fv_ref[i : i + 1, :] += jnp.concatenate(terms, axis=1)


def middle_back(row, tasks, counts, out_grad, segs, oc, lse, mh, gp, z, stat, gains, fgain, hs, w_out, w_up, w_down, after=()):
    n, d = oc.shape
    ff = w_up.shape[1]
    steps = n // BLOCK
    blk = pl.BlockSpec((BLOCK, d), lambda i, *_: (i, 0))
    wide = pl.BlockSpec((BLOCK, ff), lambda i, *_: (i, 0))
    thin = pl.BlockSpec((BLOCK, 128), lambda i, *_: (i, 0))
    s = jax.ShapeDtypeStruct
    return pl.pallas_call(
        middle_back_body,
        grid_spec=pltpu.PrefetchScalarGridSpec(
            num_scalar_prefetch=2,
            grid=(steps,),
            in_specs=[
                pl.BlockSpec((BLOCK, d), lambda i, row, *_: (row[0] * steps + i, 0)),
                whole(segs.shape),
                whole(counts.shape),
                blk,
                pl.BlockSpec((lse.shape[0], BLOCK), lambda i, *_: (0, i)),
                wide, wide, pl.BlockSpec((BLOCK, 2 * d), lambda i, *_: (i, 0)), thin,
            ]
            + [whole(x.shape) for x in (gains, fgain, hs, w_out)]
            + [ANYWHERE, whole(w_down.shape)]
            + [ANYWHERE] * len(after),
            out_specs=[
                blk, wide, blk, blk, blk, thin,
                pl.BlockSpec((8, d), lambda i, *_: (0, 0)),
                pl.BlockSpec((8, ff), lambda i, *_: (0, 0)),
            ],
            scratch_shapes=[pltpu.VMEM((BLOCK, ff), F32), pltpu.VMEM((d, ff), BF16), pltpu.SemaphoreType.DMA((1,))],
        ),
        out_shape=[
            s((n, d), BF16), s((n, ff), BF16), s((n, d), F32), s((n, d), BF16), s((n, d), BF16), s((n, 128), BF16), s((8, d), F32), s((8, ff), F32),
        ],
        compiler_params=params(60),
        cost_estimate=pl.CostEstimate(flops=COST, bytes_accessed=COST, transcendentals=0),
        name="middle_back",
    )(row, tasks, out_grad, segs, counts, oc, lse, mh, gp, z, stat, gains, fgain, hs, w_out, w_up, w_down, *after)


def early_body(h3_ref, df_ref, da_ref, du_ref, m_ref, oc_ref, out_ref, ht, ft, at):
    i = pl.program_id(0)
    steps = (pl.num_programs(0) - 1) // 2

    @pl.when(i == 0)
    def _():
        for source, target in ((h3_ref, ht), (df_ref, ft), (da_ref, at)):
            target[...] = source[...].astype(F32).T.astype(BF16)

    @pl.when(i < steps)
    def _():
        out_ref[...] = dot(ft[...], m_ref[...]).astype(BF16)

    @pl.when((i >= steps) & (i < 2 * steps))
    def _():
        out_ref[...] = dot(ht[...], du_ref[...]).astype(BF16)

    @pl.when(i >= 2 * steps)
    def _():
        out_ref[...] = dot(at[...], oc_ref[...]).astype(BF16)


def early_grads(h3, df, da, du, m, oc):
    n, d = h3.shape
    ff = du.shape[1]
    width = d
    steps = ff // width
    pick = lambda first, count: pl.BlockSpec((n, width), lambda i: (0, jnp.clip(i - first, 0, count - 1)))
    return pl.pallas_call(
        early_body,
        grid=(2 * steps + 1,),
        in_specs=[whole((n, d))] * 3 + [pick(steps, steps), pick(0, steps), pick(2 * steps, 1)],
        out_specs=pl.BlockSpec((d, width), lambda i: (0, i)),
        out_shape=jax.ShapeDtypeStruct((d, 2 * ff + d), BF16),
        scratch_shapes=[pltpu.VMEM((d, n), BF16)] * 3,
        compiler_params=params(60),
        cost_estimate=pl.CostEstimate(flops=COST, bytes_accessed=COST, transcendentals=0),
        name="early_grads",
    )(h3, df, da, du, m, oc)


def input_body(row_ref, tok_ref, dx2_ref, dq_ref, dk_ref, dv_ref, gains_ref, w_ref, *rest):
    tg_ref, nv_ref = rest[-2:]
    z, r = normed(tok_ref[...].astype(F32))
    dh1 = (
        dot(dq_ref[...], w_ref[0], NT) + dot(dk_ref[...], w_ref[1], NT) + dot(dv_ref[...], w_ref[2], NT)
    )
    tg_ref[...] = (dx2_ref[...] + norm_back(dh1, gains_ref[0:1, :].astype(F32), z, r)).astype(BF16)

    @pl.when(pl.program_id(0) == 0)
    def _():
        nv_ref[...] = jnp.zeros_like(nv_ref)

    sums = (dh1 * z, dh1, dq_ref[...].astype(F32), dv_ref[...].astype(F32))
    for i, term in enumerate(sums):
        nv_ref[i : i + 1, :] += jnp.sum(term, axis=0, keepdims=True)


def input_grad(row, tokens, dx2, dq, dk, dv, gains, w_qkv, after=()):
    n, d = dx2.shape
    steps = n // BLOCK
    blk = pl.BlockSpec((BLOCK, d), lambda i, row: (i, 0))
    return pl.pallas_call(
        input_body,
        grid_spec=pltpu.PrefetchScalarGridSpec(
            num_scalar_prefetch=1,
            grid=(steps,),
            in_specs=[pl.BlockSpec((BLOCK, d), lambda i, row: (row[0] * steps + i, 0))]
            + [blk] * 4
            + [whole(gains.shape), whole(w_qkv.shape)]
            + [pl.BlockSpec(memory_space=pl.ANY)] * len(after),
            out_specs=[blk, pl.BlockSpec((8, d), lambda i, row: (0, 0))],
        ),
        out_shape=[jax.ShapeDtypeStruct((n, d), BF16), jax.ShapeDtypeStruct((8, d), F32)],
        compiler_params=params(60),
        cost_estimate=pl.CostEstimate(flops=COST, bytes_accessed=COST, transcendentals=0),
        name="input_grad",
    )(row, tokens, dx2, dq, dk, dv, gains, w_qkv, *after)


def gate_body(*refs):
    refs[-1][0] = 0


def gate(x, *after):
    return pl.pallas_call(
        gate_body,
        in_specs=[ANYWHERE] * (1 + len(after)),
        out_specs=[ANYWHERE, pl.BlockSpec(memory_space=pltpu.SMEM)],
        out_shape=[jax.ShapeDtypeStruct(x.shape, x.dtype), jax.ShapeDtypeStruct((1,), jnp.int32)],
        input_output_aliases={0: 0},
        cost_estimate=pl.CostEstimate(flops=COST, bytes_accessed=COST, transcendentals=0),
        name="gate",
    )(x, *after)[0]


def copy_body(x_ref, o_ref):
    o_ref[...] = x_ref[...]


def copy(x):
    n, d = x.shape
    blk = pl.BlockSpec((n // 8, d), lambda i: (i, 0))
    return pl.pallas_call(
        copy_body,
        grid=(8,),
        in_specs=[blk],
        out_specs=blk,
        out_shape=jax.ShapeDtypeStruct(x.shape, x.dtype),
        name="copy",
    )(x)


def spread_body(row_ref, pair_ref, right_ref, left_ref, qkv_out, o_out, up_out, down_out):
    share = up_out.shape[1]
    cols = qkv_out.shape[2]
    pair = pair_ref[0].astype(F32) + right_ref[...].astype(F32) + left_ref[...].astype(F32)
    down_out[...] = pair[:, :share]
    up_out[...] = pair[:, share : 2 * share]
    small = pair[:, 2 * share :]
    o_out[...] = small[:, :cols].T
    for i in range(3):
        qkv_out[i] = small[:, (i + 1) * cols : (i + 2) * cols]


def spread(row, pair, pair_sums, share):
    _, n, width = pair.shape
    cols = (width - 2 * share) // 4
    s = jax.ShapeDtypeStruct
    own = lambda x: pl.BlockSpec((1,) + x.shape[1:], lambda i, row: (row[0], 0, 0))
    other = lambda x: pl.BlockSpec(x.shape[1:], lambda i, row: (0, 0))
    outs = [s((3, n, cols), F32), s((cols, n), F32), s((n, share), F32), s((n, share), F32)]
    return pl.pallas_call(
        spread_body,
        grid_spec=pltpu.PrefetchScalarGridSpec(
            num_scalar_prefetch=1,
            grid=(1,),
            in_specs=[own(pair), other(pair), other(pair)],
            out_specs=[pl.BlockSpec(x.shape, lambda i, row, k=len(x.shape): (0,) * k) for x in outs],
        ),
        out_shape=outs,
        name="spread",
    )(row, pair, *pair_sums)


def sum_scatter(x, axis):
    size = lax.axis_size(axis)
    me = lax.axis_index(axis)
    count = size.bit_length() - 1

    def swap(x, left, b):
        dim = left.index(b)
        mine = (me >> b) & 1
        send = lax.dynamic_index_in_dim(x, 1 - mine, dim, keepdims=False)
        keep = lax.dynamic_index_in_dim(x, mine, dim, keepdims=False)
        pairs = [(i, i ^ (1 << b)) for i in range(size)]
        return keep + lax.ppermute(send, axis, pairs), [o for o in left if o != b]

    left = list(range(count - 1, -1, -1))
    x, left = swap(x.reshape((2,) * count + (x.shape[0] // size, x.shape[1])), left, 0)
    half = x.shape[-1] // 2
    near, far = (x[..., :half], left), (x[..., half:], left)
    for i in range(1, count):
        near = swap(*near, i)
        far = swap(*far, count - i)
    return jnp.concatenate([near[0], far[0]], axis=-1)


def line_sums(blocks, axis):
    size = lax.axis_size(axis)
    me = lax.axis_index(axis)
    right = left = None
    for step in range(1, size):
        at = jnp.minimum(size - step + me, size - 1)
        pairs = [(i, i + 1) for i in range(step)]
        send = lax.dynamic_index_in_dim(blocks, at, 0, keepdims=False)
        right = lax.ppermute(send if right is None else send + right, axis, pairs)
        at = jnp.maximum(step - 1 - (size - 1 - me), 0)
        pairs = [(size - 1 - i, size - 2 - i) for i in range(step)]
        send = lax.dynamic_index_in_dim(blocks, at, 0, keepdims=False)
        left = lax.ppermute(send if left is None else send + left, axis, pairs)
    return right, left


def partial_sums(x, axis):
    size = lax.axis_size(axis)
    sums = [x]
    step = 1
    while step < size:
        sums.append(sums[-1] + lax.ppermute(sums[-1], axis, [(i, i ^ step) for i in range(size)]))
        step *= 2
    return sums


def add_all(x, axis):
    return partial_sums(x, axis)[-1]


def local(
    tokens, out_grad, segment_ids, row_tasks, rel_buckets, norm_gains, model_biases, w_qkv, qkv_bias,
    rel_bias, head_scale, w_out, w_up, ffn_gain, ffn_biases, w_down,
):
    parts = lax.axis_size("tensor")
    dps = lax.axis_size("dp")
    tensor_index = lax.axis_index("tensor")
    dp_index = lax.axis_index("dp")
    heads = head_scale.shape[0]
    d = tokens.shape[1]
    ff = w_up.shape[1]
    rows, seq = segment_ids.shape
    assert rows == parts

    live = jnp.sum((segment_ids >= 0).astype(F32), axis=1, keepdims=True)
    counts = jnp.sum(jnp.where(row_tasks[:, None] == jnp.arange(TASKS)[None, :], live, 0.0), axis=0)
    sums = partial_sums(jnp.broadcast_to(counts[None, :], (8, TASKS)), "dp")
    counts = sums[-1]

    back = jnp.pad(rel_buckets, (1, 0), constant_values=-1)[::-1]
    onehot = (jnp.arange(rel_bias.shape[1])[:, None] == back[None, :]).astype(BF16)
    rev = jnp.dot(rel_bias, onehot, preferred_element_type=F32)
    hv = jnp.concatenate(
        [jnp.broadcast_to(head_scale[None, :, None], (1, heads, d // heads)), qkv_bias], axis=0
    )
    hv = hv.astype(F32).reshape(3, d)
    fgain = ffn_gain[None, :]
    segs = segment_ids
    row = tensor_index[None]

    oc, lse, h1t, q, k, v, band = attend(
        row, tokens, segs, norm_gains, model_biases, w_qkv, hv, rev, sums[1:2]
    )
    layer_out, h3, m, mh, gp, z, stat = middle(
        row, tokens, oc, norm_gains, model_biases, fgain, ffn_biases, w_out, w_up, w_down, sums[2:3]
    )
    piece = d // dps
    share = ff // parts
    cols = d // parts
    layer_out = lax.all_gather(layer_out, "tensor", axis=0, tiled=True)
    df, du, dx2, da, do, aux, nv, fv = middle_back(
        row, row_tasks, counts, out_grad, segs, oc, lse, mh, gp, z, stat, norm_gains, fgain, hv, w_out, w_up, w_down
    )
    early = early_grads(h3, df, da, du, m, oc)
    dq, dk, dv, tg, late, groups = attend_back(row, q, k, v, do, aux, segs, band, h1t, (early,))
    early = lax.psum_scatter(early, "dp", scatter_dimension=0, tiled=True)
    tokens_grad, nv2 = input_grad(row, tokens, dx2, dq, dk, dv, norm_gains, w_qkv)
    nv2 = gate(nv2, layer_out)
    layer_out = copy(layer_out)
    tokens_grad = lax.all_gather(tokens_grad, "tensor", axis=0, tiled=True)
    late = sum_scatter(gate(late, nv2, early, layer_out), "dp")

    late = late.reshape(piece, groups, 3, d // groups).transpose(0, 2, 1, 3).reshape(piece, 3 * d)
    small = jnp.concatenate([early[:, 2 * ff :], late], axis=1).reshape(piece, 4, parts, cols)
    pair = jnp.concatenate(
        [
            early[:, :ff].reshape(piece, parts, share),
            early[:, ff : 2 * ff].reshape(piece, parts, share),
            small.transpose(0, 2, 1, 3).reshape(piece, parts, 4 * cols),
        ],
        axis=2,
    ).transpose(1, 0, 2)
    pair_sums = line_sums(pair, "tensor")
    project_grad, output_grad, up_grad, down_grad = spread(row, pair, pair_sums, share)
    tokens_grad = gate(tokens_grad, up_grad)
    down_grad = down_grad.T

    position = jnp.einsum("hs,bs->hb", tg, onehot.astype(F32), precision=lax.Precision.HIGHEST)
    head_sum = jnp.sum(nv[6].reshape(heads, d // heads), axis=1)
    vec = jnp.concatenate(
        [
            nv2[0:1].reshape(-1), nv[0:2].reshape(-1),
            nv2[1:2].reshape(-1), nv[2:6].reshape(-1),
            nv2[2:4].reshape(-1),
            fv[0:3].reshape(-1),
            position.reshape(-1),
            head_sum,
        ]
    )
    size = vec.shape[0]
    vec = jnp.pad(vec, (0, -size % 1024)).reshape(-1, 128)
    vec = add_all(add_all(vec, "dp"), "tensor").reshape(-1)
    at = 0

    def take(shape):
        nonlocal at
        n = 1
        for s in shape:
            n *= s
        out = vec[at : at + n].reshape(shape)
        at += n
        return out

    gains_grad = lax.dynamic_slice_in_dim(take((3, d)), dp_index * piece, piece, 1)
    biases_grad = lax.dynamic_slice_in_dim(take((5, d)), dp_index * piece, piece, 1)
    hp = heads // parts
    project_bias = lax.dynamic_slice_in_dim(take((2, heads, d // heads)), tensor_index * hp, hp, 1)
    fgain_grad = lax.dynamic_slice_in_dim(take((ff,)), tensor_index * share, share, 0)
    fbias_grad = lax.dynamic_slice_in_dim(take((2, ff)), tensor_index * share, share, 1)
    position = take(position.shape)
    bp = position.shape[1] // dps
    position = lax.dynamic_slice(position, (tensor_index * hp, dp_index * bp), (hp, bp))
    head_grad = lax.dynamic_slice_in_dim(take((heads,)), tensor_index * hp, hp, 0)
    return (
        layer_out, tokens_grad, gains_grad, biases_grad, project_grad, project_bias, position, head_grad,
        output_grad, up_grad, fgain_grad, fbias_grad, down_grad,
    )


def solution(mesh):
    rows = P("dp", None)
    return jax.shard_map(
        local,
        mesh=mesh,
        in_specs=(rows, rows, rows, P("dp")) + (P(),) * 12,
        out_specs=(
            rows,
            rows,
            P(None, "dp"),
            P(None, "dp"),
            P(None, "dp", "tensor"),
            P(None, "tensor", None),
            P("tensor", "dp"),
            P("tensor"),
            P("tensor", "dp"),
            P("dp", "tensor"),
            P("tensor"),
            P(None, "tensor"),
            P("tensor", "dp"),
        ),
        check_vma=False,
    )
```

```python
import jax
import jax.numpy as jnp
from jax import lax
from jax.experimental import pallas as pl
from jax.experimental.pallas import tpu as pltpu
from jax.sharding import PartitionSpec as P

F32 = jnp.float32
BF16 = jnp.bfloat16
TASKS = 4
EPS = 1e-05
NEG = -1e30
LOG2E = 1.4426950408889634
HEAD = 64
LONG = HEAD + 16
TILE = 256
SUB = TILE // 128
BLOCK = 256
COST = 10**6
DOCS = 16
NT = (((1,), (1,)), ((), ()))
NN = (((1,), (0,)), ((), ()))
TN = (((0,), (0,)), ((), ()))


def dot(a, b, dims=NN):
    return lax.dot_general(a, b, dims, preferred_element_type=F32)


def split3(x):
    a = x.astype(BF16)
    r = x - a.astype(F32)
    b = r.astype(BF16)
    c = (r - b.astype(F32)).astype(BF16)
    return a, b, c


def normed(z):
    c = z - jnp.mean(z, axis=-1, keepdims=True)
    r = lax.rsqrt(jnp.mean(c * c, axis=-1, keepdims=True) + EPS)
    return c * r, r


def norm_back(dz, gain, zhat, r):
    s = dz * gain
    return r * (
        s
        - jnp.mean(s, axis=-1, keepdims=True)
        - zhat * jnp.mean(s * zhat, axis=-1, keepdims=True)
    )


def params(mib):
    return pltpu.CompilerParams(vmem_limit_bytes=mib * 2**20)


ANYWHERE = pl.BlockSpec(memory_space=pl.ANY)


def whole(shape):
    return pl.BlockSpec(shape, lambda *_: (0,) * len(shape), pipeline_mode=pl.Buffered(1))


def fold_band(x):
    r = x.shape[0]
    while r > 1:
        r //= 2
        x = pltpu.roll(x[:r], r, 1) + x[r:]
    return x


def bias_tile(band, h, base):
    return jnp.concatenate(
        [
            jnp.concatenate([band[h, base + u - t] for u in range(SUB)], axis=1)
            for t in range(SUB)
        ],
        axis=0,
    )


def column(row):
    return jnp.broadcast_to(row.astype(F32), (8, row.shape[1])).T[:, 0:1]


def tile_range(segs, row, i, nb, back=False):
    ends = [(segs[row, t * TILE], segs[row, t * TILE + TILE - 1]) for t in range(nb)]
    first, last = ends[i]
    lo, hi = i, i + 1
    for t in range(i):
        lo = lo - (ends[t][1] == first).astype(jnp.int32)
    for t in range(i + 1, nb):
        shared = ends[t][0] == last
        if back:
            shared = shared & (last >= 0)
        hi = hi + shared.astype(jnp.int32)
    if back:
        hi = jnp.where(first >= 0, hi, lo)
    return lo, hi


def attend_body(
    row_ref, segs, tok_ref, seg_ref, gains_ref, biases_ref, w_ref, hv_ref, rev_ref, *rest
):
    oc_ref, lse_ref, h1t_hbm, q_hbm, k_hbm, v_hbm, band_hbm = rest[-19:-12]
    h1, h1t, q_s, k_s, v_s, band, vt, docs, km, acc, ml, sems = rest[-12:]
    row = row_ref[0]
    seq, d = tok_ref.shape
    nb = seq // TILE
    bw = seq // 128 - 1
    nh = d // HEAD
    tiles = 2 * seq // 128
    gain = gains_ref[0:1, :].astype(F32)
    shift = biases_ref[0:1, :].astype(F32)
    for b in range(seq // BLOCK):
        r = slice(b * BLOCK, (b + 1) * BLOCK)
        z, _ = normed(tok_ref[r, :].astype(F32))
        y = (z * gain + shift).astype(BF16)
        h1[r, :] = y
        h1t[:, r] = y.astype(F32).T.astype(BF16)
    lane = lax.broadcasted_iota(jnp.int32, (seq, 128), 1)
    doc = column(seg_ref[pl.ds(row, 1), :]).astype(jnp.int32) + 1
    zero = jnp.zeros((), BF16)
    hot = jnp.where(lane == doc, 1.0, 0.0).astype(BF16)
    bar = jnp.where((lane < DOCS) & (lane != doc), NEG, 0.0).astype(BF16)
    docs[0] = hot
    docs[1] = bar
    for c0 in range(0, d, 256):
        cc = slice(c0, c0 + 256)
        x = h1[...]
        q_s[:, cc] = (dot(x, w_ref[0, :, cc]) * 0.125 + hv_ref[1:2, cc] * 0.125).astype(BF16)
        k_s[:, cc] = dot(x, w_ref[1, :, cc]).astype(BF16)
        v_s[:, cc] = (dot(x, w_ref[2, :, cc]) - (-hv_ref[2:3, cc])).astype(BF16)
        for h in range(c0 // HEAD, c0 // HEAD + 4):
            base8 = jnp.broadcast_to(rev_ref[h : h + 1, :] * LOG2E, (8, 2 * seq))
            base8 = pltpu.roll(base8, 2 * seq - 127, 1, stride=1, stride_axis=0)
            for g in range(16):
                y = pltpu.roll(base8, 8 * g, 1) if g else base8
                for t in range(tiles):
                    band[h, t, 8 * g : 8 * g + 8, :] = y[:, 128 * t : 128 * t + 128]
            half = (lane < HEAD) if h % 2 == 0 else (lane >= HEAD)
            c = slice(128 * (h // 2), 128 * (h // 2) + 128)
            km[h] = jnp.where(half, k_s[:, c], zero)
        for j in (c0 // 128, c0 // 128 + 1):
            c = slice(128 * j, 128 * j + 128)
            for b in range(nb):
                vv = v_s[b * TILE : (b + 1) * TILE, c].astype(F32).T.astype(BF16)
                for h in range(2):
                    at = LONG * (2 * j + h)
                    vt[b, at : at + HEAD, :] = vv[HEAD * h : HEAD * h + HEAD]
                    vt[b, at + HEAD : at + LONG, :] = jnp.ones((LONG - HEAD, TILE), BF16)
    copies = [
        pltpu.make_async_copy(a, b, sems.at[i])
        for i, (a, b) in enumerate(
            ((h1t, h1t_hbm), (q_s, q_hbm), (k_s, k_hbm), (v_s, v_hbm), (band, band_hbm))
        )
    ]
    for copy in copies:
        copy.start()
    for qb in range(nb):
        qs = slice(qb * TILE, (qb + 1) * TILE)
        acc[...] = jnp.zeros_like(acc)
        ml[...] = jnp.full((nh, TILE), -jnp.inf, F32)

        def step(kb, _):
            ks = pl.ds(pl.multiple_of(kb * TILE, TILE), TILE)
            base = bw + SUB * qb - SUB * kb
            ss = [
                dot(
                    jnp.concatenate([km[h, ks, :], docs[0, ks, :]], axis=1),
                    jnp.concatenate([q_s[qs, 128 * (h // 2) : 128 * (h // 2) + 128], docs[1, qs, :]], axis=1),
                    NT,
                )
                for h in range(nh)
            ]
            for h in range(nh):
                s = ss[h] * LOG2E + bias_tile(band, h, base)
                old = ml[h : h + 1, :]
                top = jnp.maximum(old, jnp.max(s, axis=0, keepdims=True))
                fade = jnp.exp2(old - top)
                w = jnp.exp2(s - top)
                ml[h : h + 1, :] = top
                r = slice(LONG * h, LONG * h + LONG)
                acc[r, :] = acc[r, :] * fade + dot(vt[kb, r, :], w.astype(BF16))
            return _

        lo, hi = tile_range(segs, row, qb, nb)
        lax.fori_loop(lo, hi, step, 0)
        for j in range(nh // 2):
            outs = []
            for h in (2 * j, 2 * j + 1):
                total = acc[LONG * h + HEAD : LONG * h + HEAD + 1, :]
                lse_ref[h : h + 1, qs] = ml[h : h + 1, :] * (1 / LOG2E) + jnp.log(total)
                outs.append(acc[LONG * h : LONG * h + HEAD, :] * (1.0 / total))
            c = slice(128 * j, 128 * j + 128)
            oc_ref[qs, c] = (jnp.concatenate(outs, axis=0).T * hv_ref[0:1, c]).astype(BF16)
    lse_ref[nh:, :] = jnp.zeros((lse_ref.shape[0] - nh, seq), F32)
    for copy in copies:
        copy.wait()


def attend(row, tokens, segs, gains, biases, w_qkv, hv, rev, after=()):
    d = tokens.shape[1]
    seq = segs.shape[1]
    nh = d // HEAD
    rows = -(-nh // 8) * 8
    tiles = 2 * seq // 128
    s = jax.ShapeDtypeStruct
    return pl.pallas_call(
        attend_body,
        grid_spec=pltpu.PrefetchScalarGridSpec(
            num_scalar_prefetch=2,
            grid=(1,),
            in_specs=[pl.BlockSpec((seq, d), lambda i, row, *_: (row[0], 0), pipeline_mode=pl.Buffered(1))]
            + [whole(x.shape) for x in (segs, gains, biases, w_qkv, hv, rev)]
            + [ANYWHERE] * len(after),
            out_specs=[whole((seq, d)), whole((rows, seq))] + [ANYWHERE] * 5,
            scratch_shapes=[pltpu.VMEM((seq, d), BF16), pltpu.VMEM((d, seq), BF16)]
            + [pltpu.VMEM((seq, d), BF16)] * 3
            + [
                pltpu.VMEM((nh, tiles, 128, 128), F32),
                pltpu.VMEM((seq // TILE, LONG * nh, TILE), BF16),
                pltpu.VMEM((2, seq, 128), BF16),
                pltpu.VMEM((nh, seq, 128), BF16),
                pltpu.VMEM((LONG * nh, TILE), F32),
                pltpu.VMEM((nh, TILE), F32),
                pltpu.SemaphoreType.DMA((5,)),
            ],
        ),
        out_shape=[s((seq, d), BF16), s((rows, seq), F32), s((d, seq), BF16)]
        + [s((seq, d), BF16)] * 3
        + [s((nh, tiles, 128, 128), F32)],
        compiler_params=params(60),
        cost_estimate=pl.CostEstimate(flops=COST, bytes_accessed=COST, transcendentals=0),
        name="attend",
    )(row, segs, tokens, segs, gains, biases, w_qkv, hv, rev, *after)


def attend_back_body(
    row_ref, segs, q_ref, k_ref, v_ref, do_ref, x_ref, seg_ref, band, h1t_ref, *rest
):
    dq_ref, dk_ref, dv_ref, tg_ref, wg_ref, gband, km, vm, kt, dqt, dka, dva = rest[-12:]
    seq = q_ref.shape[0]
    nb = seq // TILE
    bw = seq // 128 - 1
    nh = q_ref.shape[1] // HEAD
    heads = pl.num_programs(0) * nh
    first = pl.program_id(0) * nh
    lane = lax.broadcasted_iota(jnp.int32, (seq, 128), 1)
    row = row_ref[0]
    hot = lane == column(seg_ref[pl.ds(row, 1), :]).astype(jnp.int32) + 1
    zero = jnp.zeros((), BF16)
    gband[...] = jnp.zeros_like(gband)
    dqt[...] = jnp.zeros_like(dqt)
    for h in range(nh):
        half = (lane < HEAD) if h % 2 == 0 else (lane >= HEAD)
        c = slice(128 * (h // 2), 128 * (h // 2) + 128)
        at = DOCS + 3 * (first + h)
        km[h, :, :128] = jnp.where(half, k_ref[:, c], zero)
        km[h, :, 128:] = jnp.where(hot | ((lane >= at) & (lane < at + 3)), 1.0, 0.0).astype(BF16)
        at = at + 3 * heads
        vm[h, :, :128] = jnp.where(half, v_ref[:, c], zero)
        vm[h, :, 128:] = jnp.where((lane >= at) & (lane < at + 3), 1.0, 0.0).astype(BF16)
    for j in range(nh // 2):
        c = slice(128 * j, 128 * j + 128)
        kt[c, :] = k_ref[:, c].astype(F32).T.astype(BF16)
    low = lax.broadcasted_iota(jnp.int32, (TILE, 128), 1) < HEAD
    for kb in range(nb):
        dka[...] = jnp.zeros_like(dka)
        dva[...] = jnp.zeros_like(dva)
        ks = slice(kb * TILE, (kb + 1) * TILE)

        def step(qb, _):
            qs = pl.ds(pl.multiple_of(qb * TILE, TILE), TILE)
            base = bw + SUB * qb - SUB * kb
            cols = [slice(128 * j, 128 * j + 128) for j in range(nh // 2)]
            qs_ = [jnp.concatenate([q_ref[qs, c], x_ref[qs, :]], axis=1) for c in cols]
            ds_ = [jnp.concatenate([do_ref[qs, c], x_ref[qs, :]], axis=1) for c in cols]
            ss = [dot(km[h, ks, :], qs_[h // 2], NT) for h in range(nh)]
            dps = [dot(vm[h, ks, :], ds_[h // 2], NT) for h in range(nh)]
            for h in range(nh):
                w = jnp.exp2(ss[h] * LOG2E + bias_tile(band, h, base))
                ds = (w * dps[h]).astype(BF16)
                dsf = ds.astype(F32)
                for off in range(1 - SUB, SUB):
                    total = None
                    for t in range(SUB):
                        u = off + t
                        if 0 <= u < SUB:
                            piece = dsf[128 * t : 128 * t + 128, 128 * u : 128 * u + 128]
                            total = piece if total is None else total + piece
                    gband[h, base + off] += total
                dva[h] += dot(w.astype(BF16), do_ref[qs, cols[h // 2]])
                dka[h] += dot(ds, q_ref[qs, cols[h // 2]])
                r = slice(HEAD * h, HEAD * h + HEAD)
                dqt[qb, r, :] += dot(kt[r, ks], ds)
            return _

        lo, hi = tile_range(segs, row, kb, nb, True)
        lax.fori_loop(lo, hi, step, 0)
        for j in range(nh // 2):
            c = slice(128 * j, 128 * j + 128)
            dk_ref[ks, c] = jnp.where(low, dka[2 * j], dka[2 * j + 1]).astype(BF16)
            dv_ref[ks, c] = jnp.where(low, dva[2 * j], dva[2 * j + 1]).astype(BF16)
    for j in range(nh // 2):
        c = slice(128 * j, 128 * j + 128)
        for b in range(nb):
            dq_ref[b * TILE : (b + 1) * TILE, c] = (
                dqt[b, c, :].T.astype(BF16).astype(F32) * 0.125
            ).astype(BF16)
    wide = HEAD * nh
    for i, ref in enumerate((dq_ref, dk_ref, dv_ref)):
        wg_ref[:, i * wide : (i + 1) * wide] = dot(h1t_ref[...], ref[...]).astype(BF16)
    for h in range(nh):
        tg_ref[0, h : h + 1, :] = fold_band(
            jnp.concatenate([gband[h, t] for t in range(2 * seq // 128)], axis=1)
        )


def attend_back(row, q, k, v, do, aux, segs, band, h1t, after=()):
    seq, width = q.shape
    heads = width // HEAD
    nh = 4 if heads % 4 == 0 else 2
    groups = heads // nh
    blk = pl.BlockSpec((seq, HEAD * nh), lambda p, *_: (0, p))
    tiles = 2 * seq // 128
    dq, dk, dv, tg, wg = pl.pallas_call(
        attend_back_body,
        grid_spec=pltpu.PrefetchScalarGridSpec(
            num_scalar_prefetch=2,
            grid=(groups,),
            in_specs=[blk] * 4
            + [
                pl.BlockSpec((seq, 128), lambda p, *_: (0, 0)),
                whole(segs.shape),
                pl.BlockSpec((nh, tiles, 128, 128), lambda p, *_: (p, 0, 0, 0)),
                whole(h1t.shape),
            ]
            + [ANYWHERE] * len(after),
            out_specs=[blk] * 3
            + [
                pl.BlockSpec((1, nh, 2 * seq), lambda p, *_: (p, 0, 0)),
                pl.BlockSpec((width, 3 * HEAD * nh), lambda p, *_: (0, p)),
            ],
            scratch_shapes=[
                pltpu.VMEM((nh, tiles, 128, 128), F32),
                pltpu.VMEM((nh, seq, 256), BF16),
                pltpu.VMEM((nh, seq, 256), BF16),
                pltpu.VMEM((HEAD * nh, seq), BF16),
                pltpu.VMEM((seq // TILE, HEAD * nh, TILE), F32),
                pltpu.VMEM((nh, TILE, 128), F32),
                pltpu.VMEM((nh, TILE, 128), F32),
            ],
        ),
        out_shape=[jax.ShapeDtypeStruct((seq, width), BF16)] * 3
        + [jax.ShapeDtypeStruct((groups, nh, 2 * seq), F32), jax.ShapeDtypeStruct((width, 3 * width), BF16)],
        compiler_params=params(60),
        cost_estimate=pl.CostEstimate(flops=COST, bytes_accessed=COST, transcendentals=0),
        name="attend_back",
    )(row, segs, q, k, v, do, aux, segs, band, h1t, *after)
    return dq, dk, dv, tg, wg, groups


def gelu_parts(u):
    dens = jnp.exp2(u * u * (-0.5 * LOG2E))
    t = 1.0 / (1.0 + (0.3275911 * 0.7071067811865476) * jnp.abs(u))
    poly = t * (0.127414796 + t * (-0.142248368 + t * (0.7107068705 + t * (-0.7265760135 + t * 0.5307027145))))
    tail = poly * dens
    phi = jnp.where(u >= 0, 1.0 - tail, tail)
    return phi, phi + u * (dens * 0.3989422804014327)


STEP = 512


def middle_body(
    row_ref, tok_ref, oc_ref, gains_ref, biases_ref, fgain_ref, fbias_ref, wo_ref, wu_ref, wd_ref, *rest
):
    out_ref, h3_ref, m_ref, mh_ref, gp_ref, z_ref, stat_ref, e_s, wu, wd, sems = rest[-11:]
    ff = wu_ref.shape[1]
    copies = [pltpu.make_async_copy(a, b, sems.at[i]) for i, (a, b) in enumerate(((wu_ref, wu), (wd_ref, wd)))]

    @pl.when(pl.program_id(0) == 0)
    def _():
        for copy in copies:
            copy.start()

    gains = gains_ref[...].astype(F32)
    biases = biases_ref[...].astype(F32)
    tok = tok_ref[...].astype(F32)
    n, d = tok.shape
    z2, r2 = normed(dot(oc_ref[...], wo_ref[...]) - (-biases[1:2]))
    x2 = tok + (z2 * gains[1:2] + biases[2:3])
    z3, r3 = normed(x2)
    h3 = (z3 * gains[2:3] + biases[3:4]).astype(BF16)
    h3_ref[...] = h3
    z_ref[:, :d] = z2.astype(BF16)
    z_ref[:, d:] = z3.astype(BF16)

    @pl.when(pl.program_id(0) == 0)
    def _():
        copies[0].wait()

    s1 = jnp.zeros((n, 1), F32)
    s2 = jnp.zeros((n, 1), F32)
    for c0 in range(0, ff, STEP):
        c = slice(c0, c0 + STEP)
        u = dot(h3, wu[:, c]) - (-fbias_ref[0:1, c].astype(F32))
        phi, slope = gelu_parts(u)
        e = u * phi
        e_s[:, c] = e
        gp_ref[:, c] = slope.astype(BF16)
        s1 += jnp.sum(e, axis=1, keepdims=True)
        s2 += jnp.sum(e * e, axis=1, keepdims=True)

    @pl.when(pl.program_id(0) == 0)
    def _():
        copies[1].wait()

    mean = s1 / ff
    r = lax.rsqrt(s2 / ff - mean * mean + EPS)
    y = jnp.zeros((n, d), F32)
    for c0 in range(0, ff, STEP):
        c = slice(c0, c0 + STEP)
        mh = (e_s[:, c] - mean) * r
        mh_ref[:, c] = mh.astype(BF16)
        m = (mh * fgain_ref[0:1, c].astype(F32) + fbias_ref[1:2, c].astype(F32)).astype(BF16)
        m_ref[:, c] = m
        y += dot(m, wd[c, :])
    out_ref[...] = (x2 + (y + biases[4:5])).astype(BF16)
    lane = lax.broadcasted_iota(jnp.int32, (n, 128), 1)
    stat_ref[...] = jnp.where(lane == 0, r2, jnp.where(lane == 1, r3, r))


def middle(row, tokens, oc, gains, biases, fgain, fbias, w_out, w_up, w_down, after=()):
    n, d = oc.shape
    ff = w_up.shape[1]
    steps = n // BLOCK
    blk = pl.BlockSpec((BLOCK, d), lambda i, row: (i, 0))
    wide = pl.BlockSpec((BLOCK, ff), lambda i, row: (i, 0))
    s = jax.ShapeDtypeStruct
    return pl.pallas_call(
        middle_body,
        grid_spec=pltpu.PrefetchScalarGridSpec(
            num_scalar_prefetch=1,
            grid=(steps,),
            in_specs=[pl.BlockSpec((BLOCK, d), lambda i, row: (row[0] * steps + i, 0)), blk]
            + [whole(x.shape) for x in (gains, biases, fgain, fbias, w_out)]
            + [ANYWHERE] * (2 + len(after)),
            out_specs=[
                blk, blk, wide, wide, wide,
                pl.BlockSpec((BLOCK, 2 * d), lambda i, row: (i, 0)),
                pl.BlockSpec((BLOCK, 128), lambda i, row: (i, 0)),
            ],
            scratch_shapes=[
                pltpu.VMEM((BLOCK, ff), F32),
                pltpu.VMEM((d, ff), BF16),
                pltpu.VMEM((ff, d), BF16),
                pltpu.SemaphoreType.DMA((2,)),
            ],
        ),
        out_shape=[s((n, d), BF16)] * 2 + [s((n, ff), BF16)] * 3 + [s((n, 2 * d), BF16), s((n, 128), F32)],
        compiler_params=params(60),
        cost_estimate=pl.CostEstimate(flops=COST, bytes_accessed=COST, transcendentals=0),
        name="middle",
    )(row, tokens, oc, gains, biases, fgain, fbias, w_out, w_up, w_down, *after)


def task_weight(counts_ref, tasks):
    counts = counts_ref[0:1, :]
    lane = lax.broadcasted_iota(jnp.int32, counts.shape, 1)
    own = jnp.sum(jnp.where(lane == tasks[0], counts, 0.0), axis=1, keepdims=True)
    return jnp.sum(counts, axis=1, keepdims=True) / (TASKS * own)


def middle_back_body(
    row_ref, tasks, og_ref, seg_ref, counts_ref, oc_ref, lse_ref, mh_ref, gp_ref, z_ref, stat_ref,
    gains_ref, fgain_ref, hs_ref, wo_ref, wu_ref, wd_ref, *rest
):
    df_ref, du_ref, dx2_ref, da_ref, do_ref, aux_ref, nv_ref, fv_ref, d_s, wu, sem = rest[-11:]
    copy = pltpu.make_async_copy(wu_ref, wu, sem.at[0])

    @pl.when(pl.program_id(0) == 0)
    def _():
        copy.start()

    d, ff = wu_ref.shape
    heads = d // HEAD
    gains = gains_ref[...].astype(F32)
    oc = oc_ref[...]
    rows = oc.shape[0]
    here = pl.ds(pl.multiple_of(pl.program_id(0) * rows, rows), rows)
    doc = column(seg_ref[pl.ds(row_ref[0], 1), here])
    g = og_ref[...].astype(F32) * jnp.where(doc >= 0, task_weight(counts_ref, tasks), 0.0)
    df = g.astype(BF16)
    df_ref[...] = df
    r2 = stat_ref[:, 0:1]
    r3 = stat_ref[:, 1:2]
    r = stat_ref[:, 2:3]
    b1 = jnp.zeros((rows, 1), F32)
    b2 = jnp.zeros((rows, 1), F32)
    gsum, bsum, usum = [], [], []
    for c0 in range(0, ff, STEP):
        c = slice(c0, c0 + STEP)
        mh = mh_ref[:, c].astype(F32)
        dm = dot(df, wd_ref[c, :], NT)
        gsum.append(jnp.sum(dm * mh, axis=0, keepdims=True))
        bsum.append(jnp.sum(dm, axis=0, keepdims=True))
        sc = dm * fgain_ref[0:1, c].astype(F32)
        d_s[:, c] = sc
        b1 += jnp.sum(sc, axis=1, keepdims=True)
        b2 += jnp.sum(sc * mh, axis=1, keepdims=True)
    b1 = b1 / ff
    b2 = b2 / ff

    @pl.when(pl.program_id(0) == 0)
    def _():
        copy.wait()

    dh3 = jnp.zeros((rows, d), F32)
    for c0 in range(0, ff, STEP):
        c = slice(c0, c0 + STEP)
        de = r * (d_s[:, c] - b1 - mh_ref[:, c].astype(F32) * b2)
        du = (de * gp_ref[:, c].astype(F32)).astype(BF16)
        du_ref[:, c] = du
        usum.append(jnp.sum(du.astype(F32), axis=0, keepdims=True))
        dh3 += dot(du, wu[:, c], NT)
    z2 = z_ref[:, :d].astype(F32)
    z3 = z_ref[:, d:].astype(F32)
    dx2 = g + norm_back(dh3, gains[2:3], z3, r3)
    dx2_ref[...] = dx2
    da = norm_back(dx2, gains[1:2], z2, r2).astype(BF16)
    da_ref[...] = da
    doc_ = dot(da, wo_ref[...], NT)
    hs = hs_ref[0:1, :]
    o = oc.astype(F32) / hs
    do = (doc_ * hs).astype(BF16)
    do_ref[...] = do

    prod = do.astype(F32) * o
    hi = prod.astype(BF16)
    lo = (prod - hi.astype(F32)).astype(BF16)
    at = DOCS + 3 * heads
    head_of = lax.broadcasted_iota(jnp.int32, (d, 128), 0) // HEAD
    lane = lax.broadcasted_iota(jnp.int32, (d, 128), 1)
    put = jnp.where((lane >= at + 3 * head_of) & (lane < at + 3 * head_of + 3), -1.0, 0.0).astype(BF16)
    delta = dot(hi, put) + dot(lo, put)
    pa, pb, pc = split3(delta)
    lane = lax.broadcasted_iota(jnp.int32, (rows, 128), 1)
    part = (lane - at + 3 * 128) % 3
    delta = jnp.where(part == 0, pa.astype(F32), jnp.where(part == 1, pb.astype(F32), pc.astype(F32)))
    hrows = lse_ref.shape[0]
    la, lb, lc = split3(lse_ref[...])
    stack = jnp.concatenate([la.astype(F32), lb.astype(F32), lc.astype(F32)], axis=0).astype(BF16)
    row = lax.broadcasted_iota(jnp.int32, (3 * hrows, 128), 0)
    col = lax.broadcasted_iota(jnp.int32, (3 * hrows, 128), 1)
    put = jnp.where((row % hrows < heads) & (col == DOCS + 3 * (row % hrows) + row // hrows), -1.0, 0.0)
    lse = dot(stack, put.astype(BF16), TN)
    bar = jnp.where((lane < DOCS) & (lane != doc.astype(jnp.int32) + 1), NEG, 0.0)
    aux_ref[...] = (bar + lse + delta).astype(BF16)

    @pl.when(pl.program_id(0) == 0)
    def _():
        nv_ref[...] = jnp.zeros_like(nv_ref)
        fv_ref[...] = jnp.zeros_like(fv_ref)

    sums = (dx2 * z2, dh3 * z3, da.astype(F32), dx2, dh3, df.astype(F32), doc_ * o)
    for i, term in enumerate(sums):
        nv_ref[i : i + 1, :] += jnp.sum(term, axis=0, keepdims=True)
    for i, terms in enumerate((gsum, usum, bsum)):
        fv_ref[i : i + 1, :] += jnp.concatenate(terms, axis=1)


def middle_back(row, tasks, counts, out_grad, segs, oc, lse, mh, gp, z, stat, gains, fgain, hs, w_out, w_up, w_down, after=()):
    n, d = oc.shape
    ff = w_up.shape[1]
    steps = n // BLOCK
    blk = pl.BlockSpec((BLOCK, d), lambda i, *_: (i, 0))
    wide = pl.BlockSpec((BLOCK, ff), lambda i, *_: (i, 0))
    thin = pl.BlockSpec((BLOCK, 128), lambda i, *_: (i, 0))
    s = jax.ShapeDtypeStruct
    return pl.pallas_call(
        middle_back_body,
        grid_spec=pltpu.PrefetchScalarGridSpec(
            num_scalar_prefetch=2,
            grid=(steps,),
            in_specs=[
                pl.BlockSpec((BLOCK, d), lambda i, row, *_: (row[0] * steps + i, 0)),
                whole(segs.shape),
                whole(counts.shape),
                blk,
                pl.BlockSpec((lse.shape[0], BLOCK), lambda i, *_: (0, i)),
                wide, wide, pl.BlockSpec((BLOCK, 2 * d), lambda i, *_: (i, 0)), thin,
            ]
            + [whole(x.shape) for x in (gains, fgain, hs, w_out)]
            + [ANYWHERE, whole(w_down.shape)]
            + [ANYWHERE] * len(after),
            out_specs=[
                blk, wide, blk, blk, blk, thin,
                pl.BlockSpec((8, d), lambda i, *_: (0, 0)),
                pl.BlockSpec((8, ff), lambda i, *_: (0, 0)),
            ],
            scratch_shapes=[pltpu.VMEM((BLOCK, ff), F32), pltpu.VMEM((d, ff), BF16), pltpu.SemaphoreType.DMA((1,))],
        ),
        out_shape=[
            s((n, d), BF16), s((n, ff), BF16), s((n, d), F32), s((n, d), BF16), s((n, d), BF16), s((n, 128), BF16), s((8, d), F32), s((8, ff), F32),
        ],
        compiler_params=params(60),
        cost_estimate=pl.CostEstimate(flops=COST, bytes_accessed=COST, transcendentals=0),
        name="middle_back",
    )(row, tasks, out_grad, segs, counts, oc, lse, mh, gp, z, stat, gains, fgain, hs, w_out, w_up, w_down, *after)


def early_body(h3_ref, df_ref, da_ref, du_ref, m_ref, oc_ref, out_ref, ht, ft, at):
    i = pl.program_id(0)
    steps = (pl.num_programs(0) - 1) // 2

    @pl.when(i == 0)
    def _():
        for source, target in ((h3_ref, ht), (df_ref, ft), (da_ref, at)):
            target[...] = source[...].astype(F32).T.astype(BF16)

    @pl.when(i < steps)
    def _():
        out_ref[...] = dot(ft[...], m_ref[...]).astype(BF16)

    @pl.when((i >= steps) & (i < 2 * steps))
    def _():
        out_ref[...] = dot(ht[...], du_ref[...]).astype(BF16)

    @pl.when(i >= 2 * steps)
    def _():
        out_ref[...] = dot(at[...], oc_ref[...]).astype(BF16)


def early_grads(h3, df, da, du, m, oc):
    n, d = h3.shape
    ff = du.shape[1]
    width = d
    steps = ff // width
    pick = lambda first, count: pl.BlockSpec((n, width), lambda i: (0, jnp.clip(i - first, 0, count - 1)))
    return pl.pallas_call(
        early_body,
        grid=(2 * steps + 1,),
        in_specs=[whole((n, d))] * 3 + [pick(steps, steps), pick(0, steps), pick(2 * steps, 1)],
        out_specs=pl.BlockSpec((d, width), lambda i: (0, i)),
        out_shape=jax.ShapeDtypeStruct((d, 2 * ff + d), BF16),
        scratch_shapes=[pltpu.VMEM((d, n), BF16)] * 3,
        compiler_params=params(60),
        cost_estimate=pl.CostEstimate(flops=COST, bytes_accessed=COST, transcendentals=0),
        name="early_grads",
    )(h3, df, da, du, m, oc)


def input_body(row_ref, tok_ref, dx2_ref, dq_ref, dk_ref, dv_ref, gains_ref, w_ref, *rest):
    tg_ref, nv_ref = rest[-2:]
    z, r = normed(tok_ref[...].astype(F32))
    dh1 = (
        dot(dq_ref[...], w_ref[0], NT) + dot(dk_ref[...], w_ref[1], NT) + dot(dv_ref[...], w_ref[2], NT)
    )
    tg_ref[...] = (dx2_ref[...] + norm_back(dh1, gains_ref[0:1, :].astype(F32), z, r)).astype(BF16)

    @pl.when(pl.program_id(0) == 0)
    def _():
        nv_ref[...] = jnp.zeros_like(nv_ref)

    sums = (dh1 * z, dh1, dq_ref[...].astype(F32), dv_ref[...].astype(F32))
    for i, term in enumerate(sums):
        nv_ref[i : i + 1, :] += jnp.sum(term, axis=0, keepdims=True)


def input_grad(row, tokens, dx2, dq, dk, dv, gains, w_qkv, after=()):
    n, d = dx2.shape
    steps = n // BLOCK
    blk = pl.BlockSpec((BLOCK, d), lambda i, row: (i, 0))
    return pl.pallas_call(
        input_body,
        grid_spec=pltpu.PrefetchScalarGridSpec(
            num_scalar_prefetch=1,
            grid=(steps,),
            in_specs=[pl.BlockSpec((BLOCK, d), lambda i, row: (row[0] * steps + i, 0))]
            + [blk] * 4
            + [whole(gains.shape), whole(w_qkv.shape)]
            + [pl.BlockSpec(memory_space=pl.ANY)] * len(after),
            out_specs=[blk, pl.BlockSpec((8, d), lambda i, row: (0, 0))],
        ),
        out_shape=[jax.ShapeDtypeStruct((n, d), BF16), jax.ShapeDtypeStruct((8, d), F32)],
        compiler_params=params(60),
        cost_estimate=pl.CostEstimate(flops=COST, bytes_accessed=COST, transcendentals=0),
        name="input_grad",
    )(row, tokens, dx2, dq, dk, dv, gains, w_qkv, *after)


def gate_body(*refs):
    refs[-1][0] = 0


def gate(x, *after):
    return pl.pallas_call(
        gate_body,
        in_specs=[ANYWHERE] * (1 + len(after)),
        out_specs=[ANYWHERE, pl.BlockSpec(memory_space=pltpu.SMEM)],
        out_shape=[jax.ShapeDtypeStruct(x.shape, x.dtype), jax.ShapeDtypeStruct((1,), jnp.int32)],
        input_output_aliases={0: 0},
        cost_estimate=pl.CostEstimate(flops=COST, bytes_accessed=COST, transcendentals=0),
        name="gate",
    )(x, *after)[0]


def copy_body(x_ref, o_ref):
    o_ref[...] = x_ref[...]


def copy(x):
    n, d = x.shape
    blk = pl.BlockSpec((n // 8, d), lambda i: (i, 0))
    return pl.pallas_call(
        copy_body,
        grid=(8,),
        in_specs=[blk],
        out_specs=blk,
        out_shape=jax.ShapeDtypeStruct(x.shape, x.dtype),
        name="copy",
    )(x)


def spread_body(row_ref, pair_ref, right_ref, left_ref, qkv_out, o_out, up_out, down_out):
    share = up_out.shape[1]
    cols = qkv_out.shape[2]
    pair = pair_ref[0].astype(F32) + right_ref[...].astype(F32) + left_ref[...].astype(F32)
    down_out[...] = pair[:, :share]
    up_out[...] = pair[:, share : 2 * share]
    small = pair[:, 2 * share :]
    o_out[...] = small[:, :cols].T
    for i in range(3):
        qkv_out[i] = small[:, (i + 1) * cols : (i + 2) * cols]


def spread(row, pair, pair_sums, share):
    _, n, width = pair.shape
    cols = (width - 2 * share) // 4
    s = jax.ShapeDtypeStruct
    own = lambda x: pl.BlockSpec((1,) + x.shape[1:], lambda i, row: (row[0], 0, 0))
    other = lambda x: pl.BlockSpec(x.shape[1:], lambda i, row: (0, 0))
    outs = [s((3, n, cols), F32), s((cols, n), F32), s((n, share), F32), s((n, share), F32)]
    return pl.pallas_call(
        spread_body,
        grid_spec=pltpu.PrefetchScalarGridSpec(
            num_scalar_prefetch=1,
            grid=(1,),
            in_specs=[own(pair), other(pair), other(pair)],
            out_specs=[pl.BlockSpec(x.shape, lambda i, row, k=len(x.shape): (0,) * k) for x in outs],
        ),
        out_shape=outs,
        name="spread",
    )(row, pair, *pair_sums)


def sum_scatter(x, axis):
    size = lax.axis_size(axis)
    me = lax.axis_index(axis)
    count = size.bit_length() - 1

    def swap(x, left, b):
        dim = left.index(b)
        mine = (me >> b) & 1
        send = lax.dynamic_index_in_dim(x, 1 - mine, dim, keepdims=False)
        keep = lax.dynamic_index_in_dim(x, mine, dim, keepdims=False)
        pairs = [(i, i ^ (1 << b)) for i in range(size)]
        return keep + lax.ppermute(send, axis, pairs), [o for o in left if o != b]

    left = list(range(count - 1, -1, -1))
    x, left = swap(x.reshape((2,) * count + (x.shape[0] // size, x.shape[1])), left, 0)
    half = x.shape[-1] // 2
    near, far = (x[..., :half], left), (x[..., half:], left)
    for i in range(1, count):
        near = swap(*near, i)
        far = swap(*far, count - i)
    return jnp.concatenate([near[0], far[0]], axis=-1)


def line_sums(blocks, axis):
    size = lax.axis_size(axis)
    me = lax.axis_index(axis)
    right = left = None
    for step in range(1, size):
        at = jnp.minimum(size - step + me, size - 1)
        pairs = [(i, i + 1) for i in range(step)]
        send = lax.dynamic_index_in_dim(blocks, at, 0, keepdims=False)
        right = lax.ppermute(send if right is None else send + right, axis, pairs)
        at = jnp.maximum(step - 1 - (size - 1 - me), 0)
        pairs = [(size - 1 - i, size - 2 - i) for i in range(step)]
        send = lax.dynamic_index_in_dim(blocks, at, 0, keepdims=False)
        left = lax.ppermute(send if left is None else send + left, axis, pairs)
    return right, left


def partial_sums(x, axis):
    size = lax.axis_size(axis)
    sums = [x]
    step = 1
    while step < size:
        sums.append(sums[-1] + lax.ppermute(sums[-1], axis, [(i, i ^ step) for i in range(size)]))
        step *= 2
    return sums


def add_all(x, axis):
    return partial_sums(x, axis)[-1]


def local(
    tokens, out_grad, segment_ids, row_tasks, rel_buckets, norm_gains, model_biases, w_qkv, qkv_bias,
    rel_bias, head_scale, w_out, w_up, ffn_gain, ffn_biases, w_down,
):
    parts = lax.axis_size("tensor")
    dps = lax.axis_size("dp")
    tensor_index = lax.axis_index("tensor")
    dp_index = lax.axis_index("dp")
    heads = head_scale.shape[0]
    d = tokens.shape[1]
    ff = w_up.shape[1]
    rows, seq = segment_ids.shape
    assert rows == parts

    live = jnp.sum((segment_ids >= 0).astype(F32), axis=1, keepdims=True)
    counts = jnp.sum(jnp.where(row_tasks[:, None] == jnp.arange(TASKS)[None, :], live, 0.0), axis=0)
    sums = partial_sums(jnp.broadcast_to(counts[None, :], (8, TASKS)), "dp")
    counts = sums[-1]

    back = jnp.pad(rel_buckets, (1, 0), constant_values=-1)[::-1]
    onehot = (jnp.arange(rel_bias.shape[1])[:, None] == back[None, :]).astype(BF16)
    rev = jnp.dot(rel_bias, onehot, preferred_element_type=F32)
    hv = jnp.concatenate(
        [jnp.broadcast_to(head_scale[None, :, None], (1, heads, d // heads)), qkv_bias], axis=0
    )
    hv = hv.astype(F32).reshape(3, d)
    fgain = ffn_gain[None, :]
    segs = segment_ids
    row = tensor_index[None]

    oc, lse, h1t, q, k, v, band = attend(
        row, tokens, segs, norm_gains, model_biases, w_qkv, hv, rev, sums[1:2]
    )
    layer_out, h3, m, mh, gp, z, stat = middle(
        row, tokens, oc, norm_gains, model_biases, fgain, ffn_biases, w_out, w_up, w_down, sums[2:3]
    )
    piece = d // dps
    share = ff // parts
    cols = d // parts
    layer_out = lax.all_gather(layer_out, "tensor", axis=0, tiled=True)
    df, du, dx2, da, do, aux, nv, fv = middle_back(
        row, row_tasks, counts, out_grad, segs, oc, lse, mh, gp, z, stat, norm_gains, fgain, hv, w_out, w_up, w_down
    )
    early = early_grads(h3, df, da, du, m, oc)
    dq, dk, dv, tg, late, groups = attend_back(row, q, k, v, do, aux, segs, band, h1t, (early,))
    early = lax.psum_scatter(early, "dp", scatter_dimension=0, tiled=True)
    tokens_grad, nv2 = input_grad(row, tokens, dx2, dq, dk, dv, norm_gains, w_qkv)
    nv2 = gate(nv2, layer_out)
    layer_out = copy(layer_out)
    tokens_grad = lax.all_gather(tokens_grad, "tensor", axis=0, tiled=True)
    late = sum_scatter(gate(late, nv2, early, layer_out), "dp")

    late = late.reshape(piece, groups, 3, d // groups).transpose(0, 2, 1, 3).reshape(piece, 3 * d)
    small = jnp.concatenate([early[:, 2 * ff :], late], axis=1).reshape(piece, 4, parts, cols)
    pair = jnp.concatenate(
        [
            early[:, :ff].reshape(piece, parts, share),
            early[:, ff : 2 * ff].reshape(piece, parts, share),
            small.transpose(0, 2, 1, 3).reshape(piece, parts, 4 * cols),
        ],
        axis=2,
    ).transpose(1, 0, 2)
    pair_sums = line_sums(pair, "tensor")
    project_grad, output_grad, up_grad, down_grad = spread(row, pair, pair_sums, share)
    tokens_grad = gate(tokens_grad, up_grad)
    down_grad = down_grad.T

    position = jnp.einsum("hs,bs->hb", gate(tg, nv2).reshape(heads, 2 * seq), onehot.astype(F32), precision=lax.Precision.HIGHEST)
    head_sum = jnp.sum(nv[6].reshape(heads, d // heads), axis=1)
    vec = jnp.concatenate(
        [
            nv2[0:1].reshape(-1), nv[0:2].reshape(-1),
            nv2[1:2].reshape(-1), nv[2:6].reshape(-1),
            nv2[2:4].reshape(-1),
            fv[0:3].reshape(-1),
            position.reshape(-1),
            head_sum,
        ]
    )
    size = vec.shape[0]
    vec = jnp.pad(vec, (0, -size % 1024)).reshape(-1, 128)
    vec = add_all(add_all(vec, "dp"), "tensor").reshape(-1)
    at = 0

    def take(shape):
        nonlocal at
        n = 1
        for s in shape:
            n *= s
        out = vec[at : at + n].reshape(shape)
        at += n
        return out

    gains_grad = lax.dynamic_slice_in_dim(take((3, d)), dp_index * piece, piece, 1)
    biases_grad = lax.dynamic_slice_in_dim(take((5, d)), dp_index * piece, piece, 1)
    hp = heads // parts
    project_bias = lax.dynamic_slice_in_dim(take((2, heads, d // heads)), tensor_index * hp, hp, 1)
    fgain_grad = lax.dynamic_slice_in_dim(take((ff,)), tensor_index * share, share, 0)
    fbias_grad = lax.dynamic_slice_in_dim(take((2, ff)), tensor_index * share, share, 1)
    position = take(position.shape)
    bp = position.shape[1] // dps
    position = lax.dynamic_slice(position, (tensor_index * hp, dp_index * bp), (hp, bp))
    head_grad = lax.dynamic_slice_in_dim(take((heads,)), tensor_index * hp, hp, 0)
    return (
        layer_out, tokens_grad, gains_grad, biases_grad, project_grad, project_bias, position, head_grad,
        output_grad, up_grad, fgain_grad, fbias_grad, down_grad,
    )


def solution(mesh):
    rows = P("dp", None)
    return jax.shard_map(
        local,
        mesh=mesh,
        in_specs=(rows, rows, rows, P("dp")) + (P(),) * 12,
        out_specs=(
            rows,
            rows,
            P(None, "dp"),
            P(None, "dp"),
            P(None, "dp", "tensor"),
            P(None, "tensor", None),
            P("tensor", "dp"),
            P("tensor"),
            P("tensor", "dp"),
            P("dp", "tensor"),
            P("tensor"),
            P(None, "tensor"),
            P("tensor", "dp"),
        ),
        check_vma=False,
    )
```

```python
import jax
import jax.numpy as jnp
from jax import lax
from jax.experimental import pallas as pl
from jax.experimental.pallas import tpu as pltpu
from jax.sharding import PartitionSpec as P

F32 = jnp.float32
BF16 = jnp.bfloat16
TASKS = 4
EPS = 1e-05
NEG = -1e30
LOG2E = 1.4426950408889634
HEAD = 64
LONG = HEAD + 16
TILE = 256
SUB = TILE // 128
BLOCK = 256
COST = 10**6
DOCS = 16
NT = (((1,), (1,)), ((), ()))
NN = (((1,), (0,)), ((), ()))
TN = (((0,), (0,)), ((), ()))


def dot(a, b, dims=NN):
    return lax.dot_general(a, b, dims, preferred_element_type=F32)


def split3(x):
    a = x.astype(BF16)
    r = x - a.astype(F32)
    b = r.astype(BF16)
    c = (r - b.astype(F32)).astype(BF16)
    return a, b, c


def normed(z):
    c = z - jnp.mean(z, axis=-1, keepdims=True)
    r = lax.rsqrt(jnp.mean(c * c, axis=-1, keepdims=True) + EPS)
    return c * r, r


def norm_back(dz, gain, zhat, r):
    s = dz * gain
    return r * (
        s
        - jnp.mean(s, axis=-1, keepdims=True)
        - zhat * jnp.mean(s * zhat, axis=-1, keepdims=True)
    )


def params(mib):
    return pltpu.CompilerParams(vmem_limit_bytes=mib * 2**20)


ANYWHERE = pl.BlockSpec(memory_space=pl.ANY)


def whole(shape):
    return pl.BlockSpec(shape, lambda *_: (0,) * len(shape), pipeline_mode=pl.Buffered(1))


def fold_band(x):
    r = x.shape[0]
    while r > 1:
        r //= 2
        x = pltpu.roll(x[:r], r, 1) + x[r:]
    return x


def bias_tile(band, h, base):
    return jnp.concatenate(
        [
            jnp.concatenate([band[h, base + u - t] for u in range(SUB)], axis=1)
            for t in range(SUB)
        ],
        axis=0,
    )


def column(row):
    return jnp.broadcast_to(row.astype(F32), (8, row.shape[1])).T[:, 0:1]


def tile_range(segs, row, i, nb, back=False):
    ends = [(segs[row, t * TILE], segs[row, t * TILE + TILE - 1]) for t in range(nb)]
    first, last = ends[i]
    lo, hi = i, i + 1
    for t in range(i):
        lo = lo - (ends[t][1] == first).astype(jnp.int32)
    for t in range(i + 1, nb):
        shared = ends[t][0] == last
        if back:
            shared = shared & (last >= 0)
        hi = hi + shared.astype(jnp.int32)
    if back:
        hi = jnp.where(first >= 0, hi, lo)
    return lo, hi


def attend_body(
    row_ref, segs, tok_ref, seg_ref, gains_ref, biases_ref, w_ref, hv_ref, rev_ref, *rest
):
    oc_ref, lse_ref, h1t_hbm, q_hbm, k_hbm, v_hbm, band_hbm = rest[-19:-12]
    h1, h1t, q_s, k_s, v_s, band, vt, docs, km, acc, ml, sems = rest[-12:]
    row = row_ref[0]
    seq, d = tok_ref.shape
    nb = seq // TILE
    bw = seq // 128 - 1
    nh = d // HEAD
    tiles = 2 * seq // 128
    gain = gains_ref[0:1, :].astype(F32)
    shift = biases_ref[0:1, :].astype(F32)
    for b in range(seq // BLOCK):
        r = slice(b * BLOCK, (b + 1) * BLOCK)
        z, _ = normed(tok_ref[r, :].astype(F32))
        y = (z * gain + shift).astype(BF16)
        h1[r, :] = y
        h1t[:, r] = y.astype(F32).T.astype(BF16)
    lane = lax.broadcasted_iota(jnp.int32, (seq, 128), 1)
    doc = column(seg_ref[pl.ds(row, 1), :]).astype(jnp.int32) + 1
    zero = jnp.zeros((), BF16)
    hot = jnp.where(lane == doc, 1.0, 0.0).astype(BF16)
    bar = jnp.where((lane < DOCS) & (lane != doc), NEG, 0.0).astype(BF16)
    docs[0] = hot
    docs[1] = bar
    for c0 in range(0, d, 256):
        cc = slice(c0, c0 + 256)
        x = h1[...]
        q_s[:, cc] = (dot(x, w_ref[0, :, cc]) * 0.125 + hv_ref[1:2, cc] * 0.125).astype(BF16)
        k_s[:, cc] = dot(x, w_ref[1, :, cc]).astype(BF16)
        v_s[:, cc] = (dot(x, w_ref[2, :, cc]) - (-hv_ref[2:3, cc])).astype(BF16)
        for h in range(c0 // HEAD, c0 // HEAD + 4):
            base8 = jnp.broadcast_to(rev_ref[h : h + 1, :] * LOG2E, (8, 2 * seq))
            base8 = pltpu.roll(base8, 2 * seq - 127, 1, stride=1, stride_axis=0)
            for g in range(16):
                y = pltpu.roll(base8, 8 * g, 1) if g else base8
                for t in range(tiles):
                    band[h, t, 8 * g : 8 * g + 8, :] = y[:, 128 * t : 128 * t + 128]
            half = (lane < HEAD) if h % 2 == 0 else (lane >= HEAD)
            c = slice(128 * (h // 2), 128 * (h // 2) + 128)
            km[h] = jnp.where(half, k_s[:, c], zero)
        for j in (c0 // 128, c0 // 128 + 1):
            c = slice(128 * j, 128 * j + 128)
            for b in range(nb):
                vv = v_s[b * TILE : (b + 1) * TILE, c].astype(F32).T.astype(BF16)
                for h in range(2):
                    at = LONG * (2 * j + h)
                    vt[b, at : at + HEAD, :] = vv[HEAD * h : HEAD * h + HEAD]
                    vt[b, at + HEAD : at + LONG, :] = jnp.ones((LONG - HEAD, TILE), BF16)
    copies = [
        pltpu.make_async_copy(a, b, sems.at[i])
        for i, (a, b) in enumerate(
            ((h1t, h1t_hbm), (q_s, q_hbm), (k_s, k_hbm), (v_s, v_hbm), (band, band_hbm))
        )
    ]
    for copy in copies:
        copy.start()
    for qb in range(nb):
        qs = slice(qb * TILE, (qb + 1) * TILE)
        acc[...] = jnp.zeros_like(acc)
        ml[...] = jnp.full((nh, TILE), -jnp.inf, F32)

        def step(kb, _):
            ks = pl.ds(pl.multiple_of(kb * TILE, TILE), TILE)
            base = bw + SUB * qb - SUB * kb
            ss = [
                dot(
                    jnp.concatenate([km[h, ks, :], docs[0, ks, :]], axis=1),
                    jnp.concatenate([q_s[qs, 128 * (h // 2) : 128 * (h // 2) + 128], docs[1, qs, :]], axis=1),
                    NT,
                )
                for h in range(nh)
            ]
            for h in range(nh):
                s = ss[h] * LOG2E + bias_tile(band, h, base)
                old = ml[h : h + 1, :]
                top = jnp.maximum(old, jnp.max(s, axis=0, keepdims=True))
                fade = jnp.exp2(old - top)
                w = jnp.exp2(s - top)
                ml[h : h + 1, :] = top
                r = slice(LONG * h, LONG * h + LONG)
                acc[r, :] = acc[r, :] * fade + dot(vt[kb, r, :], w.astype(BF16))
            return _

        lo, hi = tile_range(segs, row, qb, nb)
        lax.fori_loop(lo, hi, step, 0)
        for j in range(nh // 2):
            outs = []
            for h in (2 * j, 2 * j + 1):
                total = acc[LONG * h + HEAD : LONG * h + HEAD + 1, :]
                lse_ref[h : h + 1, qs] = ml[h : h + 1, :] * (1 / LOG2E) + jnp.log(total)
                outs.append(acc[LONG * h : LONG * h + HEAD, :] * (1.0 / total))
            c = slice(128 * j, 128 * j + 128)
            oc_ref[qs, c] = (jnp.concatenate(outs, axis=0).T * hv_ref[0:1, c]).astype(BF16)
    lse_ref[nh:, :] = jnp.zeros((lse_ref.shape[0] - nh, seq), F32)
    for copy in copies:
        copy.wait()


def attend(row, tokens, segs, gains, biases, w_qkv, hv, rev, after=()):
    d = tokens.shape[1]
    seq = segs.shape[1]
    nh = d // HEAD
    rows = -(-nh // 8) * 8
    tiles = 2 * seq // 128
    s = jax.ShapeDtypeStruct
    return pl.pallas_call(
        attend_body,
        grid_spec=pltpu.PrefetchScalarGridSpec(
            num_scalar_prefetch=2,
            grid=(1,),
            in_specs=[pl.BlockSpec((seq, d), lambda i, row, *_: (row[0], 0), pipeline_mode=pl.Buffered(1))]
            + [whole(x.shape) for x in (segs, gains, biases, w_qkv, hv, rev)]
            + [ANYWHERE] * len(after),
            out_specs=[whole((seq, d)), whole((rows, seq))] + [ANYWHERE] * 5,
            scratch_shapes=[pltpu.VMEM((seq, d), BF16), pltpu.VMEM((d, seq), BF16)]
            + [pltpu.VMEM((seq, d), BF16)] * 3
            + [
                pltpu.VMEM((nh, tiles, 128, 128), F32),
                pltpu.VMEM((seq // TILE, LONG * nh, TILE), BF16),
                pltpu.VMEM((2, seq, 128), BF16),
                pltpu.VMEM((nh, seq, 128), BF16),
                pltpu.VMEM((LONG * nh, TILE), F32),
                pltpu.VMEM((nh, TILE), F32),
                pltpu.SemaphoreType.DMA((5,)),
            ],
        ),
        out_shape=[s((seq, d), BF16), s((rows, seq), F32), s((d, seq), BF16)]
        + [s((seq, d), BF16)] * 3
        + [s((nh, tiles, 128, 128), F32)],
        compiler_params=params(60),
        cost_estimate=pl.CostEstimate(flops=COST, bytes_accessed=COST, transcendentals=0),
        name="attend",
    )(row, segs, tokens, segs, gains, biases, w_qkv, hv, rev, *after)


def attend_back_body(
    row_ref, segs, q_ref, k_ref, v_ref, do_ref, x_ref, seg_ref, band, h1t_ref, *rest
):
    dq_ref, dk_ref, dv_ref, tg_ref, wg_ref, gband, km, vm, kt, dqt, dka, dva = rest[-12:]
    seq = q_ref.shape[0]
    nb = seq // TILE
    bw = seq // 128 - 1
    nh = q_ref.shape[1] // HEAD
    heads = pl.num_programs(0) * nh
    first = pl.program_id(0) * nh
    lane = lax.broadcasted_iota(jnp.int32, (seq, 128), 1)
    row = row_ref[0]
    hot = lane == column(seg_ref[pl.ds(row, 1), :]).astype(jnp.int32) + 1
    zero = jnp.zeros((), BF16)
    gband[...] = jnp.zeros_like(gband)
    dqt[...] = jnp.zeros_like(dqt)
    for h in range(nh):
        half = (lane < HEAD) if h % 2 == 0 else (lane >= HEAD)
        c = slice(128 * (h // 2), 128 * (h // 2) + 128)
        at = DOCS + 3 * (first + h)
        km[h, :, :128] = jnp.where(half, k_ref[:, c], zero)
        km[h, :, 128:] = jnp.where(hot | ((lane >= at) & (lane < at + 3)), 1.0, 0.0).astype(BF16)
        at = at + 3 * heads
        vm[h, :, :128] = jnp.where(half, v_ref[:, c], zero)
        vm[h, :, 128:] = jnp.where((lane >= at) & (lane < at + 3), 1.0, 0.0).astype(BF16)
    for j in range(nh // 2):
        c = slice(128 * j, 128 * j + 128)
        kt[c, :] = k_ref[:, c].astype(F32).T.astype(BF16)
    low = lax.broadcasted_iota(jnp.int32, (TILE, 128), 1) < HEAD
    for kb in range(nb):
        dka[...] = jnp.zeros_like(dka)
        dva[...] = jnp.zeros_like(dva)
        ks = slice(kb * TILE, (kb + 1) * TILE)

        def step(qb, _):
            qs = pl.ds(pl.multiple_of(qb * TILE, TILE), TILE)
            base = bw + SUB * qb - SUB * kb
            cols = [slice(128 * j, 128 * j + 128) for j in range(nh // 2)]
            qs_ = [jnp.concatenate([q_ref[qs, c], x_ref[qs, :]], axis=1) for c in cols]
            ds_ = [jnp.concatenate([do_ref[qs, c], x_ref[qs, :]], axis=1) for c in cols]
            ss = [dot(km[h, ks, :], qs_[h // 2], NT) for h in range(nh)]
            dps = [dot(vm[h, ks, :], ds_[h // 2], NT) for h in range(nh)]
            for h in range(nh):
                w = jnp.exp2(ss[h] * LOG2E + bias_tile(band, h, base))
                ds = (w * dps[h]).astype(BF16)
                dsf = ds.astype(F32)
                for off in range(1 - SUB, SUB):
                    total = None
                    for t in range(SUB):
                        u = off + t
                        if 0 <= u < SUB:
                            piece = dsf[128 * t : 128 * t + 128, 128 * u : 128 * u + 128]
                            total = piece if total is None else total + piece
                    gband[h, base + off] += total
                dva[h] += dot(w.astype(BF16), do_ref[qs, cols[h // 2]])
                dka[h] += dot(ds, q_ref[qs, cols[h // 2]])
                r = slice(HEAD * h, HEAD * h + HEAD)
                dqt[qb, r, :] += dot(kt[r, ks], ds)
            return _

        lo, hi = tile_range(segs, row, kb, nb, True)
        lax.fori_loop(lo, hi, step, 0)
        for j in range(nh // 2):
            c = slice(128 * j, 128 * j + 128)
            dk_ref[ks, c] = jnp.where(low, dka[2 * j], dka[2 * j + 1]).astype(BF16)
            dv_ref[ks, c] = jnp.where(low, dva[2 * j], dva[2 * j + 1]).astype(BF16)
    for j in range(nh // 2):
        c = slice(128 * j, 128 * j + 128)
        for b in range(nb):
            dq_ref[b * TILE : (b + 1) * TILE, c] = (
                dqt[b, c, :].T.astype(BF16).astype(F32) * 0.125
            ).astype(BF16)
    wide = HEAD * nh
    for i, ref in enumerate((dq_ref, dk_ref, dv_ref)):
        wg_ref[:, i * wide : (i + 1) * wide] = dot(h1t_ref[...], ref[...]).astype(BF16)
    for h in range(nh):
        tg_ref[0, h : h + 1, :] = fold_band(
            jnp.concatenate([gband[h, t] for t in range(2 * seq // 128)], axis=1)
        )


def attend_back(row, q, k, v, do, aux, segs, band, h1t, after=()):
    seq, width = q.shape
    heads = width // HEAD
    nh = 6 if heads % 6 == 0 else 2
    groups = heads // nh
    blk = pl.BlockSpec((seq, HEAD * nh), lambda p, *_: (0, p))
    tiles = 2 * seq // 128
    dq, dk, dv, tg, wg = pl.pallas_call(
        attend_back_body,
        grid_spec=pltpu.PrefetchScalarGridSpec(
            num_scalar_prefetch=2,
            grid=(groups,),
            in_specs=[blk] * 4
            + [
                pl.BlockSpec((seq, 128), lambda p, *_: (0, 0)),
                whole(segs.shape),
                pl.BlockSpec((nh, tiles, 128, 128), lambda p, *_: (p, 0, 0, 0)),
                whole(h1t.shape),
            ]
            + [ANYWHERE] * len(after),
            out_specs=[blk] * 3
            + [
                pl.BlockSpec((1, nh, 2 * seq), lambda p, *_: (p, 0, 0)),
                pl.BlockSpec((width, 3 * HEAD * nh), lambda p, *_: (0, p)),
            ],
            scratch_shapes=[
                pltpu.VMEM((nh, tiles, 128, 128), F32),
                pltpu.VMEM((nh, seq, 256), BF16),
                pltpu.VMEM((nh, seq, 256), BF16),
                pltpu.VMEM((HEAD * nh, seq), BF16),
                pltpu.VMEM((seq // TILE, HEAD * nh, TILE), F32),
                pltpu.VMEM((nh, TILE, 128), F32),
                pltpu.VMEM((nh, TILE, 128), F32),
            ],
        ),
        out_shape=[jax.ShapeDtypeStruct((seq, width), BF16)] * 3
        + [jax.ShapeDtypeStruct((groups, nh, 2 * seq), F32), jax.ShapeDtypeStruct((width, 3 * width), BF16)],
        compiler_params=params(60),
        cost_estimate=pl.CostEstimate(flops=COST, bytes_accessed=COST, transcendentals=0),
        name="attend_back",
    )(row, segs, q, k, v, do, aux, segs, band, h1t, *after)
    return dq, dk, dv, tg, wg, groups


def gelu_parts(u):
    dens = jnp.exp2(u * u * (-0.5 * LOG2E))
    t = 1.0 / (1.0 + (0.3275911 * 0.7071067811865476) * jnp.abs(u))
    poly = t * (0.127414796 + t * (-0.142248368 + t * (0.7107068705 + t * (-0.7265760135 + t * 0.5307027145))))
    tail = poly * dens
    phi = jnp.where(u >= 0, 1.0 - tail, tail)
    return phi, phi + u * (dens * 0.3989422804014327)


STEP = 512


def middle_body(
    row_ref, tok_ref, oc_ref, gains_ref, biases_ref, fgain_ref, fbias_ref, wo_ref, wu_ref, wd_ref, *rest
):
    out_ref, h3_ref, m_ref, mh_ref, gp_ref, z_ref, stat_ref, e_s, wu, wd, sems = rest[-11:]
    ff = wu_ref.shape[1]
    copies = [pltpu.make_async_copy(a, b, sems.at[i]) for i, (a, b) in enumerate(((wu_ref, wu), (wd_ref, wd)))]

    @pl.when(pl.program_id(0) == 0)
    def _():
        for copy in copies:
            copy.start()

    gains = gains_ref[...].astype(F32)
    biases = biases_ref[...].astype(F32)
    tok = tok_ref[...].astype(F32)
    n, d = tok.shape
    z2, r2 = normed(dot(oc_ref[...], wo_ref[...]) - (-biases[1:2]))
    x2 = tok + (z2 * gains[1:2] + biases[2:3])
    z3, r3 = normed(x2)
    h3 = (z3 * gains[2:3] + biases[3:4]).astype(BF16)
    h3_ref[...] = h3
    z_ref[:, :d] = z2.astype(BF16)
    z_ref[:, d:] = z3.astype(BF16)

    @pl.when(pl.program_id(0) == 0)
    def _():
        copies[0].wait()

    s1 = jnp.zeros((n, 1), F32)
    s2 = jnp.zeros((n, 1), F32)
    for c0 in range(0, ff, STEP):
        c = slice(c0, c0 + STEP)
        u = dot(h3, wu[:, c]) - (-fbias_ref[0:1, c].astype(F32))
        phi, slope = gelu_parts(u)
        e = u * phi
        e_s[:, c] = e
        gp_ref[:, c] = slope.astype(BF16)
        s1 += jnp.sum(e, axis=1, keepdims=True)
        s2 += jnp.sum(e * e, axis=1, keepdims=True)

    @pl.when(pl.program_id(0) == 0)
    def _():
        copies[1].wait()

    mean = s1 / ff
    r = lax.rsqrt(s2 / ff - mean * mean + EPS)
    y = jnp.zeros((n, d), F32)
    for c0 in range(0, ff, STEP):
        c = slice(c0, c0 + STEP)
        mh = (e_s[:, c] - mean) * r
        mh_ref[:, c] = mh.astype(BF16)
        m = (mh * fgain_ref[0:1, c].astype(F32) + fbias_ref[1:2, c].astype(F32)).astype(BF16)
        m_ref[:, c] = m
        y += dot(m, wd[c, :])
    out_ref[...] = (x2 + (y + biases[4:5])).astype(BF16)
    lane = lax.broadcasted_iota(jnp.int32, (n, 128), 1)
    stat_ref[...] = jnp.where(lane == 0, r2, jnp.where(lane == 1, r3, r))


def middle(row, tokens, oc, gains, biases, fgain, fbias, w_out, w_up, w_down, after=()):
    n, d = oc.shape
    ff = w_up.shape[1]
    steps = n // BLOCK
    blk = pl.BlockSpec((BLOCK, d), lambda i, row: (i, 0))
    wide = pl.BlockSpec((BLOCK, ff), lambda i, row: (i, 0))
    s = jax.ShapeDtypeStruct
    return pl.pallas_call(
        middle_body,
        grid_spec=pltpu.PrefetchScalarGridSpec(
            num_scalar_prefetch=1,
            grid=(steps,),
            in_specs=[pl.BlockSpec((BLOCK, d), lambda i, row: (row[0] * steps + i, 0)), blk]
            + [whole(x.shape) for x in (gains, biases, fgain, fbias, w_out)]
            + [ANYWHERE] * (2 + len(after)),
            out_specs=[
                blk, blk, wide, wide, wide,
                pl.BlockSpec((BLOCK, 2 * d), lambda i, row: (i, 0)),
                pl.BlockSpec((BLOCK, 128), lambda i, row: (i, 0)),
            ],
            scratch_shapes=[
                pltpu.VMEM((BLOCK, ff), F32),
                pltpu.VMEM((d, ff), BF16),
                pltpu.VMEM((ff, d), BF16),
                pltpu.SemaphoreType.DMA((2,)),
            ],
        ),
        out_shape=[s((n, d), BF16)] * 2 + [s((n, ff), BF16)] * 3 + [s((n, 2 * d), BF16), s((n, 128), F32)],
        compiler_params=params(60),
        cost_estimate=pl.CostEstimate(flops=COST, bytes_accessed=COST, transcendentals=0),
        name="middle",
    )(row, tokens, oc, gains, biases, fgain, fbias, w_out, w_up, w_down, *after)


def task_weight(counts_ref, tasks):
    counts = counts_ref[0:1, :]
    lane = lax.broadcasted_iota(jnp.int32, counts.shape, 1)
    own = jnp.sum(jnp.where(lane == tasks[0], counts, 0.0), axis=1, keepdims=True)
    return jnp.sum(counts, axis=1, keepdims=True) / (TASKS * own)


def middle_back_body(
    row_ref, tasks, og_ref, seg_ref, counts_ref, oc_ref, lse_ref, mh_ref, gp_ref, z_ref, stat_ref,
    gains_ref, fgain_ref, hs_ref, wo_ref, wu_ref, wd_ref, *rest
):
    df_ref, du_ref, dx2_ref, da_ref, do_ref, aux_ref, nv_ref, fv_ref, d_s, wu, sem = rest[-11:]
    copy = pltpu.make_async_copy(wu_ref, wu, sem.at[0])

    @pl.when(pl.program_id(0) == 0)
    def _():
        copy.start()

    d, ff = wu_ref.shape
    heads = d // HEAD
    gains = gains_ref[...].astype(F32)
    oc = oc_ref[...]
    rows = oc.shape[0]
    here = pl.ds(pl.multiple_of(pl.program_id(0) * rows, rows), rows)
    doc = column(seg_ref[pl.ds(row_ref[0], 1), here])
    g = og_ref[...].astype(F32) * jnp.where(doc >= 0, task_weight(counts_ref, tasks), 0.0)
    df = g.astype(BF16)
    df_ref[...] = df
    r2 = stat_ref[:, 0:1]
    r3 = stat_ref[:, 1:2]
    r = stat_ref[:, 2:3]
    b1 = jnp.zeros((rows, 1), F32)
    b2 = jnp.zeros((rows, 1), F32)
    gsum, bsum, usum = [], [], []
    for c0 in range(0, ff, STEP):
        c = slice(c0, c0 + STEP)
        mh = mh_ref[:, c].astype(F32)
        dm = dot(df, wd_ref[c, :], NT)
        gsum.append(jnp.sum(dm * mh, axis=0, keepdims=True))
        bsum.append(jnp.sum(dm, axis=0, keepdims=True))
        sc = dm * fgain_ref[0:1, c].astype(F32)
        d_s[:, c] = sc
        b1 += jnp.sum(sc, axis=1, keepdims=True)
        b2 += jnp.sum(sc * mh, axis=1, keepdims=True)
    b1 = b1 / ff
    b2 = b2 / ff

    @pl.when(pl.program_id(0) == 0)
    def _():
        copy.wait()

    dh3 = jnp.zeros((rows, d), F32)
    for c0 in range(0, ff, STEP):
        c = slice(c0, c0 + STEP)
        de = r * (d_s[:, c] - b1 - mh_ref[:, c].astype(F32) * b2)
        du = (de * gp_ref[:, c].astype(F32)).astype(BF16)
        du_ref[:, c] = du
        usum.append(jnp.sum(du.astype(F32), axis=0, keepdims=True))
        dh3 += dot(du, wu[:, c], NT)
    z2 = z_ref[:, :d].astype(F32)
    z3 = z_ref[:, d:].astype(F32)
    dx2 = g + norm_back(dh3, gains[2:3], z3, r3)
    dx2_ref[...] = dx2
    da = norm_back(dx2, gains[1:2], z2, r2).astype(BF16)
    da_ref[...] = da
    doc_ = dot(da, wo_ref[...], NT)
    hs = hs_ref[0:1, :]
    o = oc.astype(F32) / hs
    do = (doc_ * hs).astype(BF16)
    do_ref[...] = do

    prod = do.astype(F32) * o
    hi = prod.astype(BF16)
    lo = (prod - hi.astype(F32)).astype(BF16)
    at = DOCS + 3 * heads
    head_of = lax.broadcasted_iota(jnp.int32, (d, 128), 0) // HEAD
    lane = lax.broadcasted_iota(jnp.int32, (d, 128), 1)
    put = jnp.where((lane >= at + 3 * head_of) & (lane < at + 3 * head_of + 3), -1.0, 0.0).astype(BF16)
    delta = dot(hi, put) + dot(lo, put)
    pa, pb, pc = split3(delta)
    lane = lax.broadcasted_iota(jnp.int32, (rows, 128), 1)
    part = (lane - at + 3 * 128) % 3
    delta = jnp.where(part == 0, pa.astype(F32), jnp.where(part == 1, pb.astype(F32), pc.astype(F32)))
    hrows = lse_ref.shape[0]
    la, lb, lc = split3(lse_ref[...])
    stack = jnp.concatenate([la.astype(F32), lb.astype(F32), lc.astype(F32)], axis=0).astype(BF16)
    row = lax.broadcasted_iota(jnp.int32, (3 * hrows, 128), 0)
    col = lax.broadcasted_iota(jnp.int32, (3 * hrows, 128), 1)
    put = jnp.where((row % hrows < heads) & (col == DOCS + 3 * (row % hrows) + row // hrows), -1.0, 0.0)
    lse = dot(stack, put.astype(BF16), TN)
    bar = jnp.where((lane < DOCS) & (lane != doc.astype(jnp.int32) + 1), NEG, 0.0)
    aux_ref[...] = (bar + lse + delta).astype(BF16)

    @pl.when(pl.program_id(0) == 0)
    def _():
        nv_ref[...] = jnp.zeros_like(nv_ref)
        fv_ref[...] = jnp.zeros_like(fv_ref)

    sums = (dx2 * z2, dh3 * z3, da.astype(F32), dx2, dh3, df.astype(F32), doc_ * o)
    for i, term in enumerate(sums):
        nv_ref[i : i + 1, :] += jnp.sum(term, axis=0, keepdims=True)
    for i, terms in enumerate((gsum, usum, bsum)):
        fv_ref[i : i + 1, :] += jnp.concatenate(terms, axis=1)


def middle_back(row, tasks, counts, out_grad, segs, oc, lse, mh, gp, z, stat, gains, fgain, hs, w_out, w_up, w_down, after=()):
    n, d = oc.shape
    ff = w_up.shape[1]
    steps = n // BLOCK
    blk = pl.BlockSpec((BLOCK, d), lambda i, *_: (i, 0))
    wide = pl.BlockSpec((BLOCK, ff), lambda i, *_: (i, 0))
    thin = pl.BlockSpec((BLOCK, 128), lambda i, *_: (i, 0))
    s = jax.ShapeDtypeStruct
    return pl.pallas_call(
        middle_back_body,
        grid_spec=pltpu.PrefetchScalarGridSpec(
            num_scalar_prefetch=2,
            grid=(steps,),
            in_specs=[
                pl.BlockSpec((BLOCK, d), lambda i, row, *_: (row[0] * steps + i, 0)),
                whole(segs.shape),
                whole(counts.shape),
                blk,
                pl.BlockSpec((lse.shape[0], BLOCK), lambda i, *_: (0, i)),
                wide, wide, pl.BlockSpec((BLOCK, 2 * d), lambda i, *_: (i, 0)), thin,
            ]
            + [whole(x.shape) for x in (gains, fgain, hs, w_out)]
            + [ANYWHERE, whole(w_down.shape)]
            + [ANYWHERE] * len(after),
            out_specs=[
                blk, wide, blk, blk, blk, thin,
                pl.BlockSpec((8, d), lambda i, *_: (0, 0)),
                pl.BlockSpec((8, ff), lambda i, *_: (0, 0)),
            ],
            scratch_shapes=[pltpu.VMEM((BLOCK, ff), F32), pltpu.VMEM((d, ff), BF16), pltpu.SemaphoreType.DMA((1,))],
        ),
        out_shape=[
            s((n, d), BF16), s((n, ff), BF16), s((n, d), F32), s((n, d), BF16), s((n, d), BF16), s((n, 128), BF16), s((8, d), F32), s((8, ff), F32),
        ],
        compiler_params=params(60),
        cost_estimate=pl.CostEstimate(flops=COST, bytes_accessed=COST, transcendentals=0),
        name="middle_back",
    )(row, tasks, out_grad, segs, counts, oc, lse, mh, gp, z, stat, gains, fgain, hs, w_out, w_up, w_down, *after)


def early_body(h3_ref, df_ref, da_ref, du_ref, m_ref, oc_ref, out_ref, ht, ft, at):
    i = pl.program_id(0)
    steps = (pl.num_programs(0) - 1) // 2

    @pl.when(i == 0)
    def _():
        for source, target in ((h3_ref, ht), (df_ref, ft), (da_ref, at)):
            target[...] = source[...].astype(F32).T.astype(BF16)

    @pl.when(i < steps)
    def _():
        out_ref[...] = dot(ft[...], m_ref[...]).astype(BF16)

    @pl.when((i >= steps) & (i < 2 * steps))
    def _():
        out_ref[...] = dot(ht[...], du_ref[...]).astype(BF16)

    @pl.when(i >= 2 * steps)
    def _():
        out_ref[...] = dot(at[...], oc_ref[...]).astype(BF16)


def early_grads(h3, df, da, du, m, oc):
    n, d = h3.shape
    ff = du.shape[1]
    width = d
    steps = ff // width
    pick = lambda first, count: pl.BlockSpec((n, width), lambda i: (0, jnp.clip(i - first, 0, count - 1)))
    return pl.pallas_call(
        early_body,
        grid=(2 * steps + 1,),
        in_specs=[whole((n, d))] * 3 + [pick(steps, steps), pick(0, steps), pick(2 * steps, 1)],
        out_specs=pl.BlockSpec((d, width), lambda i: (0, i)),
        out_shape=jax.ShapeDtypeStruct((d, 2 * ff + d), BF16),
        scratch_shapes=[pltpu.VMEM((d, n), BF16)] * 3,
        compiler_params=params(60),
        cost_estimate=pl.CostEstimate(flops=COST, bytes_accessed=COST, transcendentals=0),
        name="early_grads",
    )(h3, df, da, du, m, oc)


def input_body(row_ref, tok_ref, dx2_ref, dq_ref, dk_ref, dv_ref, gains_ref, w_ref, *rest):
    tg_ref, nv_ref = rest[-2:]
    z, r = normed(tok_ref[...].astype(F32))
    dh1 = (
        dot(dq_ref[...], w_ref[0], NT) + dot(dk_ref[...], w_ref[1], NT) + dot(dv_ref[...], w_ref[2], NT)
    )
    tg_ref[...] = (dx2_ref[...] + norm_back(dh1, gains_ref[0:1, :].astype(F32), z, r)).astype(BF16)

    @pl.when(pl.program_id(0) == 0)
    def _():
        nv_ref[...] = jnp.zeros_like(nv_ref)

    sums = (dh1 * z, dh1, dq_ref[...].astype(F32), dv_ref[...].astype(F32))
    for i, term in enumerate(sums):
        nv_ref[i : i + 1, :] += jnp.sum(term, axis=0, keepdims=True)


def input_grad(row, tokens, dx2, dq, dk, dv, gains, w_qkv, after=()):
    n, d = dx2.shape
    steps = n // BLOCK
    blk = pl.BlockSpec((BLOCK, d), lambda i, row: (i, 0))
    return pl.pallas_call(
        input_body,
        grid_spec=pltpu.PrefetchScalarGridSpec(
            num_scalar_prefetch=1,
            grid=(steps,),
            in_specs=[pl.BlockSpec((BLOCK, d), lambda i, row: (row[0] * steps + i, 0))]
            + [blk] * 4
            + [whole(gains.shape), whole(w_qkv.shape)]
            + [pl.BlockSpec(memory_space=pl.ANY)] * len(after),
            out_specs=[blk, pl.BlockSpec((8, d), lambda i, row: (0, 0))],
        ),
        out_shape=[jax.ShapeDtypeStruct((n, d), BF16), jax.ShapeDtypeStruct((8, d), F32)],
        compiler_params=params(60),
        cost_estimate=pl.CostEstimate(flops=COST, bytes_accessed=COST, transcendentals=0),
        name="input_grad",
    )(row, tokens, dx2, dq, dk, dv, gains, w_qkv, *after)


def gate_body(*refs):
    refs[-1][0] = 0


def gate(x, *after):
    return pl.pallas_call(
        gate_body,
        in_specs=[ANYWHERE] * (1 + len(after)),
        out_specs=[ANYWHERE, pl.BlockSpec(memory_space=pltpu.SMEM)],
        out_shape=[jax.ShapeDtypeStruct(x.shape, x.dtype), jax.ShapeDtypeStruct((1,), jnp.int32)],
        input_output_aliases={0: 0},
        cost_estimate=pl.CostEstimate(flops=COST, bytes_accessed=COST, transcendentals=0),
        name="gate",
    )(x, *after)[0]


def copy_body(x_ref, o_ref):
    o_ref[...] = x_ref[...]


def copy(x):
    n, d = x.shape
    blk = pl.BlockSpec((n // 8, d), lambda i: (i, 0))
    return pl.pallas_call(
        copy_body,
        grid=(8,),
        in_specs=[blk],
        out_specs=blk,
        out_shape=jax.ShapeDtypeStruct(x.shape, x.dtype),
        name="copy",
    )(x)


def spread_body(row_ref, pair_ref, right_ref, left_ref, qkv_out, o_out, up_out, down_out):
    share = up_out.shape[1]
    cols = qkv_out.shape[2]
    pair = pair_ref[0].astype(F32) + right_ref[...].astype(F32) + left_ref[...].astype(F32)
    down_out[...] = pair[:, :share]
    up_out[...] = pair[:, share : 2 * share]
    small = pair[:, 2 * share :]
    o_out[...] = small[:, :cols].T
    for i in range(3):
        qkv_out[i] = small[:, (i + 1) * cols : (i + 2) * cols]


def spread(row, pair, pair_sums, share):
    _, n, width = pair.shape
    cols = (width - 2 * share) // 4
    s = jax.ShapeDtypeStruct
    own = lambda x: pl.BlockSpec((1,) + x.shape[1:], lambda i, row: (row[0], 0, 0))
    other = lambda x: pl.BlockSpec(x.shape[1:], lambda i, row: (0, 0))
    outs = [s((3, n, cols), F32), s((cols, n), F32), s((n, share), F32), s((n, share), F32)]
    return pl.pallas_call(
        spread_body,
        grid_spec=pltpu.PrefetchScalarGridSpec(
            num_scalar_prefetch=1,
            grid=(1,),
            in_specs=[own(pair), other(pair), other(pair)],
            out_specs=[pl.BlockSpec(x.shape, lambda i, row, k=len(x.shape): (0,) * k) for x in outs],
        ),
        out_shape=outs,
        name="spread",
    )(row, pair, *pair_sums)


def sum_scatter(x, axis):
    size = lax.axis_size(axis)
    me = lax.axis_index(axis)
    count = size.bit_length() - 1

    def swap(x, left, b):
        dim = left.index(b)
        mine = (me >> b) & 1
        send = lax.dynamic_index_in_dim(x, 1 - mine, dim, keepdims=False)
        keep = lax.dynamic_index_in_dim(x, mine, dim, keepdims=False)
        pairs = [(i, i ^ (1 << b)) for i in range(size)]
        return keep + lax.ppermute(send, axis, pairs), [o for o in left if o != b]

    left = list(range(count - 1, -1, -1))
    x, left = swap(x.reshape((2,) * count + (x.shape[0] // size, x.shape[1])), left, 0)
    half = x.shape[-1] // 2
    near, far = (x[..., :half], left), (x[..., half:], left)
    for i in range(1, count):
        near = swap(*near, i)
        far = swap(*far, count - i)
    return jnp.concatenate([near[0], far[0]], axis=-1)


def line_sums(blocks, axis):
    size = lax.axis_size(axis)
    me = lax.axis_index(axis)
    right = left = None
    for step in range(1, size):
        at = jnp.minimum(size - step + me, size - 1)
        pairs = [(i, i + 1) for i in range(step)]
        send = lax.dynamic_index_in_dim(blocks, at, 0, keepdims=False)
        right = lax.ppermute(send if right is None else send + right, axis, pairs)
        at = jnp.maximum(step - 1 - (size - 1 - me), 0)
        pairs = [(size - 1 - i, size - 2 - i) for i in range(step)]
        send = lax.dynamic_index_in_dim(blocks, at, 0, keepdims=False)
        left = lax.ppermute(send if left is None else send + left, axis, pairs)
    return right, left


def partial_sums(x, axis):
    size = lax.axis_size(axis)
    sums = [x]
    step = 1
    while step < size:
        sums.append(sums[-1] + lax.ppermute(sums[-1], axis, [(i, i ^ step) for i in range(size)]))
        step *= 2
    return sums


def add_all(x, axis):
    return partial_sums(x, axis)[-1]


def local(
    tokens, out_grad, segment_ids, row_tasks, rel_buckets, norm_gains, model_biases, w_qkv, qkv_bias,
    rel_bias, head_scale, w_out, w_up, ffn_gain, ffn_biases, w_down,
):
    parts = lax.axis_size("tensor")
    dps = lax.axis_size("dp")
    tensor_index = lax.axis_index("tensor")
    dp_index = lax.axis_index("dp")
    heads = head_scale.shape[0]
    d = tokens.shape[1]
    ff = w_up.shape[1]
    rows, seq = segment_ids.shape
    assert rows == parts

    live = jnp.sum((segment_ids >= 0).astype(F32), axis=1, keepdims=True)
    counts = jnp.sum(jnp.where(row_tasks[:, None] == jnp.arange(TASKS)[None, :], live, 0.0), axis=0)
    sums = partial_sums(jnp.broadcast_to(counts[None, :], (8, TASKS)), "dp")
    counts = sums[-1]

    back = jnp.pad(rel_buckets, (1, 0), constant_values=-1)[::-1]
    onehot = (jnp.arange(rel_bias.shape[1])[:, None] == back[None, :]).astype(BF16)
    rev = jnp.dot(rel_bias, onehot, preferred_element_type=F32)
    hv = jnp.concatenate(
        [jnp.broadcast_to(head_scale[None, :, None], (1, heads, d // heads)), qkv_bias], axis=0
    )
    hv = hv.astype(F32).reshape(3, d)
    fgain = ffn_gain[None, :]
    segs = segment_ids
    row = tensor_index[None]

    oc, lse, h1t, q, k, v, band = attend(
        row, tokens, segs, norm_gains, model_biases, w_qkv, hv, rev, sums[1:2]
    )
    layer_out, h3, m, mh, gp, z, stat = middle(
        row, tokens, oc, norm_gains, model_biases, fgain, ffn_biases, w_out, w_up, w_down, sums[2:3]
    )
    piece = d // dps
    share = ff // parts
    cols = d // parts
    layer_out = lax.all_gather(layer_out, "tensor", axis=0, tiled=True)
    df, du, dx2, da, do, aux, nv, fv = middle_back(
        row, row_tasks, counts, out_grad, segs, oc, lse, mh, gp, z, stat, norm_gains, fgain, hv, w_out, w_up, w_down
    )
    early = early_grads(h3, df, da, du, m, oc)
    dq, dk, dv, tg, late, groups = attend_back(row, q, k, v, do, aux, segs, band, h1t, (early,))
    early = lax.psum_scatter(early, "dp", scatter_dimension=0, tiled=True)
    tokens_grad, nv2 = input_grad(row, tokens, dx2, dq, dk, dv, norm_gains, w_qkv)
    nv2 = gate(nv2, layer_out)
    layer_out = copy(layer_out)
    tokens_grad = lax.all_gather(tokens_grad, "tensor", axis=0, tiled=True)
    late = sum_scatter(gate(late, nv2, early, layer_out), "dp")

    late = late.reshape(piece, groups, 3, d // groups).transpose(0, 2, 1, 3).reshape(piece, 3 * d)
    small = jnp.concatenate([early[:, 2 * ff :], late], axis=1).reshape(piece, 4, parts, cols)
    pair = jnp.concatenate(
        [
            early[:, :ff].reshape(piece, parts, share),
            early[:, ff : 2 * ff].reshape(piece, parts, share),
            small.transpose(0, 2, 1, 3).reshape(piece, parts, 4 * cols),
        ],
        axis=2,
    ).transpose(1, 0, 2)
    pair_sums = line_sums(pair, "tensor")
    project_grad, output_grad, up_grad, down_grad = spread(row, pair, pair_sums, share)
    tokens_grad = gate(tokens_grad, up_grad)
    down_grad = down_grad.T

    position = jnp.einsum("hs,bs->hb", gate(tg, nv2).reshape(heads, 2 * seq), onehot.astype(F32), precision=lax.Precision.HIGHEST)
    head_sum = jnp.sum(nv[6].reshape(heads, d // heads), axis=1)
    vec = jnp.concatenate(
        [
            nv2[0:1].reshape(-1), nv[0:2].reshape(-1),
            nv2[1:2].reshape(-1), nv[2:6].reshape(-1),
            nv2[2:4].reshape(-1),
            fv[0:3].reshape(-1),
            position.reshape(-1),
            head_sum,
        ]
    )
    size = vec.shape[0]
    vec = jnp.pad(vec, (0, -size % 1024)).reshape(-1, 128)
    vec = add_all(add_all(vec, "dp"), "tensor").reshape(-1)
    at = 0

    def take(shape):
        nonlocal at
        n = 1
        for s in shape:
            n *= s
        out = vec[at : at + n].reshape(shape)
        at += n
        return out

    gains_grad = lax.dynamic_slice_in_dim(take((3, d)), dp_index * piece, piece, 1)
    biases_grad = lax.dynamic_slice_in_dim(take((5, d)), dp_index * piece, piece, 1)
    hp = heads // parts
    project_bias = lax.dynamic_slice_in_dim(take((2, heads, d // heads)), tensor_index * hp, hp, 1)
    fgain_grad = lax.dynamic_slice_in_dim(take((ff,)), tensor_index * share, share, 0)
    fbias_grad = lax.dynamic_slice_in_dim(take((2, ff)), tensor_index * share, share, 1)
    position = take(position.shape)
    bp = position.shape[1] // dps
    position = lax.dynamic_slice(position, (tensor_index * hp, dp_index * bp), (hp, bp))
    head_grad = lax.dynamic_slice_in_dim(take((heads,)), tensor_index * hp, hp, 0)
    return (
        layer_out, tokens_grad, gains_grad, biases_grad, project_grad, project_bias, position, head_grad,
        output_grad, up_grad, fgain_grad, fbias_grad, down_grad,
    )


def solution(mesh):
    rows = P("dp", None)
    return jax.shard_map(
        local,
        mesh=mesh,
        in_specs=(rows, rows, rows, P("dp")) + (P(),) * 12,
        out_specs=(
            rows,
            rows,
            P(None, "dp"),
            P(None, "dp"),
            P(None, "dp", "tensor"),
            P(None, "tensor", None),
            P("tensor", "dp"),
            P("tensor"),
            P("tensor", "dp"),
            P("dp", "tensor"),
            P("tensor"),
            P(None, "tensor"),
            P("tensor", "dp"),
        ),
        check_vma=False,
    )
```
